32 devices in a mesh: section: 2 (over y), dp: 16 (over z, x, core).
Axes of the slice: x: 2, y: 2, z: 4, core: 2. Of those that a mesh axis runs over, the one named last changes fastest.
Arguments:
- patches: bfloat16 [12544, 768], P('dp'), may hold values from -6 to 6
- captions: bfloat16 [8192, 768], P('dp'), may hold values from -6 to 6
- segments: int32 [64, 128], P('dp'), may hold values from 0 to 3, never falling along the last dimension, each value on 1 to 64 neighbouring positions
- seg_images: int32 [64, 4], P('dp'), may hold values from 0 to 1
- attn_w: bfloat16 [2, 768, 4608], P('section'), may hold values from -0.9 to 0.9
- w_in: bfloat16 [2, 768, 3072], P('section'), may hold values from -0.21875 to 0.21875
- w_out: bfloat16 [2, 3072, 768], P('section'), may hold values from -0.109375 to 0.109375
- norm_gains: float32 [2, 3, 768], P('section'), may hold values from 0.5 to 1.5
- cotangent: bfloat16 [8192, 768], P('dp'), may hold values from -6 to 6
Outputs:
- decoded: bfloat16 [8192, 768], P('dp', 'section')
- caption_grad: float32 [8192, 768], P('dp', 'section')
- patch_grad: float32 [12544, 768], P('dp', 'section')
- attn_grad: float32 [2, 768, 4608], P('section', 'dp')
- w_in_grad: float32 [2, 768, 3072], P('section', 'dp')
- w_out_grad: float32 [2, 3072, 768], P('section', 'dp')
- gain_grad: float32 [2, 3, 768], P('section', None, 'dp')
The draws below stay inside these ranges and needn't reach their ends.
Inputs may be any that keep to these rules, and one draw needn't show every extreme that they name: Every caption row has its 4 segments in order, numbered from 0. seg_images[r, s] names one of the 2 images of the group of caption row r.
All inputs are finite; a program needn't handle non-finite values.
Results may differ from the reference program's by a relative error of at most 0.015.
Values may be sent and summed in bfloat16 or wider, within the bound.
A program may use at most 320 MiB of HBM per device.

```python
import math
import jax
import jax.numpy as jnp
import numpy as np
from jax import lax

D = 768
FF = 3072
HEADS = 12
HEAD = 64
PATCHES = 196
ROW = 128
SEGS = 4
MICRO = 2
IMG_MB = 2
ROWS_MB = 2
PATCH_ROWS = 12544
CAP_ROWS = 64
CAP_TOKENS = 8192
N_DP = 16


def draw_attn_w(key, part):
    key = jax.random.fold_in(key, 7)
    limit = 0.9 * D ** 0.5 / 6.0
    entries = jax.random.truncated_normal(key, -limit, limit, (2, D, 6 * D), jnp.float32)
    column = jnp.arange(6 * D)[None, None, :]
    layer_index = jnp.arange(2)[:, None, None]
    larger = (column >= 3 * D) & (column < 4 * D) | (layer_index == 1) & (column >= 5 * D)
    return (entries * jnp.where(larger, 6.0, 1.0) * D ** (-0.5)).astype(jnp.bfloat16)


def place_ends(result, own_key, low, top_value):
    place = [jax.random.randint(jax.random.fold_in(own_key, axis), (), 0, length) for axis, length in enumerate(result.shape)]
    widest = result.shape.index(max(result.shape))
    next_to = place[:widest] + [(place[widest] + 1) % result.shape[widest]] + place[widest + 1:]
    return result.at[tuple(place)].set(low).at[tuple(next_to)].set(top_value)


def strengthened(values, key, source, target, shards_of, factor):
    owner, partner = [(jnp.arange(values.shape[dim]) // (values.shape[dim] // shards_of)).reshape([-1 if axis == dim else 1 for axis in range(values.ndim)]) for dim in (source, target)]
    chosen = jax.random.permutation(key, shards_of)[partner]
    strong = (owner == chosen) | (owner == (partner + shards_of // 2) % shards_of)
    return jnp.where(strong, factor * values, values)


def level_of(stream_key, extent, pieces, smallest, top_value):
    def one(dim, parts):
        draws = jax.random.uniform(jax.random.fold_in(jax.random.fold_in(stream_key, 6), dim), (parts,), jnp.float32, smallest / len(pieces), top_value / len(pieces))
        return jnp.repeat(jnp.exp(draws), extent[dim] // parts).reshape((-1,) + (1,) * (len(extent) - dim - 1))

    gain = one(*pieces[0])
    for cut in pieces[1:]:
        gain = gain * one(*cut)
    return gain


def length_profile(number_of, total, most, skew):
    portions = [(1 << 20) // math.isqrt(standing ** skew) + 1 for standing in range(2, number_of + 1)]
    rest, counts = total - most - (number_of - 1), [1] * (number_of - 1)
    while rest > 0:
        free = [i for i in range(number_of - 1) if counts[i] < most]
        mass, budget = sum([portions[i] for i in free]), rest
        for i in free:
            more = min(most - counts[i], max(1, budget * portions[i] // mass), rest)
            counts[i] = counts[i] + more
            rest = rest - more
    return np.array([most] + counts)


def ragged_sizes(rng, count, total, most, lean):
    if count == 2:
        one = jax.random.randint(rng, (), max(1, total - most), min(most, total - 1) + 1)
        return jnp.stack([one, total - one])
    lengths = jnp.asarray(length_profile(count, total, most, lean), jnp.int32)
    pairs = (count - 1) // 2
    donor, sink = lengths[1:1 + 2 * pairs:2], lengths[2:2 + 2 * pairs:2]
    margin = jnp.minimum(donor - 1, most - sink)
    moved = jax.random.randint(jax.random.fold_in(rng, 1), (pairs,), 0, 1 << 20) % (margin + 1)
    lengths = lengths.at[1:1 + 2 * pairs:2].set(donor - moved).at[2:2 + 2 * pairs:2].set(sink + moved)
    return lengths[jax.random.permutation(jax.random.fold_in(rng, 2), count)]


def gaussian(rng, dims, width, bound, shards=(), kind=jnp.bfloat16):
    array = width * jax.random.normal(rng, dims, jnp.float32)
    if shards:
        array = array * level_of(rng, dims, shards, -0.22, 0.18)
    return jnp.clip(array, -bound, bound).astype(kind)


def gaussian_with(own_key, extent, deviation, bound, pieces, heavy, kind=jnp.bfloat16):
    values = deviation * jax.random.normal(own_key, extent, jnp.float32)
    if pieces:
        values = values * level_of(own_key, extent, pieces, -0.22, 0.18)
    return jnp.clip(strengthened(values, jax.random.fold_in(own_key, 3), *heavy), -bound, bound).astype(kind)


def setup_inputs(seed: int = 0) -> dict:
    key_of = jax.random.split(jax.random.key(seed), 10)
    return {
        "patches": gaussian_with(key_of[0], (PATCH_ROWS, D), 1.0, 6.0, ((0, 16),), (0, 1, 16, 2.0)),
        "captions": gaussian_with(key_of[1], (CAP_TOKENS, D), 1.0, 6.0, ((0, 16),), (0, 1, 16, 2.0)),
        "segments": jax.vmap(lambda own: jnp.searchsorted(jnp.cumsum(ragged_sizes(own, SEGS, ROW, ROW // 2, 1)), jnp.arange(ROW), side="right"))(jax.random.split(key_of[2], CAP_ROWS)).reshape((CAP_ROWS, ROW)).astype(jnp.int32),
        "seg_images": place_ends(jax.random.randint(key_of[3], (CAP_ROWS, SEGS), 0, IMG_MB), jax.random.fold_in(key_of[3], 1), 0, IMG_MB - 1).astype(jnp.int32),
        "attn_w": draw_attn_w(jax.random.fold_in(key_of[9], 71), 0),
        "w_in": gaussian(key_of[5], (2, D, FF), D ** -0.5, 0.21875, ((0, 2),)),
        "w_out": gaussian(key_of[6], (2, FF, D), FF ** -0.5, 0.109375, ((0, 2),)),
        "norm_gains": jnp.clip(1.0 + 0.1 * jax.random.normal(key_of[7], (2, 3, D), jnp.float32), 0.5, 1.5),
        "cotangent": gaussian(key_of[8], (CAP_TOKENS, D), 1.0, 6.0, ((0, 16),)),
    }


NORM_EPS = 1e-06
SCORE_SCALE = 0.125
MASKED = -1e+30
EXACT = lax.Precision.HIGHEST

@jax.custom_vjp
def low(v):
    return lax.optimization_barrier(v.astype(jnp.bfloat16)).astype(jnp.float32)

@jax.custom_vjp
def low_back(v):
    return v

def low_keep(v):
    return (low(v), None)

def low_pass(kept, grad):
    return (grad,)

def back_keep(v):
    return (v, None)

def back_low(kept, grad):
    return (low(grad),)
low.defvjp(low_keep, low_pass)
low_back.defvjp(back_keep, back_low)

def round_both(values):
    return low(low_back(values))

def dense_mul(left_side, right_side):
    return jnp.dot(left_side, right_side, precision=EXACT)

def layer_norm(values, gain_row):
    row_mean = lax.optimization_barrier(jnp.mean(values, -1, keepdims=True))
    centred = values - row_mean
    spread = lax.optimization_barrier(jnp.mean(centred * centred, -1, keepdims=True))
    return centred * lax.rsqrt(spread + NORM_EPS) * gain_row

def split_heads(values, lead):
    return values.reshape(lead + (HEADS, HEAD))

def attend(queries, key_rows, values, key_mask):
    scores = low_back(jnp.einsum('bqhe,bkhe->bhqk', queries, key_rows, precision=EXACT) * SCORE_SCALE)
    if key_mask is not None:
        scores = jnp.where(key_mask[:, None], scores, MASKED)
    chances = low(jax.nn.softmax(scores, axis=-1))
    mixed = round_both(jnp.einsum('bhqk,bkhe->bqhe', chances, values, precision=EXACT))
    return mixed.reshape(-1, D)

def attention_sub(resid, gain_row, attn_mat, lead, key_mask):
    a_low = low(layer_norm(resid, gain_row))
    qkv_rows = round_both(dense_mul(a_low, attn_mat[:, :3 * D]))
    mixed = attend(split_heads(qkv_rows[:, :D], lead), split_heads(qkv_rows[:, D:2 * D], lead), split_heads(qkv_rows[:, 2 * D:], lead), key_mask)
    return resid + low_back(dense_mul(mixed, attn_mat[:, 3 * D:4 * D]))

def feed_forward(resid, gain_row, w_in, w_out):
    b_low = low(layer_norm(resid, gain_row))
    hidden = low_back(dense_mul(b_low, w_in))
    act_low = low(jax.nn.gelu(hidden, approximate=False))
    return resid + low_back(dense_mul(act_low, w_out))

def encode(patch_rows, attn_mat, w_in, w_out, gain_set):
    after_attn = attention_sub(patch_rows, gain_set[0], attn_mat, (IMG_MB, PATCHES), None)
    after_mlp = feed_forward(after_attn, gain_set[1], w_in, w_out)
    return round_both(dense_mul(low(layer_norm(after_mlp, gain_set[2])), attn_mat[:, 4 * D:]))

def decode(caption_rows, context, seg_rows, image_rows, attn_mat, w_in, w_out, gain_set):
    position = jnp.arange(ROW).astype(jnp.int32)
    self_mask = (position[:, None] >= position[None, :])[None] & (seg_rows[:, :, None] == seg_rows[:, None, :])
    after_attn = attention_sub(caption_rows, gain_set[0], attn_mat, (ROWS_MB, ROW), self_mask)
    c_low = low(layer_norm(after_attn, gain_set[1]))
    cross_q = round_both(dense_mul(c_low, attn_mat[:, 4 * D:5 * D]))
    seg_match = seg_rows[:, :, None] == jnp.arange(SEGS).astype(jnp.int32)[None, None, :]
    token_image = lax.optimization_barrier(jnp.sum(jnp.where(seg_match, image_rows[:, None, :], 0), -1)).reshape(1, -1)
    patch_image = (jnp.arange(IMG_MB * PATCHES) // PATCHES).astype(jnp.int32)
    cross_mask = token_image[:, :, None] == patch_image[None, None, :]
    image_lead = (1, IMG_MB * PATCHES)
    crossed = attend(split_heads(cross_q, (1, ROWS_MB * ROW)), split_heads(context[:, :D], image_lead), split_heads(context[:, D:], image_lead), cross_mask)
    after_cross = after_attn + low_back(dense_mul(crossed, attn_mat[:, 5 * D:]))
    return feed_forward(after_cross, gain_set[2], w_in, w_out)

def reference(patches, captions, segments, seg_images, attn_w, w_in, w_out, norm_gains, cotangent):
    groups = N_DP * MICRO
    patch_groups = patches.astype(jnp.float32).reshape(groups // 4, 4, IMG_MB * PATCHES, D)
    caption_groups = captions.astype(jnp.float32).reshape(groups // 4, 4, ROWS_MB * ROW, D)
    seg_groups = segments.reshape(groups // 4, 4, ROWS_MB, ROW)
    image_groups = seg_images.reshape(groups // 4, 4, ROWS_MB, SEGS)

    def forward(patch_all, caption_all, attn_all, inner_all, outer_all, gain_all):

        def one_group(patch_rows, caption_rows, seg_rows, image_rows):
            context = encode(patch_rows, attn_all[0], inner_all[0], outer_all[0], gain_all[0])
            return decode(caption_rows, context, seg_rows, image_rows, attn_all[1], inner_all[1], outer_all[1], gain_all[1])
        group_fn = jax.checkpoint(jax.vmap(one_group))

        def scan_step(carry_on, group_items):
            return (carry_on, group_fn(*group_items))
        return lax.scan(scan_step, jnp.zeros((), jnp.float32), (patch_all, caption_all, seg_groups, image_groups))[1]
    decoded_f32, pull_back = jax.vjp(forward, patch_groups, caption_groups, attn_w.astype(jnp.float32), w_in.astype(jnp.float32), w_out.astype(jnp.float32), norm_gains.astype(jnp.float32))
    gradients = pull_back(cotangent.astype(jnp.float32).reshape(decoded_f32.shape))
    return (decoded_f32.reshape(-1, D).astype(jnp.bfloat16), gradients[1].reshape(-1, D), gradients[0].reshape(-1, D), gradients[2], gradients[3], gradients[4], gradients[5])
```

```python
import functools

import jax
import jax.numpy as jnp
from jax import lax
from jax.experimental import pallas as pl
from jax.experimental.pallas import tpu as pltpu
from jax.sharding import PartitionSpec as P

D = 768
FF = 3072
HEADS = 12
HEAD = 64
PATCHES = 196
ROW = 128
SEGS = 4
MICRO = 2
IMG_MB = 2
ROWS_MB = 2


NORM_EPS = 1e-06
SCORE_SCALE = 0.125
MASKED = -1e30
ROOT_HALF = 0.7071067811865476
INV_ROOT_TWO_PI = 0.3989422804014327


MESH = pl.DeviceIdType.MESH
CHUNK_COLS = 256
GAIN_STEPS = 4
LAG = 2
MIB = 1 << 20


def butterfly_partner(dp, weight):
    return dp + weight * (1 - 2 * ((dp // weight) % 2))


def rs_kernel(n_bits, blocks, lag, *refs):
    n_src = len(blocks)
    sources = refs[:n_src]
    gains_ref = refs[n_src]
    out_ref, gains_out = refs[n_src + 1], refs[n_src + 2]
    own, recv_core = refs[n_src + 3], refs[n_src + 4]
    recv = refs[n_src + 5 : n_src + 5 + n_bits - 1]
    (gain_sum, gain_in, own_sem, send_sem, recv_sem, gain_send, gain_recv) = refs[
        n_src + 5 + n_bits - 1 :
    ]
    dp = lax.axis_index("dp")
    bits = [(dp // (1 << b)) % 2 for b in range(n_bits)]
    partners = [butterfly_partner(dp, 1 << b) for b in range(n_bits)]
    barrier = pltpu.get_barrier_semaphore()
    for b in range(n_bits):
        pl.semaphore_signal(barrier, inc=1, device_id={"dp": partners[b]}, device_id_type=MESH)
    pl.semaphore_wait(barrier, n_bits)

    rows = own.shape[-2]
    lead = (slice(None),) * (n_bits - 1)
    total = sum(count for count, _ in blocks)

    def own_copy(src, index):
        return pltpu.make_async_copy(src, own.at[index], own_sem.at[index])

    def core_copy(src, index):
        return pltpu.make_async_remote_copy(
            src_ref=src, dst_ref=recv_core.at[index], send_sem=send_sem.at[0, index],
            recv_sem=recv_sem.at[0, index], device_id={"dp": partners[0]}, device_id_type=MESH)

    def gain_copy(b):
        return pltpu.make_async_remote_copy(
            src_ref=gain_sum.at[b], dst_ref=gain_in.at[b], send_sem=gain_send.at[b],
            recv_sem=gain_recv.at[b], device_id={"dp": partners[b]}, device_id_type=MESH)

    gain_sum[0] = gains_ref[...]
    gain_copy(0).start()

    base = 0
    for source, (count, col_blocks) in zip(sources, blocks):
        def launch(i, carry, source=source, base=base, col_blocks=col_blocks):
            row = pl.multiple_of((i // col_blocks) * rows, rows)
            col = pl.multiple_of((i % col_blocks) * CHUNK_COLS, CHUNK_COLS)
            part = (pl.ds(row, rows), pl.ds(col, CHUNK_COLS))
            core_copy(source.at[lead + (1 - bits[0],) + part], base + i).start()
            own_copy(source.at[lead + (bits[0],) + part], base + i).start()
            return carry
        lax.fori_loop(0, count, launch, 0)
        base += count

    def stage_copy(stage, index):
        held = own if stage == 1 else recv[stage - 2]
        keep = (slice(None),) * (n_bits - 1 - stage)
        return pltpu.make_async_remote_copy(
            src_ref=held.at[(index,) + keep + (1 - bits[stage],)], dst_ref=recv[stage - 1].at[index],
            send_sem=send_sem.at[stage, index], recv_sem=recv_sem.at[stage, index],
            device_id={"dp": partners[stage]}, device_id_type=MESH)

    def src_any(index):
        return sources[0].at[lead + (bits[0], pl.ds(0, rows), pl.ds(0, CHUNK_COLS))]

    def body(i, carry):
        for stage in range(n_bits):
            j = i - stage * lag
            @pl.when((j >= 0) & (j < total))
            def _(stage=stage, j=j):
                f32 = jnp.float32
                if stage == 0:
                    own_copy(src_any(j), j).wait()
                    core_copy(src_any(j), j).wait()
                    own[j] = (own[j].astype(f32) + recv_core[j].astype(f32)).astype(jnp.bfloat16)
                else:
                    stage_copy(stage, j).wait()
                    held = own if stage == 1 else recv[stage - 2]
                    keep = (slice(None),) * (n_bits - 1 - stage)
                    mine = held[(j,) + keep + (bits[stage],)].astype(f32)
                    summed = mine + recv[stage - 1][j].astype(f32)
                    if stage == n_bits - 1:
                        out_ref[j] = summed
                    else:
                        recv[stage - 1][j] = summed.astype(jnp.bfloat16)
                if stage < n_bits - 1:
                    stage_copy(stage + 1, j).start()
        for b in range(n_bits):
            @pl.when(i == GAIN_STEPS * (b + 1))
            def _(b=b):
                gain_copy(b).wait()
                summed = gain_sum[b] + gain_in[b]
                if b == n_bits - 1:
                    gains_out[...] = summed
                else:
                    gain_sum[b + 1] = summed
                    gain_copy(b + 1).start()
        return carry

    lax.fori_loop(0, total + (n_bits - 1) * lag, body, 0)


def reduce_scatter(sources, gains, n_dp):
    n_bits = n_dp.bit_length() - 1
    rows = min(source.shape[0] for source in sources) // n_dp
    shaped, blocks = [], []
    for source in sources:
        share = source.shape[0] // n_dp
        shaped.append(source.reshape((2,) * n_bits + (share, source.shape[1])))
        col_blocks = source.shape[1] // CHUNK_COLS
        blocks.append(((share // rows) * col_blocks, col_blocks))
    total = sum(count for count, _ in blocks)
    low = jnp.bfloat16
    half = (2,) * (n_bits - 1)
    scratch = [pltpu.VMEM((total,) + half + (rows, CHUNK_COLS), low)] * 2
    scratch += [pltpu.VMEM((total,) + half[b:] + (rows, CHUNK_COLS), low) for b in range(1, n_bits)]
    scratch += [
        pltpu.VMEM((n_bits,) + gains.shape, jnp.float32),
        pltpu.VMEM((n_bits,) + gains.shape, jnp.float32),
        pltpu.SemaphoreType.DMA((total,)),
        pltpu.SemaphoreType.DMA((n_bits, total)),
        pltpu.SemaphoreType.DMA((n_bits, total)),
        pltpu.SemaphoreType.DMA((n_bits,)),
        pltpu.SemaphoreType.DMA((n_bits,)),
    ]
    any_spec = pl.BlockSpec(memory_space=pl.ANY)
    vmem_spec = pl.BlockSpec(memory_space=pltpu.VMEM)
    return pl.pallas_call(
        functools.partial(rs_kernel, n_bits, tuple(blocks), LAG),
        name="share_sums",
        out_shape=(
            jax.ShapeDtypeStruct((total, rows, CHUNK_COLS), jnp.float32),
            jax.ShapeDtypeStruct(gains.shape, jnp.float32),
        ),
        in_specs=[any_spec] * len(sources) + [vmem_spec],
        out_specs=(vmem_spec, vmem_spec),
        scratch_shapes=scratch,
        compiler_params=pltpu.CompilerParams(
            collective_id=0, has_side_effects=True, vmem_limit_bytes=48 * MIB
        ),
    )(*shaped, gains)


def shifted(block, axis, distance):
    devices = range(lax.axis_size(axis))
    route = [(i - distance, i) for i in devices if i - distance in devices]
    return lax.ppermute(block, axis, route)


def matmul(left_side, right_side):
    return jnp.dot(left_side, right_side, preferred_element_type=jnp.float32)


def matmul_nt(left_side, right_side):
    return lax.dot_general(
        left_side, right_side, (((1,), (1,)), ((), ())), preferred_element_type=jnp.float32
    )


def matmul_tn(left_side, right_side):
    return lax.dot_general(
        left_side, right_side, (((0,), (0,)), ((), ())), preferred_element_type=jnp.float32
    )


def norm_fwd(values, gain_row):
    row_mean = jnp.mean(values, -1, keepdims=True)
    centred = values - row_mean
    inverse = lax.rsqrt(jnp.mean(centred * centred, -1, keepdims=True) + NORM_EPS)
    normed = centred * inverse
    return ((normed * gain_row).astype(jnp.bfloat16), normed, inverse)


def norm_bwd(upstream, normed, inverse, gain_row):
    scaled = upstream * gain_row
    row_inner = (
        scaled
        - jnp.mean(scaled, -1, keepdims=True)
        - normed * jnp.mean(scaled * normed, -1, keepdims=True)
    )
    return (row_inner * inverse, jnp.sum(upstream * normed, 0))


def gelu_parts(hidden):
    normal_cdf = 0.5 * (1.0 + jax.scipy.special.erf(hidden * ROOT_HALF))
    return (
        hidden * normal_cdf,
        normal_cdf + hidden * INV_ROOT_TWO_PI * jnp.exp(-0.5 * hidden * hidden),
    )


def masked_scores(queries, key_rows, key_mask):
    scores = (
        jnp.einsum("bqhe,bkhe->bhqk", queries, key_rows, preferred_element_type=jnp.float32)
        * SCORE_SCALE
    )
    if key_mask is not None:
        scores = jnp.where(key_mask[:, None], scores, MASKED)
    return scores


def attend_fwd(queries, key_rows, values, key_mask):
    scores = masked_scores(queries, key_rows, key_mask)
    row_top = jnp.max(scores, -1, keepdims=True)
    log_total = jnp.log(jnp.sum(jnp.exp(scores - row_top), -1, keepdims=True)) + row_top
    attn_probs = jnp.exp(scores - log_total).astype(jnp.bfloat16)
    mixed = jnp.einsum("bhqk,bkhe->bqhe", attn_probs, values, preferred_element_type=jnp.float32)
    return (mixed.astype(jnp.bfloat16), log_total)


def attend_bwd(queries, key_rows, values, key_mask, log_total, grad_mixed):
    attn_probs = jnp.exp(masked_scores(queries, key_rows, key_mask) - log_total)
    grad_probs = jnp.einsum(
        "bqhe,bkhe->bhqk", grad_mixed, values, preferred_element_type=jnp.float32
    )
    row_inner = jnp.sum(grad_probs * attn_probs, -1, keepdims=True)
    grad_scores = (attn_probs * (grad_probs - row_inner)).astype(jnp.bfloat16)
    grad_query = (
        jnp.einsum("bhqk,bkhe->bqhe", grad_scores, key_rows, preferred_element_type=jnp.float32)
        * SCORE_SCALE
    )
    grad_key = (
        jnp.einsum("bhqk,bqhe->bkhe", grad_scores, queries, preferred_element_type=jnp.float32)
        * SCORE_SCALE
    )
    grad_value = jnp.einsum(
        "bhqk,bqhe->bkhe",
        attn_probs.astype(jnp.bfloat16),
        grad_mixed,
        preferred_element_type=jnp.float32,
    )
    return (grad_query, grad_key, grad_value)


def split_three(qkv_low, head_shape):
    return tuple(
        (qkv_low[:, index * D : (index + 1) * D].reshape(head_shape) for index in range(3))
    )


def attention_forward(resid, gain_row, attn_mat, head_shape, key_mask):
    a_low, a_hat, a_inv = norm_fwd(resid, gain_row)
    qkv_low = matmul(a_low, attn_mat[:, : 3 * D]).astype(jnp.bfloat16)
    queries, key_rows, values = split_three(qkv_low, head_shape)
    mixed, log_total = attend_fwd(queries, key_rows, values, key_mask)
    mixed_low = mixed.reshape(-1, D)
    return (
        resid + matmul(mixed_low, attn_mat[:, 3 * D : 4 * D]),
        (a_low, a_hat, a_inv, qkv_low, mixed_low, log_total),
    )


def attention_backward(
    upstream,
    a_low,
    a_hat,
    a_inv,
    qkv_low,
    mixed_low,
    log_total,
    key_mask,
    head_shape,
    attn_mat,
    gain_row,
):
    grad_att = upstream.astype(jnp.bfloat16)
    grad_mixed = (
        matmul_nt(grad_att, attn_mat[:, 3 * D : 4 * D]).astype(jnp.bfloat16).reshape(head_shape)
    )
    queries, key_rows, values = split_three(qkv_low, head_shape)
    grad_query, grad_key, grad_value = attend_bwd(
        queries, key_rows, values, key_mask, log_total, grad_mixed
    )
    grad_qkv = jnp.concatenate(
        [grad_query.reshape(-1, D), grad_key.reshape(-1, D), grad_value.reshape(-1, D)], 1
    ).astype(jnp.bfloat16)
    grad_input, grad_gain = norm_bwd(
        matmul_nt(grad_qkv, attn_mat[:, : 3 * D]), a_hat, a_inv, gain_row
    )
    return (upstream + grad_input, grad_gain, (a_low, grad_qkv, mixed_low, grad_att))


def mlp_forward(resid, gain_row, inner_w, outer_w):
    b_low, b_hat, b_inv = norm_fwd(resid, gain_row)
    activated, gelu_slope = gelu_parts(matmul(b_low, inner_w))
    act_low = activated.astype(jnp.bfloat16)
    return (resid + matmul(act_low, outer_w), (b_low, b_hat, b_inv, gelu_slope, act_low))


def mlp_backward(upstream, mlp_kept, inner_w, outer_w, gain_row):
    b_low, b_hat, b_inv, gelu_slope, act_low = mlp_kept
    grad_y = upstream.astype(jnp.bfloat16)
    grad_hidden = (matmul_nt(grad_y, outer_w) * gelu_slope).astype(jnp.bfloat16)
    grad_input, grad_gain = norm_bwd(matmul_nt(grad_hidden, inner_w), b_hat, b_inv, gain_row)
    return (upstream + grad_input, grad_gain, (b_low, grad_hidden, act_low, grad_y))


def encoder_forward(patch_rows, attn_mat, inner_w, outer_w, gain_set):
    head_shape = (IMG_MB, PATCHES, HEADS, HEAD)
    after_attn, attn_kept = attention_forward(
        patch_rows.astype(jnp.float32), gain_set[0], attn_mat, head_shape, None
    )
    after_mlp, mlp_kept = mlp_forward(after_attn, gain_set[1], inner_w, outer_w)
    c_low, c_hat, c_inv = norm_fwd(after_mlp, gain_set[2])
    context = matmul(c_low, attn_mat[:, 4 * D :]).astype(jnp.bfloat16)
    return (context, (attn_kept, mlp_kept, (c_low, c_hat, c_inv)))


def encoder_backward(patch_rows, grad_context, attn_mat, inner_w, outer_w, gain_set):
    head_shape = (IMG_MB, PATCHES, HEADS, HEAD)
    attn_kept, mlp_kept, norm_kept = encoder_forward(
        patch_rows, attn_mat, inner_w, outer_w, gain_set
    )[1]
    c_low, c_hat, c_inv = norm_kept
    grad_top, gain_top = norm_bwd(
        matmul_nt(grad_context, attn_mat[:, 4 * D :]), c_hat, c_inv, gain_set[2]
    )
    grad_mid, gain_mid, mlp_pairs = mlp_backward(grad_top, mlp_kept, inner_w, outer_w, gain_set[1])
    grad_input, gain_low, attn_pairs = attention_backward(
        grad_mid, *attn_kept, None, head_shape, attn_mat, gain_set[0]
    )
    gains = jnp.stack([gain_low, gain_mid, gain_top])
    return (grad_input, attn_pairs + mlp_pairs + (c_low, grad_context, gains))


def decoder_step(
    caption_rows, context, seg_rows, image_rows, cot_rows, attn_mat, inner_w, outer_w, gain_set
):
    head_shape = (ROWS_MB, ROW, HEADS, HEAD)
    cross_shape = (1, ROWS_MB * ROW, HEADS, HEAD)
    image_shape = (1, IMG_MB * PATCHES, HEADS, HEAD)
    position = jnp.arange(ROW)
    self_mask = (position[:, None] >= position[None, :])[None] & (
        seg_rows[:, :, None] == seg_rows[:, None, :]
    )
    seg_match = seg_rows[:, :, None] == jnp.arange(SEGS)[None, None, :]
    token_image = jnp.sum(jnp.where(seg_match, image_rows[:, None, :], 0), -1).reshape(1, -1)
    cross_mask = token_image[:, :, None] == (jnp.arange(IMG_MB * PATCHES) // PATCHES)[None, None, :]
    after_attn, attn_kept = attention_forward(
        caption_rows.astype(jnp.float32), gain_set[0], attn_mat, head_shape, self_mask
    )
    c_low, c_hat, c_inv = norm_fwd(after_attn, gain_set[1])
    cross_q = matmul(c_low, attn_mat[:, 4 * D : 5 * D]).astype(jnp.bfloat16).reshape(cross_shape)
    image_keys = context[:, :D].reshape(image_shape)
    image_values = context[:, D:].reshape(image_shape)
    crossed, cross_total = attend_fwd(cross_q, image_keys, image_values, cross_mask)
    crossed_low = crossed.reshape(-1, D)
    after_cross = after_attn + matmul(crossed_low, attn_mat[:, 5 * D :])
    after_mlp, mlp_kept = mlp_forward(after_cross, gain_set[2], inner_w, outer_w)
    grad_cross, gain_top, mlp_pairs = mlp_backward(
        cot_rows.astype(jnp.float32), mlp_kept, inner_w, outer_w, gain_set[2]
    )
    grad_cross_low = grad_cross.astype(jnp.bfloat16)
    grad_crossed = (
        matmul_nt(grad_cross_low, attn_mat[:, 5 * D :]).astype(jnp.bfloat16).reshape(cross_shape)
    )
    grad_query, grad_key, grad_value = attend_bwd(
        cross_q, image_keys, image_values, cross_mask, cross_total, grad_crossed
    )
    grad_cross_q = grad_query.reshape(-1, D).astype(jnp.bfloat16)
    grad_context = jnp.concatenate([grad_key.reshape(-1, D), grad_value.reshape(-1, D)], 1).astype(
        jnp.bfloat16
    )
    grad_norm, gain_mid = norm_bwd(
        matmul_nt(grad_cross_q, attn_mat[:, 4 * D : 5 * D]), c_hat, c_inv, gain_set[1]
    )
    grad_input, gain_low, attn_pairs = attention_backward(
        grad_cross + grad_norm, *attn_kept, self_mask, head_shape, attn_mat, gain_set[0]
    )
    gains = jnp.stack([gain_low, gain_mid, gain_top])
    cross_pairs = (c_low, grad_cross_q, crossed_low, grad_cross_low)
    return (after_mlp, grad_input, grad_context, attn_pairs + cross_pairs + mlp_pairs + (gains,))


def join_rows(kept_list, index):
    return jnp.concatenate([member[index] for member in kept_list], 0)


def encoder_weights(kept_list):
    parts = [join_rows(kept_list, index) for index in range(10)]
    gains = kept_list[0][10]
    for member in kept_list[1:]:
        gains = gains + member[10]
    return (
        matmul_tn(parts[0], parts[1]),
        matmul_tn(parts[2], parts[3]),
        matmul_tn(parts[8], parts[9]),
        matmul_tn(parts[4], parts[5]),
        matmul_tn(parts[6], parts[7]),
        gains,
    )


def decoder_weights(kept_list):
    parts = [join_rows(kept_list, index) for index in range(12)]
    gains = kept_list[0][12]
    for member in kept_list[1:]:
        gains = gains + member[12]
    last_cols = jnp.concatenate([matmul_tn(parts[4], parts[5]), matmul_tn(parts[6], parts[7])], 1)
    return (
        matmul_tn(parts[0], parts[1]),
        matmul_tn(parts[2], parts[3]),
        last_cols,
        matmul_tn(parts[8], parts[9]),
        matmul_tn(parts[10], parts[11]),
        gains,
    )


def weight_pass(is_first, enc_list, dec_list):
    return lax.cond(
        is_first,
        lambda operands: encoder_weights(operands[0]),
        lambda operands: decoder_weights(operands[1]),
        (enc_list, dec_list),
    )


def zero_set(shape_list):
    return tuple((jnp.zeros(shape, kind) for shape, kind in shape_list))


def pass_up(context):
    return shifted(context, "section", 1)


def pass_down(grad_context):
    return shifted(grad_context, "section", -1)


def chunk_columns(chunks, rows, columns):
    col_blocks = columns // CHUNK_COLS
    shaped = chunks.reshape(rows // chunks.shape[1], col_blocks, chunks.shape[1], CHUNK_COLS)
    return shaped.transpose(0, 2, 1, 3).reshape(rows, columns)


def summed_shares(attn_part, in_part, out_part, gains):
    n_dp = lax.axis_size("dp")
    share_rows = D // n_dp
    if n_dp & (n_dp - 1) or share_rows % 16:
        wide = [part.astype(jnp.float32) for part in (attn_part, in_part, out_part)]
        sums = [lax.psum_scatter(part, "dp", scatter_dimension=0, tiled=True) for part in wide]
        return (*sums, lax.psum_scatter(gains, "dp", scatter_dimension=1, tiled=True))
    padded = jnp.pad(gains, ((0, 8 - gains.shape[0]), (0, 0)))
    chunks, gain_sums = reduce_scatter([attn_part, in_part, out_part], padded, n_dp)
    counts = [part.size // n_dp // (share_rows * CHUNK_COLS) for part in (attn_part, in_part)]
    first, second = counts[0], counts[0] + counts[1]
    own_gains = lax.dynamic_slice_in_dim(
        gain_sums[: gains.shape[0]], lax.axis_index("dp") * share_rows, share_rows, 1
    )
    return (
        chunk_columns(chunks[:first], share_rows, attn_part.shape[1]),
        chunk_columns(chunks[first:second], share_rows, in_part.shape[1]),
        chunk_columns(chunks[second:], out_part.shape[0] // n_dp, out_part.shape[1]),
        own_gains,
    )


def local(patches, captions, segments, seg_images, attn_w, w_in, w_out, norm_gains, cotangent):
    attn_mat = attn_w[0]
    inner_w = w_in[0]
    outer_w = w_out[0]
    gain_set = norm_gains[0]
    is_first = lax.axis_index("section") == 0
    patch_block = IMG_MB * PATCHES
    caption_block = ROWS_MB * ROW
    low_kind = jnp.bfloat16
    wide_kind = jnp.float32
    enc_shapes = [
        ((patch_block, D), low_kind),
        ((patch_block, 3 * D), low_kind),
        ((patch_block, D), low_kind),
        ((patch_block, D), low_kind),
        ((patch_block, D), low_kind),
        ((patch_block, FF), low_kind),
        ((patch_block, FF), low_kind),
        ((patch_block, D), low_kind),
        ((patch_block, D), low_kind),
        ((patch_block, 2 * D), low_kind),
        ((3, D), wide_kind),
    ]
    dec_shapes = [
        ((caption_block, D), low_kind),
        ((caption_block, 3 * D), low_kind),
        ((caption_block, D), low_kind),
        ((caption_block, D), low_kind),
        ((caption_block, D), low_kind),
        ((caption_block, D), low_kind),
        ((caption_block, D), low_kind),
        ((caption_block, D), low_kind),
        ((caption_block, D), low_kind),
        ((caption_block, FF), low_kind),
        ((caption_block, FF), low_kind),
        ((caption_block, D), low_kind),
        ((3, D), wide_kind),
    ]
    empty_ctx = jnp.zeros((patch_block, 2 * D), jnp.bfloat16)
    empty_patch = jnp.zeros((patch_block, D), jnp.float32)
    empty_caption = jnp.zeros((caption_block, D), jnp.float32)
    context_in = empty_ctx
    grad_in = empty_ctx
    enc_list = []
    dec_list = []
    patch_rows_list = []
    decoded_list = []
    caption_rows_list = []
    for tick_index in range(MICRO + 2):
        enc_fwd = tick_index < MICRO
        enc_bwd = tick_index >= 2
        dec_on = 1 <= tick_index <= MICRO

        def encoder_tick(
            operands, tick_index=tick_index, enc_fwd=enc_fwd, enc_bwd=enc_bwd, dec_on=dec_on
        ):
            context_now, grad_now = operands
            send_up = empty_ctx
            if enc_fwd:
                start_row = tick_index * patch_block
                send_up = encoder_forward(
                    patches[start_row : start_row + patch_block],
                    attn_mat,
                    inner_w,
                    outer_w,
                    gain_set,
                )[0]
            results = [send_up, empty_ctx]
            if enc_bwd:
                start_row = (tick_index - 2) * patch_block
                grad_rows, enc_kept = encoder_backward(
                    patches[start_row : start_row + patch_block],
                    grad_now,
                    attn_mat,
                    inner_w,
                    outer_w,
                    gain_set,
                )
                results = results + [grad_rows, enc_kept]
            if dec_on:
                results = results + [empty_caption, empty_caption, zero_set(dec_shapes)]
            return tuple(results)

        def decoder_tick(
            operands, tick_index=tick_index, enc_fwd=enc_fwd, enc_bwd=enc_bwd, dec_on=dec_on
        ):
            context_now, grad_now = operands
            results = [empty_ctx]
            send_down = empty_ctx
            extra = []
            if dec_on:
                micro_index = tick_index - 1
                start_row = micro_index * caption_block
                start_seq = micro_index * ROWS_MB
                out_rows, grad_rows, send_down, dec_kept = decoder_step(
                    captions[start_row : start_row + caption_block],
                    context_now,
                    segments[start_seq : start_seq + ROWS_MB],
                    seg_images[start_seq : start_seq + ROWS_MB],
                    cotangent[start_row : start_row + caption_block],
                    attn_mat,
                    inner_w,
                    outer_w,
                    gain_set,
                )
                extra = [out_rows, grad_rows, dec_kept]
            results = results + [send_down]
            if enc_bwd:
                results = results + [empty_patch, zero_set(enc_shapes)]
            return tuple(results + extra)

        outcome = lax.cond(is_first, encoder_tick, decoder_tick, (context_in, grad_in))
        send_up, send_down = (outcome[0], outcome[1])
        rest = list(outcome[2:])
        if enc_bwd:
            patch_rows_list.append(rest[0])
            enc_list.append(rest[1])
            rest = rest[2:]
        if dec_on:
            decoded_list.append(rest[0])
            caption_rows_list.append(rest[1])
            dec_list.append(rest[2])
        if enc_fwd:
            context_in = pass_up(send_up)
        if dec_on:
            grad_in = pass_down(send_down)
    all_parts = weight_pass(is_first, enc_list, dec_list)
    attn_part = jnp.concatenate(all_parts[:3], 1).astype(low_kind)
    attn_share, in_share, out_share, gain_share = summed_shares(
        attn_part, all_parts[3].astype(low_kind), all_parts[4].astype(low_kind), all_parts[5]
    )
    patch_grad = jnp.concatenate(patch_rows_list, 0)
    decoded = jnp.concatenate(decoded_list, 0)
    caption_grad = jnp.concatenate(caption_rows_list, 0)
    half_width = D // 2
    sent_patch = shifted(patch_grad[:, half_width:].astype(jnp.bfloat16), "section", 1).astype(
        jnp.float32
    )
    patch_out = jnp.where(is_first, patch_grad[:, :half_width], sent_patch)
    got_decoded, got_grad = (
        shifted(decoded[:, :half_width].astype(jnp.bfloat16), "section", -1).astype(jnp.float32),
        shifted(caption_grad[:, :half_width].astype(jnp.bfloat16), "section", -1).astype(
            jnp.float32
        ),
    )
    decoded_out = jnp.where(is_first, got_decoded, decoded[:, half_width:]).astype(jnp.bfloat16)
    caption_out = jnp.where(is_first, got_grad, caption_grad[:, half_width:])
    return (
        decoded_out,
        caption_out,
        patch_out,
        attn_share[None],
        in_share[None],
        out_share[None],
        gain_share[None],
    )


def solution(mesh):
    placed = (
        P("dp", None),
        P("dp", None),
        P("dp", None),
        P("dp", None),
        P("section", None, None),
        P("section", None, None),
        P("section", None, None),
        P("section", None, None),
        P("dp", None),
    )
    return jax.shard_map(
        local,
        mesh=mesh,
        in_specs=placed,
        out_specs=(
            P("dp", "section"),
            P("dp", "section"),
            P("dp", "section"),
            P("section", "dp", None),
            P("section", "dp", None),
            P("section", "dp", None),
            P("section", None, "dp"),
        ),
        check_vma=False,
    )
```

```python
import functools
import jax
import jax.numpy as jnp
from jax import lax
from jax.experimental import pallas as pl
from jax.experimental.pallas import tpu as pltpu
from jax.sharding import PartitionSpec as P

D = 768
FF = 3072
HEADS = 12
HEAD = 64
PATCHES = 196
ROW = 128
SEGS = 4
MICRO = 2
IMG_MB = 2
ROWS_MB = 2
NORM_EPS = 1e-06
SCORE_SCALE = 0.125
MASKED = -1e30
ROOT_HALF = 0.7071067811865476
INV_ROOT_TWO_PI = 0.3989422804014327
MESH = pl.DeviceIdType.MESH
MIB = 1 << 20

LOW = jnp.bfloat16
WIDE = jnp.float32
IMG_ROWS = -(-PATCHES // 16) * 16
ENC_MB = IMG_MB * IMG_ROWS
ENC_ROWS = MICRO * ENC_MB
DEC_MB = ROWS_MB * ROW
DEC_ROWS = MICRO * DEC_MB
PAIR = 2 * HEAD
PAIRS = HEADS // 2
HALF = D // 2
QUARTER = D // 4


def dot_nn(left, right):
    return lax.dot_general(left, right, (((1,), (0,)), ((), ())), preferred_element_type=WIDE)


def dot_nt(left, right):
    return lax.dot_general(left, right, (((1,), (1,)), ((), ())), preferred_element_type=WIDE)


def dot_tn(left, right):
    return lax.dot_general(left, right, (((0,), (0,)), ((), ())), preferred_element_type=WIDE)


def rows_at(start, size):
    return pl.ds(pl.multiple_of(start, 16), size)


def cols_at(start, size):
    return pl.ds(pl.multiple_of(start, 128), size)


def norm_hat(values):
    centred = values - jnp.mean(values, -1, keepdims=True)
    inverse = lax.rsqrt(jnp.mean(centred * centred, -1, keepdims=True) + NORM_EPS)
    return centred * inverse, inverse


def norm_low(values, gain):
    return (norm_hat(values)[0] * gain).astype(LOW)


def norm_back(upstream, values, gain):
    normed, inverse = norm_hat(values)
    scaled = upstream * gain
    inner = (
        scaled
        - jnp.mean(scaled, -1, keepdims=True)
        - normed * jnp.mean(scaled * normed, -1, keepdims=True)
    )
    return inner * inverse, jnp.sum(upstream * normed, 0, keepdims=True)


def gelu_parts(hidden):
    normal_cdf = 0.5 * (1.0 + lax.erf(hidden * ROOT_HALF))
    slope = normal_cdf + hidden * INV_ROOT_TWO_PI * jnp.exp(-0.5 * hidden * hidden)
    return hidden * normal_cdf, slope


def first_lanes(rows):
    return lax.broadcasted_iota(jnp.int32, (rows, PAIR), 1) < HEAD


def split_pair(block):
    first = (lax.broadcasted_iota(jnp.int32, (1, PAIR), 1) < HEAD).astype(WIDE)
    return jnp.concatenate([block * first.astype(LOW), block * (1.0 - first).astype(LOW)], 0)


def join_pair(stacked):
    rows = stacked.shape[0] // 2
    return jnp.where(first_lanes(rows), stacked[:rows], stacked[rows:])


def attend_pair(queries, keys, values, bias):
    stacked = split_pair(queries) * jnp.asarray(SCORE_SCALE, LOW)
    scores = dot_nt(stacked, keys) + bias
    powers = jnp.exp(scores - jnp.max(scores, -1, keepdims=True))
    chances = powers * (1.0 / jnp.sum(powers, -1, keepdims=True))
    return join_pair(dot_nn(chances.astype(LOW), values)).astype(LOW)


def attend_pair_back(queries, keys, values, grad_mixed, bias):
    stacked = split_pair(queries) * jnp.asarray(SCORE_SCALE, LOW)
    grads = split_pair(grad_mixed)
    scores = dot_nt(keys, stacked) + bias
    powers = jnp.exp(scores - jnp.max(scores, 0, keepdims=True))
    chances = powers * (1.0 / jnp.sum(powers, 0, keepdims=True))
    grad_chances = dot_nt(values, grads)
    inner = jnp.sum(grad_chances * chances, 0, keepdims=True)
    grad_scores = (chances * (grad_chances - inner)).astype(LOW)
    grad_keys = dot_nn(grad_scores, stacked)
    grad_values = dot_nn(chances.astype(LOW), grads)
    grad_queries = join_pair(dot_tn(grad_scores, keys)) * SCORE_SCALE
    return grad_queries.astype(LOW), grad_keys.astype(LOW), grad_values.astype(LOW)


def loop(count, body):
    lax.fori_loop(0, count, lambda i, carry: (body(i), carry)[1], 0)


def main_kernel(*refs):
    (
        patches, captions, segments, seg_images, attn_w, w_in, w_out, gains, cot,
        a_out, o_out, c_out, b_out, u_out, dqkv_out, g1_out, g2_out, dh_out,
        co_out, dq_out, up_out, dctx_out, gain_out, patch_own, decoded_own, caption_own, exch_out,
        wa, wi, wo, wctx, x, ct, a, o, b, c, qkv, u, slope, x1, x2, g1, g2, landed, dmix, ctx,
        co, cq, g2w, tmp, sent, bias, bias_t, exch, decoded_half,
        load_sem, out_sem, up_send, up_recv, ctx_send, ctx_recv,
    ) = refs
    section = lax.axis_index("section")
    dp = lax.axis_index("dp")
    quarter = dp % 4
    side = dp + 2 * (1 - 2 * ((dp // 2) % 2))
    twin = dp + 1 - 2 * (dp % 2)
    other_quarter = quarter + 2 * (1 - 2 * (quarter // 2))
    barrier = pltpu.get_barrier_semaphore()
    for target in ({"section": 1 - section}, {"dp": side}, {"dp": twin}):
        pl.semaphore_signal(barrier, inc=1, device_id=target, device_id_type=MESH)
    pl.semaphore_wait(barrier, 3)

    gain_out[...] = jnp.zeros_like(gain_out)
    first_gain, second_gain, third_gain = gains[0, 0:1, :], gains[0, 1:2, :], gains[0, 2:3, :]

    def across(src, index):
        return pltpu.make_async_remote_copy(
            src_ref=src, dst_ref=landed.at[index], send_sem=up_send.at[index],
            recv_sem=up_recv.at[index], device_id={"section": 1 - section}, device_id_type=MESH)

    def ctx_part(index):
        return wctx.at[rows_at(index * QUARTER, QUARTER), :]

    def ctx_copy(src, part, target, slot):
        return pltpu.make_async_remote_copy(
            src_ref=src, dst_ref=ctx_part(part), send_sem=ctx_send.at[slot],
            recv_sem=ctx_recv.at[slot], device_id=target, device_id_type=MESH)

    def load(src, dst, slot):
        return pltpu.make_async_copy(src, dst, load_sem.at[slot])

    weight_loads = [
        load(attn_w.at[0, :, 0 : 3 * D], wa.at[:, 0 : 3 * D], 0),
        load(attn_w.at[0, :, 3 * D :], wa.at[:, 3 * D :], 1),
        load(w_in.at[0], wi, 2),
        load(w_out.at[0], wo, 3),
    ]

    def store(src, dst, slot):
        return pltpu.make_async_copy(src, dst, out_sem.at[slot])

    def add_gain(index, row):
        gain_out[index : index + 1, :] = gain_out[index : index + 1, :] + row

    def encoder():
        ctx_copy(
            attn_w.at[0, rows_at(quarter * QUARTER, QUARTER), 4 * D : 6 * D], quarter,
            {"section": 1 - section}, 0,
        ).start()
        rows_in = load(patches, g1.at[0 : patches.shape[0]], 4)
        rows_in.start()
        for copy in weight_loads:
            copy.start()
        rows_in.wait()
        for image in range(MICRO * IMG_MB):
            low_rows = g1[image * PATCHES : (image + 1) * PATCHES, :]
            x[image * IMG_ROWS : image * IMG_ROWS + PATCHES, :] = low_rows
            x[image * IMG_ROWS + PATCHES : (image + 1) * IMG_ROWS, :] = jnp.zeros(
                (IMG_ROWS - PATCHES, D), LOW
            )
        key_bias = jnp.where(
            lax.broadcasted_iota(jnp.int32, (1, IMG_ROWS), 1) < PATCHES, 0.0, MASKED
        )
        key_bias_t = jnp.where(
            lax.broadcasted_iota(jnp.int32, (IMG_ROWS, 1), 0) < PATCHES, 0.0, MASKED
        )

        def forward(micro):
            base = micro * ENC_MB
            rows = rows_at(base, ENC_MB)

            def low_norm(i):
                part = rows_at(base + i * IMG_ROWS, IMG_ROWS)
                a[part, :] = norm_low(x[part, :].astype(WIDE), first_gain)

            loop(IMG_MB, low_norm)

            @pl.when(micro == 0)
            def _():
                weight_loads[0].wait()

            def project(j):
                cols = cols_at(j * D, D)
                qkv[rows, cols] = dot_nn(a[rows, :], wa[:, cols]).astype(LOW)

            loop(3, project)

            def attend(i):
                part = rows_at(base + (i // PAIRS) * IMG_ROWS, IMG_ROWS)
                lane = (i % PAIRS) * PAIR
                o[part, cols_at(lane, PAIR)] = attend_pair(
                    qkv[part, cols_at(lane, PAIR)], qkv[part, cols_at(D + lane, PAIR)],
                    qkv[part, cols_at(2 * D + lane, PAIR)], key_bias,
                )

            loop(IMG_MB * PAIRS, attend)

            @pl.when(micro == 0)
            def _():
                weight_loads[1].wait()

            x1[rows, :] = x[rows, :].astype(WIDE) + dot_nn(o[rows, :], wa[:, 3 * D : 4 * D])

            def mid_norm(i):
                part = rows_at(base + i * IMG_ROWS, IMG_ROWS)
                b[part, :] = norm_low(x1[part, :], second_gain)

            loop(IMG_MB, mid_norm)

            @pl.when(micro == 0)
            def _():
                weight_loads[2].wait()

            def expand(j):
                cols = cols_at(j * 512, 512)
                active, bend = gelu_parts(dot_nn(b[rows, :], wi[:, cols]))
                u[rows, cols] = active.astype(LOW)
                slope[rows, cols] = bend.astype(LOW)

            loop(FF // 512, expand)

            @pl.when(micro == 0)
            def _():
                weight_loads[3].wait()

            x2[rows, :] = x1[rows, :] + dot_nn(u[rows, :], wo[...])

            def top_norm(i):
                part = rows_at(base + i * IMG_ROWS, IMG_ROWS)
                c[part, :] = norm_low(x2[part, :], third_gain)

            loop(IMG_MB, top_norm)
            across(c.at[rows, :], micro).start()

        loop(MICRO, forward)
        stores = [store(a, a_out, 0), store(o, o_out, 1), store(b, b_out, 2), store(u, u_out, 3)]
        for copy in stores:
            copy.start()

        def backward(micro):
            base = micro * ENC_MB
            rows = rows_at(base, ENC_MB)
            across(c.at[rows, :], micro).wait()

            def top_norm(i):
                part = rows_at(base + i * IMG_ROWS, IMG_ROWS)
                upstream = landed[micro, rows_at(i * IMG_ROWS, IMG_ROWS), :].astype(WIDE)
                grad, gain_row = norm_back(upstream, x2[part, :], third_gain)
                x2[part, :] = grad
                g2[part, :] = grad.astype(LOW)
                add_gain(2, gain_row)

            loop(IMG_MB, top_norm)

            def expand(j):
                cols = cols_at(j * D, D)
                hidden = dot_nt(g2[rows, :], wo[cols, :])
                slope[rows, cols] = (hidden * slope[rows, cols].astype(WIDE)).astype(LOW)

            loop(FF // D, expand)
            tmp[0:ENC_MB, :] = dot_nt(slope[rows, :], wi[...])

            def mid_norm(i):
                part = rows_at(base + i * IMG_ROWS, IMG_ROWS)
                grad, gain_row = norm_back(
                    tmp[rows_at(i * IMG_ROWS, IMG_ROWS), :], x1[part, :], second_gain
                )
                grad = grad + x2[part, :]
                x1[part, :] = grad
                g1[part, :] = grad.astype(LOW)
                add_gain(1, gain_row)

            loop(IMG_MB, mid_norm)
            dmix[0:ENC_MB, :] = dot_nt(g1[rows, :], wa[:, 3 * D : 4 * D]).astype(LOW)

            def attend(i):
                part = rows_at(base + (i // PAIRS) * IMG_ROWS, IMG_ROWS)
                lane = (i % PAIRS) * PAIR
                grads = attend_pair_back(
                    qkv[part, cols_at(lane, PAIR)], qkv[part, cols_at(D + lane, PAIR)],
                    qkv[part, cols_at(2 * D + lane, PAIR)],
                    dmix[rows_at((i // PAIRS) * IMG_ROWS, IMG_ROWS), cols_at(lane, PAIR)], key_bias_t,
                )
                for index in range(3):
                    qkv[part, cols_at(index * D + lane, PAIR)] = grads[index]

            loop(IMG_MB * PAIRS, attend)
            tmp[0:ENC_MB, :] = dot_nt(qkv[rows, :], wa[:, 0 : 3 * D])

            def low_norm(i):
                part = rows_at(base + i * IMG_ROWS, IMG_ROWS)
                grad, gain_row = norm_back(
                    tmp[rows_at(i * IMG_ROWS, IMG_ROWS), :], x[part, :].astype(WIDE), first_gain
                )
                x1[part, :] = x1[part, :] + grad
                exch[part, :] = x1[part, HALF:].astype(LOW)
                add_gain(0, gain_row)

            loop(IMG_MB, low_norm)

        loop(MICRO, backward)
        late = [
            store(qkv, dqkv_out, 4), store(g1, g1_out, 5), store(g2, g2_out, 6),
            store(slope, dh_out, 7), store(x1.at[:, 0:HALF], patch_own, 8), store(exch, exch_out, 9),
        ]
        for copy in late:
            copy.start()
        for copy in stores + late:
            copy.wait()
        ctx_copy(
            attn_w.at[0, rows_at(quarter * QUARTER, QUARTER), 4 * D : 6 * D], quarter,
            {"section": 1 - section}, 0,
        ).wait_send()

    def decoder():
        rows_in = load(captions, x.at[0:DEC_ROWS], 4)
        cot_in = load(cot, ct, 5)
        rows_in.start()
        for copy in weight_loads:
            copy.start()
        cot_in.start()
        rows_in.wait()
        full = slice(0, DEC_ROWS)

        def low_norm(i):
            part = rows_at(i * ROW, ROW)
            a[part, :] = norm_low(x[part, :].astype(WIDE), first_gain)

        loop(DEC_ROWS // ROW, low_norm)
        weight_loads[0].wait()

        def project(j):
            cols = cols_at(j * D, D)
            qkv[full, cols] = dot_nn(a[full, :], wa[:, cols]).astype(LOW)

        loop(3, project)

        def segment_pair(row):
            across_rows = jnp.broadcast_to(
                segments[pl.ds(row, 1), :].astype(WIDE), (ROW, ROW)
            )
            return across_rows, across_rows.T

        def self_bias(row, transposed):
            along, down = segment_pair(row)
            sub = lax.broadcasted_iota(jnp.int32, (ROW, ROW), 0)
            lane = lax.broadcasted_iota(jnp.int32, (ROW, ROW), 1)
            order = (lane >= sub) if transposed else (sub >= lane)
            single = jnp.where((along == down) & order, 0.0, MASKED)
            return jnp.concatenate([single, single], 1 if transposed else 0)

        def self_attend(row):
            part = rows_at(row * ROW, ROW)
            row_bias = self_bias(row, False)

            def pair(i):
                lane = i * PAIR
                o[part, cols_at(lane, PAIR)] = attend_pair(
                    qkv[part, cols_at(lane, PAIR)], qkv[part, cols_at(D + lane, PAIR)],
                    qkv[part, cols_at(2 * D + lane, PAIR)], row_bias,
                )

            loop(PAIRS, pair)

        loop(DEC_ROWS // ROW, self_attend)
        weight_loads[1].wait()
        x1[full, :] = x[full, :].astype(WIDE) + dot_nn(o[full, :], wa[:, 3 * D : 4 * D])

        def mid_norm(i):
            part = rows_at(i * ROW, ROW)
            c[part, :] = norm_low(x1[part, :], second_gain)

        loop(DEC_ROWS // ROW, mid_norm)
        cq[...] = dot_nn(c[full, :], wa[:, 4 * D : 5 * D]).astype(LOW)
        weight_loads[3].wait()
        cot_in.wait()

        def cot_project(j):
            cols = cols_at(j * D, D)
            slope[full, cols] = dot_nt(ct[...], wo[cols, :]).astype(LOW)

        loop(FF // D, cot_project)
        weight_loads[2].wait()

        ctx_copy(ctx_part(quarter), quarter, {"section": 1 - section}, 0).wait_recv()
        ctx_copy(ctx_part(quarter), quarter, {"dp": side}, 1).start()
        ctx_copy(ctx_part(quarter), quarter, {"dp": twin}, 2).start()
        ctx_copy(ctx_part(quarter), other_quarter, {"dp": side}, 1).wait_recv()
        ctx_copy(ctx_part(other_quarter), other_quarter, {"dp": twin}, 3).start()
        ctx_copy(ctx_part(quarter), quarter, {"dp": twin}, 2).wait_recv()
        ctx_copy(ctx_part(quarter), quarter, {"dp": twin}, 3).wait_recv()

        def cross_bias(micro):
            key = lax.broadcasted_iota(jnp.int32, (ROW, ENC_MB), 1)
            key_t = lax.broadcasted_iota(jnp.int32, (ENC_MB, ROW), 0)

            def one(i):
                row = micro * ROWS_MB + i
                along, down = segment_pair(row)
                image_along = jnp.zeros((ROW, ROW), WIDE)
                image_down = jnp.zeros((ROW, ROW), WIDE)
                for seg in range(SEGS):
                    image = seg_images[row, seg].astype(WIDE)
                    image_along = jnp.where(along == seg, image, image_along)
                    image_down = jnp.where(down == seg, image, image_down)
                allowed = jnp.zeros((ROW, ENC_MB), jnp.bool_)
                allowed_t = jnp.zeros((ENC_MB, ROW), jnp.bool_)
                for image in range(IMG_MB):
                    low, high = image * IMG_ROWS, image * IMG_ROWS + PATCHES
                    allowed = allowed | (
                        (key >= low) & (key < high) & (image_down[:, 0:1] == image)
                    )
                    allowed_t = allowed_t | (
                        (key_t >= low) & (key_t < high) & (image_along[0:1, :] == image)
                    )
                bias[rows_at(i * ROW, ROW), :] = jnp.where(allowed, 0.0, MASKED)
                bias_t[i] = jnp.where(allowed_t, 0.0, MASKED)

            loop(ROWS_MB, one)

        def cross(micro):
            cross_bias(micro)
            base = micro * DEC_MB
            rows = rows_at(base, DEC_MB)
            keys = rows_at(micro * ENC_MB, ENC_MB)
            across(sent.at[micro], micro).wait_recv()

            def context(j):
                cols = cols_at(j * D, D)
                ctx[keys, cols] = dot_nn(landed[micro], wctx[:, cols]).astype(LOW)

            loop(2, context)

            def attend(i):
                lane = i * PAIR
                half_bias = bias[...]
                co[rows, cols_at(lane, PAIR)] = attend_pair(
                    cq[rows, cols_at(lane, PAIR)], ctx[keys, cols_at(lane, PAIR)],
                    ctx[keys, cols_at(D + lane, PAIR)], jnp.concatenate([half_bias, half_bias], 0),
                )

            loop(PAIRS, attend)
            x2[rows, :] = x1[rows, :] + dot_nn(co[rows, :], wa[:, 5 * D : 6 * D])

            def top_norm(i):
                part = rows_at(base + i * ROW, ROW)
                b[part, :] = norm_low(x2[part, :], third_gain)

            loop(ROWS_MB, top_norm)

            def expand(j):
                cols = cols_at(j * 512, 512)
                active, bend = gelu_parts(dot_nn(b[rows, :], wi[:, cols]))
                u[rows, cols] = active.astype(LOW)
                slope[rows, cols] = (bend * slope[rows, cols].astype(WIDE)).astype(LOW)

            loop(FF // 512, expand)
            tmp[0:DEC_MB, :] = dot_nt(slope[rows, :], wi[...])

            def top_back(i):
                part = rows_at(base + i * ROW, ROW)
                grad, gain_row = norm_back(tmp[rows_at(i * ROW, ROW), :], x2[part, :], third_gain)
                grad = grad + ct[part, :].astype(WIDE)
                g2w[part, :] = grad
                g2[part, :] = grad.astype(LOW)
                add_gain(2, gain_row)

            loop(ROWS_MB, top_back)
            dmix[0:DEC_MB, :] = dot_nt(g2[rows, :], wa[:, 5 * D : 6 * D]).astype(LOW)

            def attend_back(i):
                lane = i * PAIR
                parts = [bias_t[j] for j in range(ROWS_MB)]
                grads = attend_pair_back(
                    cq[rows, cols_at(lane, PAIR)], ctx[keys, cols_at(lane, PAIR)],
                    ctx[keys, cols_at(D + lane, PAIR)], dmix[0:DEC_MB, cols_at(lane, PAIR)],
                    jnp.concatenate(parts + parts, 1),
                )
                cq[rows, cols_at(lane, PAIR)] = grads[0]
                ctx[keys, cols_at(lane, PAIR)] = grads[1]
                ctx[keys, cols_at(D + lane, PAIR)] = grads[2]

            loop(PAIRS, attend_back)
            sent[micro] = dot_nt(ctx[keys, :], wctx[...]).astype(LOW)
            across(sent.at[micro], micro).start()

        loop(MICRO, cross)
        stores = [
            store(a.at[full], a_out.at[full], 0), store(o.at[full], o_out.at[full], 1),
            store(b.at[full], b_out.at[full], 2), store(u.at[full], u_out.at[full], 3),
            store(slope.at[full], dh_out.at[full], 7), store(g2.at[full], g2_out.at[full], 6),
            store(co, co_out, 10), store(cq, dq_out, 11), store(landed, up_out, 12),
            store(ctx, dctx_out, 13), store(c.at[full], c_out.at[full], 14),
        ]
        for copy in stores:
            copy.start()

        def finish(micro):
            base = micro * DEC_MB
            rows = rows_at(base, DEC_MB)
            tmp[0:DEC_MB, :] = dot_nt(cq[rows, :], wa[:, 4 * D : 5 * D])

            def mid_back(i):
                part = rows_at(base + i * ROW, ROW)
                grad, gain_row = norm_back(tmp[rows_at(i * ROW, ROW), :], x1[part, :], second_gain)
                grad = grad + g2w[part, :]
                x1[part, :] = grad
                g1[part, :] = grad.astype(LOW)
                add_gain(1, gain_row)

            loop(ROWS_MB, mid_back)
            dmix[0:DEC_MB, :] = dot_nt(g1[rows, :], wa[:, 3 * D : 4 * D]).astype(LOW)

            def self_back(i):
                part = rows_at(base + i * ROW, ROW)
                row_bias = self_bias(micro * ROWS_MB + i, True)

                def pair(j):
                    lane = j * PAIR
                    grads = attend_pair_back(
                        qkv[part, cols_at(lane, PAIR)], qkv[part, cols_at(D + lane, PAIR)],
                        qkv[part, cols_at(2 * D + lane, PAIR)],
                        dmix[rows_at(i * ROW, ROW), cols_at(lane, PAIR)], row_bias,
                    )
                    for index in range(3):
                        qkv[part, cols_at(index * D + lane, PAIR)] = grads[index]

                loop(PAIRS, pair)

            loop(ROWS_MB, self_back)
            tmp[0:DEC_MB, :] = dot_nt(qkv[rows, :], wa[:, 0 : 3 * D])

            def low_back(i):
                part = rows_at(base + i * ROW, ROW)
                grad, gain_row = norm_back(
                    tmp[rows_at(i * ROW, ROW), :], x[part, :].astype(WIDE), first_gain
                )
                x1[part, :] = x1[part, :] + grad
                exch[rows_at(DEC_ROWS + base + i * ROW, ROW), :] = x1[part, 0:HALF].astype(LOW)
                add_gain(0, gain_row)

            loop(ROWS_MB, low_back)
            decoded = (x2[rows, :] + dot_nn(u[rows, :], wo[...])).astype(LOW)
            exch[rows, :] = decoded[:, 0:HALF]
            decoded_half[rows, :] = decoded[:, HALF:]

        loop(MICRO, finish)
        late = [
            store(qkv.at[full], dqkv_out.at[full], 4), store(g1.at[full], g1_out.at[full], 5),
            store(x1.at[full, HALF:], caption_own, 8), store(exch, exch_out, 9),
            store(decoded_half, decoded_own, 15),
        ]
        for copy in late:
            copy.start()
        for copy in stores + late:
            copy.wait()
        for micro in range(MICRO):
            across(sent.at[micro], micro).wait_send()
        ctx_copy(ctx_part(quarter), quarter, {"dp": side}, 1).wait_send()
        ctx_copy(ctx_part(quarter), quarter, {"dp": twin}, 2).wait_send()
        ctx_copy(ctx_part(quarter), quarter, {"dp": twin}, 3).wait_send()

    @pl.when(section == 0)
    def _():
        encoder()

    @pl.when(section == 1)
    def _():
        decoder()


def main_call(patches, captions, segments, seg_images, attn_w, w_in, w_out, gains, cot):
    def low(*shape):
        return jax.ShapeDtypeStruct(shape, LOW)

    def wide(*shape):
        return jax.ShapeDtypeStruct(shape, WIDE)

    outs = [
        low(ENC_ROWS, D), low(ENC_ROWS, D), low(DEC_ROWS, D), low(ENC_ROWS, D), low(ENC_ROWS, FF),
        low(ENC_ROWS, 3 * D), low(ENC_ROWS, D), low(ENC_ROWS, D), low(ENC_ROWS, FF),
        low(DEC_ROWS, D), low(DEC_ROWS, D), low(MICRO, ENC_MB, D), low(ENC_ROWS, 2 * D),
        wide(8, D), wide(ENC_ROWS, HALF), low(DEC_ROWS, HALF), wide(DEC_ROWS, HALF),
        low(2 * DEC_ROWS, HALF),
    ]
    any_spec = pl.BlockSpec(memory_space=pl.ANY)
    vmem_spec = pl.BlockSpec(memory_space=pltpu.VMEM)
    out_specs = [any_spec] * len(outs)
    out_specs[13] = vmem_spec
    vmem = pltpu.VMEM
    scratch = [
        vmem((D, 6 * D), LOW), vmem((D, FF), LOW), vmem((FF, D), LOW), vmem((D, 2 * D), LOW),
        vmem((ENC_ROWS, D), LOW), vmem((DEC_ROWS, D), LOW),
        vmem((ENC_ROWS, D), LOW), vmem((ENC_ROWS, D), LOW), vmem((ENC_ROWS, D), LOW),
        vmem((ENC_ROWS, D), LOW),
        vmem((ENC_ROWS, 3 * D), LOW), vmem((ENC_ROWS, FF), LOW), vmem((ENC_ROWS, FF), LOW),
        vmem((ENC_ROWS, D), WIDE), vmem((ENC_ROWS, D), WIDE),
        vmem((ENC_ROWS, D), LOW), vmem((ENC_ROWS, D), LOW),
        vmem((MICRO, ENC_MB, D), LOW), vmem((max(ENC_MB, DEC_ROWS), D), LOW),
        vmem((ENC_ROWS, 2 * D), LOW),
        vmem((DEC_ROWS, D), LOW), vmem((DEC_ROWS, D), LOW), vmem((DEC_ROWS, D), WIDE),
        vmem((ENC_MB, D), WIDE), vmem((MICRO, ENC_MB, D), LOW),
        vmem((DEC_MB, ENC_MB), WIDE), vmem((ROWS_MB, ENC_MB, ROW), WIDE),
        vmem((2 * DEC_ROWS, HALF), LOW), vmem((DEC_ROWS, HALF), LOW),
        pltpu.SemaphoreType.DMA((6,)), pltpu.SemaphoreType.DMA((16,)),
        pltpu.SemaphoreType.DMA((MICRO,)), pltpu.SemaphoreType.DMA((MICRO,)),
        pltpu.SemaphoreType.DMA((4,)), pltpu.SemaphoreType.DMA((4,)),
    ]
    return pl.pallas_call(
        main_kernel,
        name="layers",
        out_shape=outs,
        in_specs=[any_spec, any_spec, vmem_spec, pl.BlockSpec(memory_space=pltpu.SMEM)]
        + [any_spec] * 3 + [vmem_spec, any_spec],
        out_specs=out_specs,
        scratch_shapes=scratch,
        compiler_params=pltpu.CompilerParams(
            collective_id=1, has_side_effects=True, vmem_limit_bytes=63 * MIB
        ),
    )(patches, captions, segments, seg_images, attn_w, w_in, w_out, gains, cot)


CHUNK = 256
SLOTS = 8
FIRST_LAG = 2
LAG = 2
GAIN_STEPS = 5
OUT_IDS = 12
ONLY_DEC = 12
CTX_IDS = 6


def grads_kernel(n_bits, *refs):
    (
        a_in, o_in, c_in, b_in, u_in, dqkv_in, g1_in, g2_in, dh_in, co_in, dq_in, up_in, dctx_in,
        gains_in, patch_own, decoded_own, caption_own, exch_in, cot_in,
        shares, gains_out, patch_out, decoded_out, caption_out,
        a, o, c, b, u, dqkv, g1, g2, dh, co, dq, up, dctx, cot,
        part, ctx_sum, exch, patch_rows, gain_sum, gain_in,
    ) = refs[:44]
    recv = refs[44 : 44 + n_bits]
    load_sem, own_sem, send_sem, recv_sem, gain_send, gain_recv, far_send, far_recv = refs[44 + n_bits :]
    section = lax.axis_index("section")
    dp = lax.axis_index("dp")
    bits = [(dp // (1 << k)) % 2 for k in range(n_bits)]
    partners = [{"dp": dp + (1 << k) * (1 - 2 * bits[k])} for k in range(n_bits)]
    across = {"section": 1 - section}
    barrier = pltpu.get_barrier_semaphore()
    for target in partners + [across]:
        pl.semaphore_signal(barrier, inc=1, device_id=target, device_id_type=MESH)
    pl.semaphore_wait(barrier, n_bits + 1)

    rows = part.shape[-2]
    owners = 1 << n_bits
    total = recv[0].shape[0]
    begin = ONLY_DEC * (1 - section)

    def remote(src, dst, send, receive, target):
        return pltpu.make_async_remote_copy(
            src_ref=src, dst_ref=dst, send_sem=send, recv_sem=receive, device_id=target,
            device_id_type=MESH)

    def gain_copy(k):
        return remote(gain_sum.at[k], gain_in.at[k], gain_send.at[k], gain_recv.at[k], partners[k])

    def exch_copy():
        return remote(exch_in, exch, far_send.at[0], far_recv.at[0], across)

    def ctx_copy():
        return remote(ctx_sum, shares.at[0:CTX_IDS], far_send.at[1], far_recv.at[1], across)

    gain_sum[0] = gains_in[...]
    gain_copy(0).start()

    def load_plan(is_dec):
        count = DEC_ROWS if is_dec else ENC_ROWS

        def short(src, dst):
            return src.at[0:count], dst.at[0:count]

        plan = {
            0: short(u_in, u), 1: short(g2_in, g2), 2: short(b_in, b), 3: short(dh_in, dh),
            4: short(a_in, a), 5: short(dqkv_in, dqkv), 6: short(o_in, o), 7: short(g1_in, g1),
        }
        if is_dec:
            only = {
                8: (up_in, up), 9: (dctx_in, dctx), 10: (c_in, c), 11: (dq_in, dq),
                12: (co_in, co), 13: (cot_in, cot),
            }
            plan = {**only, **plan}
        return plan

    def need(is_dec, *slots):
        plan = load_plan(is_dec)
        for slot in slots:
            pltpu.make_async_copy(*plan[slot], load_sem.at[slot]).wait()

    for is_dec in (False, True):
        @pl.when(section == int(is_dec))
        def _(is_dec=is_dec):
            for slot, (src, dst) in load_plan(is_dec).items():
                pltpu.make_async_copy(src, dst, load_sem.at[slot]).start()
            if is_dec:
                pltpu.make_async_copy(decoded_own, decoded_out, load_sem.at[14]).start()
                pltpu.make_async_copy(caption_own, caption_out, load_sem.at[15]).start()
            else:
                pltpu.make_async_copy(patch_own, patch_rows, load_sem.at[14]).start()

    def core_copy(index):
        slot = index % SLOTS
        return remote(part.at[slot, 1 - bits[0]], recv[0].at[index], send_sem.at[0, index],
                      recv_sem.at[0, index], partners[0])

    def stage_copy(stage, index):
        keep = (slice(None),) * (n_bits - 1 - stage)
        return remote(
            recv[stage - 1].at[(index,) + keep + (1 - bits[stage],)], recv[stage].at[index],
            send_sem.at[stage, index], recv_sem.at[stage, index], partners[stage])

    def advance(i):
        for stage in range(n_bits):
            j = i - FIRST_LAG - stage * LAG

            @pl.when((j >= begin) & (j < total))
            def _(stage=stage, j=j):
                if stage == 0:
                    core_copy(j).wait()
                    mine = part[j % SLOTS, bits[0]]
                else:
                    stage_copy(stage, j).wait()
                    keep = (slice(None),) * (n_bits - 1 - stage)
                    mine = recv[stage - 1][(j,) + keep + (bits[stage],)]
                summed = mine.astype(WIDE) + recv[stage][j].astype(WIDE)
                if stage < n_bits - 1:
                    recv[stage][j] = summed.astype(LOW)
                    stage_copy(stage + 1, j).start()
                else:
                    @pl.when(j < CTX_IDS)
                    def _():
                        ctx_sum[j] = summed

                    @pl.when(j >= CTX_IDS)
                    def _():
                        shares[j - CTX_IDS] = summed

                    @pl.when(j == CTX_IDS - 1)
                    def _():
                        ctx_copy().start()
        for k in range(n_bits):
            @pl.when(i == ONLY_DEC + GAIN_STEPS * (k + 1))
            def _(k=k):
                gain_copy(k).wait()
                summed = gain_sum[k] + gain_in[k]
                if k == n_bits - 1:
                    gains_out[...] = summed
                else:
                    gain_sum[k + 1] = summed
                    gain_copy(k + 1).start()

    def place(index, first_owner, block):
        for k in range(block.shape[0] // rows):
            owner = first_owner + k
            path = tuple((owner >> bit) & 1 for bit in reversed(range(1, n_bits)))
            part[(index % SLOTS, owner & 1) + path] = block[k * rows : (k + 1) * rows].astype(LOW)

    def simple_phase(first, count, left, right, col, row_count):
        def step(i):
            index = first + i
            cols = cols_at(col + i * CHUNK, CHUNK)
            if row_count is None:
                value = dot_tn(left[...].reshape(-1, D), right[:, cols])
            else:
                value = dot_tn(left[0:row_count, :], right[0:row_count, cols])
            place(index, 0, value)
            core_copy(index).start()
            advance(index)
        loop(count, step)

    def out_phase(first, right, row_count):
        share = FF // owners
        blocks = share // rows
        step_owners = D // share

        def step(i):
            cols = cols_at(i * CHUNK, CHUNK)
            base = first + i * blocks
            for piece in range(FF // D):
                value = dot_tn(u[0:row_count, piece * D : (piece + 1) * D], right[0:row_count, cols])
                for k in range(step_owners):
                    for q in range(blocks):
                        low = k * share + q * rows
                        place(base + q, piece * step_owners + k, value[low : low + rows])
            loop(blocks, lambda q: core_copy(base + q).start())
            loop(blocks, lambda q: advance(base + q))
        loop(D // CHUNK, step)

    @pl.when(section == 1)
    def _():
        need(True, 8, 9)
        simple_phase(0, CTX_IDS, up, dctx, 0, None)
        need(True, 10, 11)
        simple_phase(CTX_IDS, 3, c, dq, 0, DEC_ROWS)
        need(True, 12, 1)
        simple_phase(CTX_IDS + 3, 3, co, g2, 0, DEC_ROWS)

    for is_dec in (False, True):
        @pl.when(section == int(is_dec))
        def _(is_dec=is_dec):
            count = DEC_ROWS if is_dec else ENC_ROWS
            need(is_dec, 0, 13 if is_dec else 1)
            out_phase(ONLY_DEC, cot if is_dec else g2, count)
            need(is_dec, 2, 3)
            simple_phase(ONLY_DEC + OUT_IDS, FF // CHUNK, b, dh, 0, count)

    exch_copy().start()

    for is_dec in (False, True):
        @pl.when(section == int(is_dec))
        def _(is_dec=is_dec):
            count = DEC_ROWS if is_dec else ENC_ROWS
            need(is_dec, 4, 5)
            first = ONLY_DEC + OUT_IDS + FF // CHUNK
            simple_phase(first, 3 * D // CHUNK, a, dqkv, 0, count)
            need(is_dec, 6, 7)
            simple_phase(first + 3 * D // CHUNK, D // CHUNK, o, g1, 0, count)

    exch_copy().wait()

    @pl.when(section == 0)
    def _():
        pltpu.make_async_copy(patch_own, patch_rows, load_sem.at[14]).wait()
        for image in range(MICRO * IMG_MB):
            patch_out[image * PATCHES : (image + 1) * PATCHES, :] = patch_rows[
                image * IMG_ROWS : image * IMG_ROWS + PATCHES, :
            ]
        decoded_out[...] = exch[0:DEC_ROWS, :]
        caption_out[...] = exch[DEC_ROWS : 2 * DEC_ROWS, :].astype(WIDE)

    @pl.when(section == 1)
    def _():
        pltpu.make_async_copy(decoded_own, decoded_out, load_sem.at[14]).wait()
        pltpu.make_async_copy(caption_own, caption_out, load_sem.at[15]).wait()
        for image in range(MICRO * IMG_MB):
            patch_out[image * PATCHES : (image + 1) * PATCHES, :] = exch[
                image * IMG_ROWS : image * IMG_ROWS + PATCHES, :
            ].astype(WIDE)

    loop(FIRST_LAG + (n_bits - 1) * LAG, lambda i: advance(total + i))

    @pl.when(section == 0)
    def _():
        ctx_copy().wait_recv()

    @pl.when(section == 1)
    def _():
        ctx_copy().wait_send()


def grads_call(n_dp, *operands):
    n_bits = n_dp.bit_length() - 1
    rows = D // n_dp
    share = FF // n_dp
    total = ONLY_DEC + 2 * OUT_IDS + 4 * D // CHUNK
    vmem = pltpu.VMEM
    pair = (2,) * (n_bits - 1)
    any_spec = pl.BlockSpec(memory_space=pl.ANY)
    vmem_spec = pl.BlockSpec(memory_space=pltpu.VMEM)
    sem = pltpu.SemaphoreType.DMA
    scratch = [
        vmem((ENC_ROWS, D), LOW), vmem((ENC_ROWS, D), LOW), vmem((DEC_ROWS, D), LOW),
        vmem((ENC_ROWS, D), LOW), vmem((ENC_ROWS, FF), LOW), vmem((ENC_ROWS, 3 * D), LOW),
        vmem((ENC_ROWS, D), LOW), vmem((ENC_ROWS, D), LOW), vmem((ENC_ROWS, FF), LOW),
        vmem((DEC_ROWS, D), LOW), vmem((DEC_ROWS, D), LOW), vmem((MICRO, ENC_MB, D), LOW),
        vmem((ENC_ROWS, 2 * D), LOW), vmem((DEC_ROWS, D), LOW),
        vmem((SLOTS, 2) + pair + (rows, CHUNK), LOW), vmem((CTX_IDS, rows, CHUNK), WIDE),
        vmem((2 * DEC_ROWS, HALF), LOW), vmem((ENC_ROWS, HALF), WIDE),
        vmem((n_bits, 8, D), WIDE), vmem((n_bits, 8, D), WIDE),
    ]
    scratch += [vmem((total,) + pair[k:] + (rows, CHUNK), LOW) for k in range(n_bits)]
    scratch += [
        sem((16,)), sem((1,)), sem((n_bits, total)), sem((n_bits, total)), sem((n_bits,)),
        sem((n_bits,)), sem((2,)), sem((2,)),
    ]
    in_specs = [any_spec] * len(operands)
    in_specs[13] = vmem_spec
    return pl.pallas_call(
        functools.partial(grads_kernel, n_bits),
        name="weight_sums",
        out_shape=(
            jax.ShapeDtypeStruct((total - CTX_IDS, rows, CHUNK), WIDE),
            jax.ShapeDtypeStruct((8, D), WIDE),
            jax.ShapeDtypeStruct((MICRO * IMG_MB * PATCHES, HALF), WIDE),
            jax.ShapeDtypeStruct((DEC_ROWS, HALF), LOW),
            jax.ShapeDtypeStruct((DEC_ROWS, HALF), WIDE),
        ),
        in_specs=in_specs,
        out_specs=(vmem_spec,) * 5,
        scratch_shapes=scratch,
        compiler_params=pltpu.CompilerParams(
            collective_id=2, has_side_effects=True, vmem_limit_bytes=63 * MIB
        ),
    )(*operands)


def pick_columns(chunks, rows, columns):
    shaped = chunks.reshape(columns // CHUNK, rows // chunks.shape[1], chunks.shape[1], CHUNK)
    return shaped.transpose(1, 2, 0, 3).reshape(rows, columns)


def kernel_sums(n_dp, operands):
    chunks, gain_sums, patch_out, decoded_out, caption_out = grads_call(n_dp, *operands)
    rows = D // n_dp
    last = CTX_IDS
    outer = last + OUT_IDS
    inner = outer + OUT_IDS
    attn_share = jnp.concatenate(
        [pick_columns(chunks[inner:], rows, 4 * D), pick_columns(chunks[:last], rows, 2 * D)], 1
    )
    in_share = pick_columns(chunks[outer:inner], rows, FF)
    out_share = pick_columns(chunks[last:outer], FF // n_dp, D)
    own_gains = lax.dynamic_slice_in_dim(gain_sums[:3], lax.axis_index("dp") * rows, rows, 1)
    return decoded_out, caption_out, patch_out, attn_share, in_share, out_share, own_gains


def shifted(block, distance):
    devices = range(lax.axis_size("section"))
    route = [(i - distance, i) for i in devices if i - distance in devices]
    return lax.ppermute(block, "section", route)


def plain_sums(operands):
    (
        a, o, c, b, u, dqkv, g1, g2, dh, co, dq, up, dctx,
        gains, patch_own, decoded_own, caption_own, exch, cot,
    ) = operands
    is_first = lax.axis_index("section") == 0
    up = up.reshape(ENC_ROWS, D)

    def encoder_parts():
        return (
            jnp.concatenate([dot_tn(a, dqkv), dot_tn(o, g1)], 1), jnp.zeros((D, 2 * D), WIDE),
            jnp.zeros((D, 2 * D), WIDE), dot_tn(b, dh), dot_tn(u, g2),
        )

    def decoder_parts():
        rows = slice(0, DEC_ROWS)
        return (
            jnp.concatenate([dot_tn(a[rows], dqkv[rows]), dot_tn(o[rows], g1[rows])], 1),
            jnp.concatenate([dot_tn(c, dq), dot_tn(co, g2[rows])], 1),
            dot_tn(up, dctx), dot_tn(b[rows], dh[rows]), dot_tn(u[rows], cot),
        )

    parts = lax.cond(is_first, encoder_parts, decoder_parts)
    sums = [lax.psum_scatter(part, "dp", scatter_dimension=0, tiled=True) for part in parts]
    last = jnp.where(is_first, shifted(sums[2], -1), sums[1])
    moved = lax.ppermute(exch, "section", [(0, 1), (1, 0)])

    def unpad(block):
        shaped = block[:ENC_ROWS].reshape(MICRO * IMG_MB, IMG_ROWS, HALF)
        return shaped[:, :PATCHES].reshape(-1, HALF).astype(WIDE)

    return (
        jnp.where(is_first, moved[:DEC_ROWS], decoded_own),
        jnp.where(is_first, moved[DEC_ROWS:].astype(WIDE), caption_own),
        jnp.where(is_first, unpad(patch_own), unpad(moved)),
        jnp.concatenate([sums[0], last], 1),
        sums[3],
        sums[4],
        lax.psum_scatter(gains[:3], "dp", scatter_dimension=1, tiled=True),
    )


def local(patches, captions, segments, seg_images, attn_w, w_in, w_out, norm_gains, cotangent):
    n_dp = lax.axis_size("dp")
    kept = main_call(
        patches, captions, segments, seg_images, attn_w, w_in, w_out, norm_gains, cotangent
    )
    operands = list(kept) + [cotangent]
    if n_dp & (n_dp - 1) == 0 and (D // n_dp) % 16 == 0:
        results = kernel_sums(n_dp, operands)
    else:
        results = plain_sums(operands)
    return results[:3] + tuple(share[None] for share in results[3:])


def solution(mesh):
    placed = (
        P("dp", None),
        P("dp", None),
        P("dp", None),
        P("dp", None),
        P("section", None, None),
        P("section", None, None),
        P("section", None, None),
        P("section", None, None),
        P("dp", None),
    )
    return jax.shard_map(
        local,
        mesh=mesh,
        in_specs=placed,
        out_specs=(
            P("dp", "section"),
            P("dp", "section"),
            P("dp", "section"),
            P("section", "dp", None),
            P("section", "dp", None),
            P("section", "dp", None),
            P("section", None, "dp"),
        ),
        check_vma=False,
    )
```

```python
import functools
import jax
import jax.numpy as jnp
from jax import lax
from jax.experimental import pallas as pl
from jax.experimental.pallas import tpu as pltpu
from jax.sharding import PartitionSpec as P

D = 768
FF = 3072
HEADS = 12
HEAD = 64
PATCHES = 196
ROW = 128
SEGS = 4
MICRO = 2
IMG_MB = 2
ROWS_MB = 2
NORM_EPS = 1e-06
SCORE_SCALE = 0.125
MASKED = -1e30
ROOT_HALF = 0.7071067811865476
INV_ROOT_TWO_PI = 0.3989422804014327
MESH = pl.DeviceIdType.MESH
MIB = 1 << 20

LOW = jnp.bfloat16
WIDE = jnp.float32
IMG_ROWS = -(-PATCHES // 16) * 16
ENC_MB = IMG_MB * IMG_ROWS
ENC_ROWS = MICRO * ENC_MB
DEC_MB = ROWS_MB * ROW
DEC_ROWS = MICRO * DEC_MB
PAIR = 2 * HEAD
PAIRS = HEADS // 2
HALF = D // 2
QUARTER = D // 4
CROSS_PAIRS = 3
EXPAND_UNROLL = 3
BACK_UNROLL = 4
CONTEXT_UNROLL = 2
PROJECT_UNROLL = 3
BACK_PAIRS = 3
CROSS_BACK_PAIRS = 2


def dot_nn(left, right):
    return lax.dot_general(left, right, (((1,), (0,)), ((), ())), preferred_element_type=WIDE)


def dot_nt(left, right):
    return lax.dot_general(left, right, (((1,), (1,)), ((), ())), preferred_element_type=WIDE)


def dot_tn(left, right):
    return lax.dot_general(left, right, (((0,), (0,)), ((), ())), preferred_element_type=WIDE)


def rows_at(start, size):
    return pl.ds(pl.multiple_of(start, 16), size)


def cols_at(start, size):
    if isinstance(start, int):
        return slice(start, start + size)
    return pl.ds(pl.multiple_of(start, 128), size)


def norm_hat(values):
    centred = values - jnp.mean(values, -1, keepdims=True)
    inverse = lax.rsqrt(jnp.mean(centred * centred, -1, keepdims=True) + NORM_EPS)
    return centred * inverse, inverse


def norm_low(values, gain):
    return (norm_hat(values)[0] * gain).astype(LOW)


def norm_back(upstream, values, gain):
    normed, inverse = norm_hat(values)
    scaled = upstream * gain
    inner = (
        scaled
        - jnp.mean(scaled, -1, keepdims=True)
        - normed * jnp.mean(scaled * normed, -1, keepdims=True)
    )
    return inner * inverse, jnp.sum(upstream * normed, 0, keepdims=True)


def gelu_parts(hidden):
    normal_cdf = 0.5 * (1.0 + lax.erf(hidden * ROOT_HALF))
    slope = normal_cdf + hidden * INV_ROOT_TWO_PI * jnp.exp(-0.5 * hidden * hidden)
    return hidden * normal_cdf, slope


def first_lanes(rows):
    return lax.broadcasted_iota(jnp.int32, (rows, PAIR), 1) < HEAD


def split_pair(block):
    first = (lax.broadcasted_iota(jnp.int32, (1, PAIR), 1) < HEAD).astype(WIDE)
    return jnp.concatenate([block * first.astype(LOW), block * (1.0 - first).astype(LOW)], 0)


def join_pair(stacked):
    rows = stacked.shape[0] // 2
    return jnp.where(first_lanes(rows), stacked[:rows], stacked[rows:])


def attend(pairs, bias):
    stacked = [split_pair(queries) * SCORE_SCALE for queries, _, _ in pairs]
    scores = [dot_nt(stack, pair[1]) + bias for stack, pair in zip(stacked, pairs)]
    powers = [jnp.exp(block - jnp.max(block, -1, keepdims=True)) for block in scores]
    scales = [1.0 / jnp.sum(block, -1, keepdims=True) for block in powers]
    return [
        join_pair(dot_nn(block.astype(LOW), pair[2]) * scale).astype(LOW)
        for block, pair, scale in zip(powers, pairs, scales)
    ]


def attend_back(pairs, bias):
    stacked = [split_pair(pair[0]) * SCORE_SCALE for pair in pairs]
    grads = [split_pair(pair[3]) for pair in pairs]
    scores = [dot_nt(pair[1], stack) + bias for pair, stack in zip(pairs, stacked)]
    grad_chances = [dot_nt(pair[2], grad) for pair, grad in zip(pairs, grads)]
    powers = [jnp.exp(block - jnp.max(block, 0, keepdims=True)) for block in scores]
    chances = [block * (1.0 / jnp.sum(block, 0, keepdims=True)) for block in powers]
    inner = [jnp.sum(left * right, 0, keepdims=True) for left, right in zip(grad_chances, chances)]
    grad_scores = [
        (chance * (grad - mean)).astype(LOW)
        for chance, grad, mean in zip(chances, grad_chances, inner)
    ]
    grad_keys = [dot_nn(grad, stack) for grad, stack in zip(grad_scores, stacked)]
    grad_values = [dot_nn(chance.astype(LOW), grad) for chance, grad in zip(chances, grads)]
    grad_queries = [
        join_pair(dot_tn(grad, pair[1])) * SCORE_SCALE for grad, pair in zip(grad_scores, pairs)
    ]
    return [
        tuple(part.astype(LOW) for part in parts)
        for parts in zip(grad_queries, grad_keys, grad_values)
    ]


def pair_cols(pair, column=0):
    start = column * D + pair * PAIR
    return cols_at(start, PAIR) if not isinstance(start, int) else slice(start, start + PAIR)


def attend_rows(qkv, rows, mixed, bias):
    pairs = [[qkv[rows, pair_cols(pair, part)] for part in range(3)] for pair in range(PAIRS)]
    for pair, result in enumerate(attend(pairs, bias)):
        mixed[rows, pair_cols(pair)] = result


def attend_rows_back(qkv, rows, grad_mixed, grad_rows, bias, group):
    pairs = [
        [qkv[rows, pair_cols(pair, part)] for part in range(3)]
        + [grad_mixed[grad_rows, pair_cols(pair)]]
        for pair in group
    ]
    for pair, results in zip(group, attend_back(pairs, bias)):
        for part in range(3):
            qkv[rows, pair_cols(pair, part)] = results[part]


def loop(count, body, unroll=1):
    def several(i, carry):
        for k in range(unroll):
            body(i * unroll + k)
        return carry

    if count == unroll:
        several(0, 0)
    else:
        lax.fori_loop(0, count // unroll, several, 0)


def main_kernel(*refs):
    (
        patches, captions, segments, seg_images, attn_w, w_in, w_out, gains, cot,
        a_out, o_out, c_out, b_out, u_out, dqkv_out, g1_out, g2_out, dh_out,
        co_out, dq_out, up_out, dctx_out, gain_out, patch_own, decoded_own, caption_own, exch_out,
        wa, wi, wo, wctx, x, ct, a, o, b, c, qkv, u, slope, x1, x2, g1, g2, landed, dmix, ctx,
        co, cq, g2w, tmp, sent, bias, bias_t, exch, decoded_half,
        gain_rows, load_sem, out_sem, up_send, up_recv, ctx_send, ctx_recv,
    ) = refs
    section = lax.axis_index("section")
    dp = lax.axis_index("dp")
    quarter = dp % 4
    side = dp + 2 * (1 - 2 * ((dp // 2) % 2))
    twin = dp + 1 - 2 * (dp % 2)
    other_quarter = quarter + 2 * (1 - 2 * (quarter // 2))
    barrier = pltpu.get_barrier_semaphore()
    for target in ({"section": 1 - section}, {"dp": side}, {"dp": twin}):
        pl.semaphore_signal(barrier, inc=1, device_id=target, device_id_type=MESH)
    pl.semaphore_wait(barrier, 3)

    gain_out[...] = jnp.zeros_like(gain_out)

    def across(src, index):
        return pltpu.make_async_remote_copy(
            src_ref=src, dst_ref=landed.at[index], send_sem=up_send.at[index],
            recv_sem=up_recv.at[index], device_id={"section": 1 - section}, device_id_type=MESH)

    def ctx_part(index):
        return wctx.at[rows_at(index * QUARTER, QUARTER), :]

    def ctx_copy(src, part, target, slot):
        return pltpu.make_async_remote_copy(
            src_ref=src, dst_ref=ctx_part(part), send_sem=ctx_send.at[slot],
            recv_sem=ctx_recv.at[slot], device_id=target, device_id_type=MESH)

    def load(src, dst, slot):
        return pltpu.make_async_copy(src, dst, load_sem.at[slot])

    weight_loads = [
        load(attn_w.at[0, :, 0 : 3 * D], wa.at[:, 0 : 3 * D], 0),
        load(attn_w.at[0, :, 3 * D :], wa.at[:, 3 * D :], 1),
        load(w_in.at[0], wi, 2),
        load(w_out.at[0], wo, 3),
    ]

    gain_in = load(gains.at[0], gain_rows, 6)
    gain_in.start()

    def store(src, dst, slot):
        return pltpu.make_async_copy(src, dst, out_sem.at[slot])

    def add_gain(index, row):
        gain_out[index : index + 1, :] = gain_out[index : index + 1, :] + row

    def encoder():
        ctx_copy(
            attn_w.at[0, rows_at(quarter * QUARTER, QUARTER), 4 * D : 6 * D], quarter,
            {"section": 1 - section}, 0,
        ).start()
        rows_in = load(patches, g1.at[0 : patches.shape[0]], 4)
        rows_in.start()
        for copy in weight_loads:
            copy.start()
        rows_in.wait()
        for image in range(MICRO * IMG_MB):
            low_rows = g1[image * PATCHES : (image + 1) * PATCHES, :]
            x[image * IMG_ROWS : image * IMG_ROWS + PATCHES, :] = low_rows
            x[image * IMG_ROWS + PATCHES : (image + 1) * IMG_ROWS, :] = jnp.zeros(
                (IMG_ROWS - PATCHES, D), LOW
            )
        key_bias = jnp.where(
            lax.broadcasted_iota(jnp.int32, (1, IMG_ROWS), 1) < PATCHES, 0.0, MASKED
        )
        key_bias_t = jnp.where(
            lax.broadcasted_iota(jnp.int32, (IMG_ROWS, 1), 0) < PATCHES, 0.0, MASKED
        )

        def forward(micro):
            base = micro * ENC_MB
            rows = rows_at(base, ENC_MB)

            def low_norm(i):
                part = rows_at(base + i * IMG_ROWS, IMG_ROWS)
                a[part, :] = norm_low(x[part, :].astype(WIDE), first_gain)

            loop(IMG_MB, low_norm)

            @pl.when(micro == 0)
            def _():
                weight_loads[0].wait()

            def project(j):
                cols = cols_at(j * D, D)
                qkv[rows, cols] = dot_nn(a[rows, :], wa[:, cols]).astype(LOW)

            loop(3, project, PROJECT_UNROLL)

            def attend_image(i):
                attend_rows(qkv, rows_at(base + i * IMG_ROWS, IMG_ROWS), o, key_bias)

            loop(IMG_MB, attend_image)

            @pl.when(micro == 0)
            def _():
                weight_loads[1].wait()

            x1[rows, :] = x[rows, :].astype(WIDE) + dot_nn(o[rows, :], wa[:, 3 * D : 4 * D])

            def mid_norm(i):
                part = rows_at(base + i * IMG_ROWS, IMG_ROWS)
                b[part, :] = norm_low(x1[part, :], second_gain)

            loop(IMG_MB, mid_norm)

            @pl.when(micro == 0)
            def _():
                weight_loads[2].wait()

            @pl.when(micro > 0)
            def _():
                store(u.at[0:ENC_MB], u_out.at[rows], 3).wait()

            def expand(j):
                cols = cols_at(j * 512, 512)
                active, bend = gelu_parts(dot_nn(b[rows, :], wi[:, cols]))
                u[0:ENC_MB, cols] = active.astype(LOW)
                slope[rows, cols] = bend.astype(LOW)

            loop(FF // 512, expand, EXPAND_UNROLL)

            @pl.when(micro == 0)
            def _():
                weight_loads[3].wait()

            x2[rows, :] = x1[rows, :] + dot_nn(u[0:ENC_MB, :], wo[...])
            store(u.at[0:ENC_MB], u_out.at[rows], 3).start()

            def top_norm(i):
                part = rows_at(base + i * IMG_ROWS, IMG_ROWS)
                c[part, :] = norm_low(x2[part, :], third_gain)

            loop(IMG_MB, top_norm)
            across(c.at[rows, :], micro).start()

        loop(MICRO, forward)
        stores = [store(a, a_out, 0), store(o, o_out, 1), store(b, b_out, 2)]
        for copy in stores:
            copy.start()

        def backward(micro):
            base = micro * ENC_MB
            rows = rows_at(base, ENC_MB)
            across(c.at[rows, :], micro).wait()

            def top_norm(i):
                part = rows_at(base + i * IMG_ROWS, IMG_ROWS)
                upstream = landed[micro, rows_at(i * IMG_ROWS, IMG_ROWS), :].astype(WIDE)
                grad, gain_row = norm_back(upstream, x2[part, :], third_gain)
                x2[part, :] = grad
                g2[part, :] = grad.astype(LOW)
                add_gain(2, gain_row)

            loop(IMG_MB, top_norm)

            def expand(j):
                cols = cols_at(j * D, D)
                hidden = dot_nt(g2[rows, :], wo[cols, :])
                slope[rows, cols] = (hidden * slope[rows, cols].astype(WIDE)).astype(LOW)

            loop(FF // D, expand, BACK_UNROLL)
            tmp[0:ENC_MB, :] = dot_nt(slope[rows, :], wi[...])

            def mid_norm(i):
                part = rows_at(base + i * IMG_ROWS, IMG_ROWS)
                grad, gain_row = norm_back(
                    tmp[rows_at(i * IMG_ROWS, IMG_ROWS), :], x1[part, :], second_gain
                )
                grad = grad + x2[part, :]
                x1[part, :] = grad
                g1[part, :] = grad.astype(LOW)
                add_gain(1, gain_row)

            loop(IMG_MB, mid_norm)
            dmix[0:ENC_MB, :] = dot_nt(g1[rows, :], wa[:, 3 * D : 4 * D]).astype(LOW)

            def attend_image(i):
                image = i // (PAIRS // BACK_PAIRS)
                first = (i % (PAIRS // BACK_PAIRS)) * BACK_PAIRS
                attend_rows_back(
                    qkv, rows_at(base + image * IMG_ROWS, IMG_ROWS), dmix,
                    rows_at(image * IMG_ROWS, IMG_ROWS), key_bias_t,
                    [first + pair for pair in range(BACK_PAIRS)],
                )

            loop(IMG_MB * PAIRS // BACK_PAIRS, attend_image)
            tmp[0:ENC_MB, :] = dot_nt(qkv[rows, :], wa[:, 0 : 3 * D])

            def low_norm(i):
                part = rows_at(base + i * IMG_ROWS, IMG_ROWS)
                grad, gain_row = norm_back(
                    tmp[rows_at(i * IMG_ROWS, IMG_ROWS), :], x[part, :].astype(WIDE), first_gain
                )
                x1[part, :] = x1[part, :] + grad
                exch[part, :] = x1[part, HALF:].astype(LOW)
                add_gain(0, gain_row)

            loop(IMG_MB, low_norm)

        loop(MICRO, backward)
        late = [
            store(qkv, dqkv_out, 4), store(g1, g1_out, 5), store(g2, g2_out, 6),
            store(slope, dh_out, 7), store(x1.at[:, 0:HALF], patch_own, 8), store(exch, exch_out, 9),
        ]
        for copy in late:
            copy.start()
        for copy in stores + late + [store(u.at[0:ENC_MB], u_out.at[0:ENC_MB], 3)]:
            copy.wait()
        ctx_copy(
            attn_w.at[0, rows_at(quarter * QUARTER, QUARTER), 4 * D : 6 * D], quarter,
            {"section": 1 - section}, 0,
        ).wait_send()

    def decoder():
        rows_in = load(captions, x.at[0:DEC_ROWS], 4)
        cot_in = load(cot, ct, 5)
        rows_in.start()
        for copy in weight_loads:
            copy.start()
        cot_in.start()
        rows_in.wait()
        full = slice(0, DEC_ROWS)

        def low_norm(i):
            part = rows_at(i * ROW, ROW)
            a[part, :] = norm_low(x[part, :].astype(WIDE), first_gain)

        loop(DEC_ROWS // ROW, low_norm)
        weight_loads[0].wait()

        def project(j):
            cols = cols_at(j * D, D)
            qkv[full, cols] = dot_nn(a[full, :], wa[:, cols]).astype(LOW)

        loop(3, project)

        def segment_pair(row):
            across_rows = jnp.broadcast_to(
                segments[pl.ds(row, 1), :].astype(WIDE), (ROW, ROW)
            )
            return across_rows, across_rows.T

        def self_bias(row, transposed):
            along, down = segment_pair(row)
            sub = lax.broadcasted_iota(jnp.int32, (ROW, ROW), 0)
            lane = lax.broadcasted_iota(jnp.int32, (ROW, ROW), 1)
            order = (lane >= sub) if transposed else (sub >= lane)
            single = jnp.where((along == down) & order, 0.0, MASKED)
            return jnp.concatenate([single, single], 1 if transposed else 0)

        def self_attend(row):
            attend_rows(qkv, rows_at(row * ROW, ROW), o, self_bias(row, False))

        loop(DEC_ROWS // ROW, self_attend)
        weight_loads[1].wait()
        x1[full, :] = x[full, :].astype(WIDE) + dot_nn(o[full, :], wa[:, 3 * D : 4 * D])

        def mid_norm(i):
            part = rows_at(i * ROW, ROW)
            c[part, :] = norm_low(x1[part, :], second_gain)

        loop(DEC_ROWS // ROW, mid_norm)
        cq[...] = dot_nn(c[full, :], wa[:, 4 * D : 5 * D]).astype(LOW)
        weight_loads[3].wait()
        cot_in.wait()

        def cot_project(j):
            cols = cols_at(j * D, D)
            slope[full, cols] = dot_nt(ct[...], wo[cols, :]).astype(LOW)

        loop(FF // D, cot_project)
        weight_loads[2].wait()

        ctx_copy(ctx_part(quarter), quarter, {"section": 1 - section}, 0).wait_recv()
        ctx_copy(ctx_part(quarter), quarter, {"dp": side}, 1).start()
        ctx_copy(ctx_part(quarter), quarter, {"dp": twin}, 2).start()
        ctx_copy(ctx_part(quarter), other_quarter, {"dp": side}, 1).wait_recv()
        ctx_copy(ctx_part(other_quarter), other_quarter, {"dp": twin}, 3).start()
        ctx_copy(ctx_part(quarter), quarter, {"dp": twin}, 2).wait_recv()
        ctx_copy(ctx_part(quarter), quarter, {"dp": twin}, 3).wait_recv()

        def cross_bias(micro):
            key = lax.broadcasted_iota(jnp.int32, (ROW, ENC_MB), 1)
            key_t = lax.broadcasted_iota(jnp.int32, (ENC_MB, ROW), 0)

            def one(i):
                row = micro * ROWS_MB + i
                along, down = segment_pair(row)
                image_along = jnp.zeros((ROW, ROW), WIDE)
                image_down = jnp.zeros((ROW, ROW), WIDE)
                for seg in range(SEGS):
                    image = seg_images[row, seg].astype(WIDE)
                    image_along = jnp.where(along == seg, image, image_along)
                    image_down = jnp.where(down == seg, image, image_down)
                allowed = jnp.zeros((ROW, ENC_MB), jnp.bool_)
                allowed_t = jnp.zeros((ENC_MB, ROW), jnp.bool_)
                for image in range(IMG_MB):
                    low, high = image * IMG_ROWS, image * IMG_ROWS + PATCHES
                    allowed = allowed | (
                        (key >= low) & (key < high) & (image_down[:, 0:1] == image)
                    )
                    allowed_t = allowed_t | (
                        (key_t >= low) & (key_t < high) & (image_along[0:1, :] == image)
                    )
                bias[rows_at(i * ROW, ROW), :] = jnp.where(allowed, 0.0, MASKED)
                bias_t[i] = jnp.where(allowed_t, 0.0, MASKED)

            loop(ROWS_MB, one)

        def cross(micro):
            cross_bias(micro)
            base = micro * DEC_MB
            rows = rows_at(base, DEC_MB)
            keys = rows_at(micro * ENC_MB, ENC_MB)
            across(sent.at[micro], micro).wait_recv()

            def context(j):
                cols = cols_at(j * D, D)
                ctx[keys, cols] = dot_nn(landed[micro], wctx[:, cols]).astype(LOW)

            loop(2, context, CONTEXT_UNROLL)

            def attend_some(i):
                half_bias = bias[...]
                group = [i * CROSS_PAIRS + k for k in range(CROSS_PAIRS)]
                pairs = [
                    (cq[rows, pair_cols(pair)], ctx[keys, pair_cols(pair)], ctx[keys, pair_cols(pair, 1)])
                    for pair in group
                ]
                results = attend(pairs, jnp.concatenate([half_bias, half_bias], 0))
                for pair, result in zip(group, results):
                    co[rows, pair_cols(pair)] = result

            loop(PAIRS // CROSS_PAIRS, attend_some)
            x2[rows, :] = x1[rows, :] + dot_nn(co[rows, :], wa[:, 5 * D : 6 * D])

            def top_norm(i):
                part = rows_at(base + i * ROW, ROW)
                b[part, :] = norm_low(x2[part, :], third_gain)

            loop(ROWS_MB, top_norm)

            def expand(j):
                cols = cols_at(j * 512, 512)
                active, bend = gelu_parts(dot_nn(b[rows, :], wi[:, cols]))
                u[rows, cols] = active.astype(LOW)
                slope[rows, cols] = (bend * slope[rows, cols].astype(WIDE)).astype(LOW)

            loop(FF // 512, expand, EXPAND_UNROLL)
            tmp[0:DEC_MB, :] = dot_nt(slope[rows, :], wi[...])

            def top_back(i):
                part = rows_at(base + i * ROW, ROW)
                grad, gain_row = norm_back(tmp[rows_at(i * ROW, ROW), :], x2[part, :], third_gain)
                grad = grad + ct[part, :].astype(WIDE)
                g2w[part, :] = grad
                g2[part, :] = grad.astype(LOW)
                add_gain(2, gain_row)

            loop(ROWS_MB, top_back)
            dmix[0:DEC_MB, :] = dot_nt(g2[rows, :], wa[:, 5 * D : 6 * D]).astype(LOW)

            def attend_back_some(i):
                parts = [bias_t[j] for j in range(ROWS_MB)]
                group = [i * CROSS_BACK_PAIRS + k for k in range(CROSS_BACK_PAIRS)]
                pairs = [
                    (
                        cq[rows, pair_cols(pair)], ctx[keys, pair_cols(pair)],
                        ctx[keys, pair_cols(pair, 1)], dmix[0:DEC_MB, pair_cols(pair)],
                    )
                    for pair in group
                ]
                results = attend_back(pairs, jnp.concatenate(parts + parts, 1))
                for pair, grads in zip(group, results):
                    cq[rows, pair_cols(pair)] = grads[0]
                    ctx[keys, pair_cols(pair)] = grads[1]
                    ctx[keys, pair_cols(pair, 1)] = grads[2]

            loop(PAIRS // CROSS_BACK_PAIRS, attend_back_some)
            sent[micro] = dot_nt(ctx[keys, :], wctx[...]).astype(LOW)
            across(sent.at[micro], micro).start()

        loop(MICRO, cross)
        stores = [
            store(a.at[full], a_out.at[full], 0), store(o.at[full], o_out.at[full], 1),
            store(b.at[full], b_out.at[full], 2), store(u.at[full], u_out.at[full], 3),
            store(slope.at[full], dh_out.at[full], 7), store(g2.at[full], g2_out.at[full], 6),
            store(co, co_out, 10), store(cq, dq_out, 11), store(landed, up_out, 12),
            store(ctx, dctx_out, 13), store(c.at[full], c_out.at[full], 14),
        ]
        for copy in stores:
            copy.start()

        def finish(micro):
            base = micro * DEC_MB
            rows = rows_at(base, DEC_MB)
            tmp[0:DEC_MB, :] = dot_nt(cq[rows, :], wa[:, 4 * D : 5 * D])

            def mid_back(i):
                part = rows_at(base + i * ROW, ROW)
                grad, gain_row = norm_back(tmp[rows_at(i * ROW, ROW), :], x1[part, :], second_gain)
                grad = grad + g2w[part, :]
                x1[part, :] = grad
                g1[part, :] = grad.astype(LOW)
                add_gain(1, gain_row)

            loop(ROWS_MB, mid_back)
            dmix[0:DEC_MB, :] = dot_nt(g1[rows, :], wa[:, 3 * D : 4 * D]).astype(LOW)

            def self_back(i):
                attend_rows_back(
                    qkv, rows_at(base + i * ROW, ROW), dmix, rows_at(i * ROW, ROW),
                    self_bias(micro * ROWS_MB + i, True), list(range(PAIRS)),
                )

            loop(ROWS_MB, self_back)
            tmp[0:DEC_MB, :] = dot_nt(qkv[rows, :], wa[:, 0 : 3 * D])

            def low_back(i):
                part = rows_at(base + i * ROW, ROW)
                grad, gain_row = norm_back(
                    tmp[rows_at(i * ROW, ROW), :], x[part, :].astype(WIDE), first_gain
                )
                x1[part, :] = x1[part, :] + grad
                exch[rows_at(DEC_ROWS + base + i * ROW, ROW), :] = x1[part, 0:HALF].astype(LOW)
                add_gain(0, gain_row)

            loop(ROWS_MB, low_back)
            decoded = (x2[rows, :] + dot_nn(u[rows, :], wo[...])).astype(LOW)
            exch[rows, :] = decoded[:, 0:HALF]
            decoded_half[rows, :] = decoded[:, HALF:]

        loop(MICRO, finish)
        late = [
            store(qkv.at[full], dqkv_out.at[full], 4), store(g1.at[full], g1_out.at[full], 5),
            store(x1.at[full, HALF:], caption_own, 8), store(exch, exch_out, 9),
            store(decoded_half, decoded_own, 15),
        ]
        for copy in late:
            copy.start()
        for copy in stores + late:
            copy.wait()
        for micro in range(MICRO):
            across(sent.at[micro], micro).wait_send()
        ctx_copy(ctx_part(quarter), quarter, {"dp": side}, 1).wait_send()
        ctx_copy(ctx_part(quarter), quarter, {"dp": twin}, 2).wait_send()
        ctx_copy(ctx_part(quarter), quarter, {"dp": twin}, 3).wait_send()

    gain_in.wait()
    first_gain, second_gain, third_gain = gain_rows[0:1, :], gain_rows[1:2, :], gain_rows[2:3, :]

    @pl.when(section == 0)
    def _():
        encoder()

    @pl.when(section == 1)
    def _():
        decoder()


def main_call(patches, captions, segments, seg_images, attn_w, w_in, w_out, gains, cot):
    def low(*shape):
        return jax.ShapeDtypeStruct(shape, LOW)

    def wide(*shape):
        return jax.ShapeDtypeStruct(shape, WIDE)

    outs = [
        low(ENC_ROWS, D), low(ENC_ROWS, D), low(DEC_ROWS, D), low(ENC_ROWS, D), low(ENC_ROWS, FF),
        low(ENC_ROWS, 3 * D), low(ENC_ROWS, D), low(ENC_ROWS, D), low(ENC_ROWS, FF),
        low(DEC_ROWS, D), low(DEC_ROWS, D), low(MICRO, ENC_MB, D), low(ENC_ROWS, 2 * D),
        wide(8, D), wide(ENC_ROWS, HALF), low(DEC_ROWS, HALF), wide(DEC_ROWS, HALF),
        low(2 * DEC_ROWS, HALF),
    ]
    any_spec = pl.BlockSpec(memory_space=pl.ANY)
    vmem_spec = pl.BlockSpec(memory_space=pltpu.VMEM)
    out_specs = [any_spec] * len(outs)
    out_specs[13] = vmem_spec
    vmem = pltpu.VMEM
    scratch = [
        vmem((D, 6 * D), LOW), vmem((D, FF), LOW), vmem((FF, D), LOW), vmem((D, 2 * D), LOW),
        vmem((ENC_ROWS, D), LOW), vmem((DEC_ROWS, D), LOW),
        vmem((ENC_ROWS, D), LOW), vmem((ENC_ROWS, D), LOW), vmem((ENC_ROWS, D), LOW),
        vmem((ENC_ROWS, D), LOW),
        vmem((ENC_ROWS, 3 * D), LOW), vmem((max(ENC_MB, DEC_ROWS), FF), LOW), vmem((ENC_ROWS, FF), LOW),
        vmem((ENC_ROWS, D), WIDE), vmem((ENC_ROWS, D), WIDE),
        vmem((ENC_ROWS, D), LOW), vmem((ENC_ROWS, D), LOW),
        vmem((MICRO, ENC_MB, D), LOW), vmem((max(ENC_MB, DEC_ROWS), D), LOW),
        vmem((ENC_ROWS, 2 * D), LOW),
        vmem((DEC_ROWS, D), LOW), vmem((DEC_ROWS, D), LOW), vmem((DEC_ROWS, D), WIDE),
        vmem((ENC_MB, D), WIDE), vmem((MICRO, ENC_MB, D), LOW),
        vmem((DEC_MB, ENC_MB), WIDE), vmem((ROWS_MB, ENC_MB, ROW), WIDE),
        vmem((2 * DEC_ROWS, HALF), LOW), vmem((DEC_ROWS, HALF), LOW),
        vmem((3, D), WIDE), pltpu.SemaphoreType.DMA((7,)), pltpu.SemaphoreType.DMA((16,)),
        pltpu.SemaphoreType.DMA((MICRO,)), pltpu.SemaphoreType.DMA((MICRO,)),
        pltpu.SemaphoreType.DMA((4,)), pltpu.SemaphoreType.DMA((4,)),
    ]
    return pl.pallas_call(
        main_kernel,
        name="layers",
        out_shape=outs,
        in_specs=[any_spec, any_spec, vmem_spec, pl.BlockSpec(memory_space=pltpu.SMEM)]
        + [any_spec] * 5,
        out_specs=out_specs,
        scratch_shapes=scratch,
        compiler_params=pltpu.CompilerParams(
            collective_id=1, has_side_effects=True, vmem_limit_bytes=63 * MIB
        ),
    )(patches, captions, segments, seg_images, attn_w, w_in, w_out, gains, cot)


CHUNK = 256
SLOTS = 8
FIRST_LAG = 2
FAR_EVERY = 6
LAG = 4
GAIN_STEPS = 5
OUT_IDS = 12
ONLY_DEC = 12
CTX_IDS = 6


def grads_kernel(n_bits, *refs):
    (
        a_in, o_in, c_in, b_in, u_in, dqkv_in, g1_in, g2_in, dh_in, co_in, dq_in, up_in, dctx_in,
        gains_in, patch_own, decoded_own, caption_own, exch_in, cot_in,
        shares, gain_share, patch_out, decoded_out, caption_out,
        a, o, c, b, u, dqkv, g1, g2, dh, co, dq, up, dctx, cot,
        part, ctx_sum, exch, patch_rows, gain_sum, gain_in,
    ) = refs[:44]
    recv = refs[44 : 44 + n_bits]
    load_sem, own_sem, send_sem, recv_sem, gain_send, gain_recv, far_send, far_recv = refs[44 + n_bits :]
    section = lax.axis_index("section")
    dp = lax.axis_index("dp")
    bits = [(dp // (1 << k)) % 2 for k in range(n_bits)]
    partners = [{"dp": dp + (1 << k) * (1 - 2 * bits[k])} for k in range(n_bits)]
    across = {"section": 1 - section}
    barrier = pltpu.get_barrier_semaphore()

    def greet(target):
        pl.semaphore_signal(barrier, inc=1, device_id=target, device_id_type=MESH)

    for target in partners:
        greet(target)

    @pl.when(section == 1)
    def _():
        pl.semaphore_wait(barrier, n_bits)
        greet(across)

    @pl.when(section == 0)
    def _():
        pl.semaphore_wait(barrier, n_bits + 1)
        greet(across)

    rows = part.shape[-2]
    owners = 1 << n_bits
    total = recv[0].shape[0]
    begin = ONLY_DEC * (1 - section)

    def remote(src, dst, send, receive, target):
        return pltpu.make_async_remote_copy(
            src_ref=src, dst_ref=dst, send_sem=send, recv_sem=receive, device_id=target,
            device_id_type=MESH)

    def gain_copy(k):
        return remote(gain_sum.at[k], gain_in.at[k], gain_send.at[k], gain_recv.at[k], partners[k])

    def exch_copy():
        return remote(exch_in, exch, far_send.at[0], far_recv.at[0], across)

    def ctx_copy():
        return remote(ctx_sum, shares.at[0:CTX_IDS], far_send.at[1], far_recv.at[1], across)

    gain_sum[0] = gains_in[...]
    gain_copy(0).start()

    def load_plan(is_dec):
        count = DEC_ROWS if is_dec else ENC_ROWS

        def short(src, dst):
            return src.at[0:count], dst.at[0:count]

        plan = {
            0: short(u_in, u), 1: short(g2_in, g2), 2: short(b_in, b), 3: short(dh_in, dh),
            4: short(a_in, a), 5: short(dqkv_in, dqkv), 6: short(o_in, o), 7: short(g1_in, g1),
        }
        if is_dec:
            only = {
                8: (up_in, up), 9: (dctx_in, dctx), 10: (c_in, c), 11: (dq_in, dq),
                12: (co_in, co), 13: (cot_in, cot),
            }
            plan = {**only, **plan}
        return plan

    def need(is_dec, *slots):
        plan = load_plan(is_dec)
        for slot in slots:
            pltpu.make_async_copy(*plan[slot], load_sem.at[slot]).wait()

    for is_dec in (False, True):
        @pl.when(section == int(is_dec))
        def _(is_dec=is_dec):
            for slot, (src, dst) in load_plan(is_dec).items():
                pltpu.make_async_copy(src, dst, load_sem.at[slot]).start()
            if is_dec:
                pltpu.make_async_copy(decoded_own, decoded_out, load_sem.at[14]).start()
                pltpu.make_async_copy(caption_own, caption_out, load_sem.at[15]).start()
            else:
                pltpu.make_async_copy(patch_own, patch_rows, load_sem.at[14]).start()

    def core_copy(index):
        slot = index % SLOTS
        return remote(part.at[slot, 1 - bits[0]], recv[0].at[index], send_sem.at[0, index],
                      recv_sem.at[0, index], partners[0])

    near_first = list(range(1, n_bits))
    far_first = list(range(2, n_bits)) + [1]

    def stage_cut(order, stage, index, flip):
        bit = order[stage - 1]
        left = sorted(order[stage - 1 :], reverse=True)
        value = bits[bit] + flip * (1 - 2 * bits[bit])
        return (index,) + (slice(None),) * left.index(bit) + (value,)

    def stage_copy(order, stage, index):
        return remote(
            recv[stage - 1].at[stage_cut(order, stage, index, 1)], recv[stage].at[index],
            send_sem.at[stage, index], recv_sem.at[stage, index], partners[order[stage - 1]])

    def in_order(index, action):
        is_far = index % FAR_EVERY == FAR_EVERY // 2

        @pl.when(is_far)
        def _():
            action(far_first)

        @pl.when(jnp.logical_not(is_far))
        def _():
            action(near_first)

    def advance(i):
        for stage in range(n_bits):
            j = i - FIRST_LAG - stage * LAG

            @pl.when((j >= begin) & (j < total))
            def _(stage=stage, j=j):
                if stage == 0:
                    core_copy(j).wait()
                    summed = part[j % SLOTS, bits[0]].astype(WIDE) + recv[0][j].astype(WIDE)
                    recv[0][j] = summed.astype(LOW)
                    in_order(j, lambda order: stage_copy(order, 1, j).start())
                elif stage < n_bits - 1:
                    def step(order):
                        stage_copy(order, stage, j).wait()
                        mine = recv[stage - 1][stage_cut(order, stage, j, 0)]
                        summed = mine.astype(WIDE) + recv[stage][j].astype(WIDE)
                        recv[stage][j] = summed.astype(LOW)
                        stage_copy(order, stage + 1, j).start()

                    in_order(j, step)
                else:
                    def step(order):
                        stage_copy(order, stage, j).wait()

                    in_order(j, step)
                    last = jnp.where(j % FAR_EVERY == FAR_EVERY // 2, bits[far_first[-1]], bits[near_first[-1]])
                    mine = recv[stage - 1][j, last]
                    summed = mine.astype(WIDE) + recv[stage][j].astype(WIDE)

                    @pl.when(j < CTX_IDS)
                    def _():
                        ctx_sum[j] = summed

                    @pl.when(j >= CTX_IDS)
                    def _():
                        shares[j - CTX_IDS] = summed

        for k in range(n_bits):
            @pl.when(i == ONLY_DEC + GAIN_STEPS * (k + 1))
            def _(k=k):
                gain_copy(k).wait()
                summed = gain_sum[k] + gain_in[k]
                if k == n_bits - 1:
                    own = jnp.zeros((8, rows), WIDE)
                    for owner in range(owners):
                        own = jnp.where(dp == owner, summed[:, owner * rows : (owner + 1) * rows], own)
                    gain_share[...] = own
                else:
                    gain_sum[k + 1] = summed
                    gain_copy(k + 1).start()

    def place(index, first_owner, block):
        for k in range(block.shape[0] // rows):
            owner = first_owner + k
            path = tuple((owner >> bit) & 1 for bit in reversed(range(1, n_bits)))
            part[(index % SLOTS, owner & 1) + path] = block[k * rows : (k + 1) * rows].astype(LOW)

    def simple_phase(first, count, left, right, col, row_count):
        def step(i):
            index = first + i
            cols = cols_at(col + i * CHUNK, CHUNK)
            if row_count is None:
                value = dot_tn(left[...].reshape(-1, D), right[:, cols])
            else:
                value = dot_tn(left[0:row_count, :], right[0:row_count, cols])
            place(index, 0, value)
            core_copy(index).start()
            advance(index)
        loop(count, step)

    def out_phase(first, right, row_count):
        share = FF // owners
        blocks = share // rows
        step_owners = D // share

        def step(i):
            cols = cols_at(i * CHUNK, CHUNK)
            base = first + i * blocks
            for piece in range(FF // D):
                value = dot_tn(u[0:row_count, piece * D : (piece + 1) * D], right[0:row_count, cols])
                for k in range(step_owners):
                    for q in range(blocks):
                        low = k * share + q * rows
                        place(base + q, piece * step_owners + k, value[low : low + rows])
            loop(blocks, lambda q: core_copy(base + q).start())
            loop(blocks, lambda q: advance(base + q))
        loop(D // CHUNK, step)

    @pl.when(section == 1)
    def _():
        need(True, 8, 9)
        simple_phase(0, CTX_IDS, up, dctx, 0, None)
        need(True, 10, 11)
        simple_phase(CTX_IDS, 3, c, dq, 0, DEC_ROWS)
        need(True, 12, 1)
        simple_phase(CTX_IDS + 3, 3, co, g2, 0, DEC_ROWS)

    for is_dec in (False, True):
        @pl.when(section == int(is_dec))
        def _(is_dec=is_dec):
            count = DEC_ROWS if is_dec else ENC_ROWS
            need(is_dec, 0, 13 if is_dec else 1)
            out_phase(ONLY_DEC, cot if is_dec else g2, count)
            need(is_dec, 2, 3)
            simple_phase(ONLY_DEC + OUT_IDS, FF // CHUNK, b, dh, 0, count)

    @pl.when(section == 1)
    def _():
        pl.semaphore_wait(barrier, 1)
        ctx_copy().start()

    exch_copy().start()

    for is_dec in (False, True):
        @pl.when(section == int(is_dec))
        def _(is_dec=is_dec):
            count = DEC_ROWS if is_dec else ENC_ROWS
            need(is_dec, 4, 5)
            first = ONLY_DEC + OUT_IDS + FF // CHUNK
            simple_phase(first, 3 * D // CHUNK, a, dqkv, 0, count)
            need(is_dec, 6, 7)
            simple_phase(first + 3 * D // CHUNK, D // CHUNK, o, g1, 0, count)

    exch_copy().wait()

    @pl.when(section == 0)
    def _():
        pltpu.make_async_copy(patch_own, patch_rows, load_sem.at[14]).wait()
        for image in range(MICRO * IMG_MB):
            patch_out[image * PATCHES : (image + 1) * PATCHES, :] = patch_rows[
                image * IMG_ROWS : image * IMG_ROWS + PATCHES, :
            ]
        decoded_out[...] = exch[0:DEC_ROWS, :]
        caption_out[...] = exch[DEC_ROWS : 2 * DEC_ROWS, :].astype(WIDE)

    @pl.when(section == 1)
    def _():
        pltpu.make_async_copy(decoded_own, decoded_out, load_sem.at[14]).wait()
        pltpu.make_async_copy(caption_own, caption_out, load_sem.at[15]).wait()
        for image in range(MICRO * IMG_MB):
            patch_out[image * PATCHES : (image + 1) * PATCHES, :] = exch[
                image * IMG_ROWS : image * IMG_ROWS + PATCHES, :
            ].astype(WIDE)

    loop(FIRST_LAG + (n_bits - 1) * LAG, lambda i: advance(total + i))

    @pl.when(section == 0)
    def _():
        ctx_copy().wait_recv()

    @pl.when(section == 1)
    def _():
        ctx_copy().wait_send()


def grads_call(n_dp, *operands):
    n_bits = n_dp.bit_length() - 1
    rows = D // n_dp
    share = FF // n_dp
    total = ONLY_DEC + 2 * OUT_IDS + 4 * D // CHUNK
    vmem = pltpu.VMEM
    pair = (2,) * (n_bits - 1)
    any_spec = pl.BlockSpec(memory_space=pl.ANY)
    vmem_spec = pl.BlockSpec(memory_space=pltpu.VMEM)
    sem = pltpu.SemaphoreType.DMA
    scratch = [
        vmem((ENC_ROWS, D), LOW), vmem((ENC_ROWS, D), LOW), vmem((DEC_ROWS, D), LOW),
        vmem((ENC_ROWS, D), LOW), vmem((ENC_ROWS, FF), LOW), vmem((ENC_ROWS, 3 * D), LOW),
        vmem((ENC_ROWS, D), LOW), vmem((ENC_ROWS, D), LOW), vmem((ENC_ROWS, FF), LOW),
        vmem((DEC_ROWS, D), LOW), vmem((DEC_ROWS, D), LOW), vmem((MICRO, ENC_MB, D), LOW),
        vmem((ENC_ROWS, 2 * D), LOW), vmem((DEC_ROWS, D), LOW),
        vmem((SLOTS, 2) + pair + (rows, CHUNK), LOW), vmem((CTX_IDS, rows, CHUNK), WIDE),
        vmem((2 * DEC_ROWS, HALF), LOW), vmem((ENC_ROWS, HALF), WIDE),
        vmem((n_bits, 8, D), WIDE), vmem((n_bits, 8, D), WIDE),
    ]
    scratch += [vmem((total,) + pair[k:] + (rows, CHUNK), LOW) for k in range(n_bits)]
    scratch += [
        sem((16,)), sem((1,)), sem((n_bits, total)), sem((n_bits, total)), sem((n_bits,)),
        sem((n_bits,)), sem((2,)), sem((2,)),
    ]
    in_specs = [any_spec] * len(operands)
    in_specs[13] = vmem_spec
    return pl.pallas_call(
        functools.partial(grads_kernel, n_bits),
        name="weight_sums",
        out_shape=(
            jax.ShapeDtypeStruct((total - CTX_IDS, rows, CHUNK), WIDE),
            jax.ShapeDtypeStruct((8, rows), WIDE),
            jax.ShapeDtypeStruct((MICRO * IMG_MB * PATCHES, HALF), WIDE),
            jax.ShapeDtypeStruct((DEC_ROWS, HALF), LOW),
            jax.ShapeDtypeStruct((DEC_ROWS, HALF), WIDE),
        ),
        in_specs=in_specs,
        out_specs=(vmem_spec,) * 5,
        scratch_shapes=scratch,
        compiler_params=pltpu.CompilerParams(
            collective_id=2, has_side_effects=True, vmem_limit_bytes=63 * MIB
        ),
    )(*operands)


def place_kernel(
    shares, gain_share, patch_in, decoded_in, caption_in,
    decoded_out, caption_out, patch_out, attn_out, in_out, out_out, gain_out, sem,
):
    rows = shares.shape[1]
    moves = [
        (patch_in, patch_out), (caption_in, caption_out), (decoded_in, decoded_out),
        (gain_share.at[0:3], gain_out.at[0]),
    ]
    first_w_in = CTX_IDS + OUT_IDS
    first_attn = first_w_in + FF // CHUNK
    blocks = OUT_IDS * CHUNK // D

    def cols(index):
        return slice(index * CHUNK, (index + 1) * CHUNK)

    for k in range(4 * D // CHUNK):
        moves.append((shares.at[first_attn + k], attn_out.at[0, :, cols(k)]))
    for k in range(CTX_IDS):
        moves.append((shares.at[k], attn_out.at[0, :, cols(4 * D // CHUNK + k)]))
    for k in range(FF // CHUNK):
        moves.append((shares.at[first_w_in + k], in_out.at[0, :, cols(k)]))
    for k in range(OUT_IDS):
        part = slice((k % blocks) * rows, (k % blocks + 1) * rows)
        moves.append((shares.at[CTX_IDS + k], out_out.at[0, part, cols(k // blocks)]))
    copies = [
        pltpu.make_async_copy(src, dst, sem.at[index]) for index, (src, dst) in enumerate(moves)
    ]
    for copy in copies:
        copy.start()
    for copy in copies:
        copy.wait()


def kernel_sums(n_dp, operands):
    results = grads_call(n_dp, *operands)
    rows = D // n_dp
    any_spec = pl.BlockSpec(memory_space=pl.ANY)
    patch_out, decoded_out, caption_out = results[2:]
    shapes = [decoded_out, caption_out, patch_out] + [
        jax.ShapeDtypeStruct(shape, WIDE)
        for shape in ((1, rows, 6 * D), (1, rows, FF), (1, FF // n_dp, D), (1, 3, rows))
    ]
    return pl.pallas_call(
        place_kernel,
        name="place_sums",
        out_shape=[jax.ShapeDtypeStruct(item.shape, item.dtype) for item in shapes],
        in_specs=[any_spec] * 5,
        out_specs=[pl.BlockSpec(memory_space=pltpu.VMEM)] * 7,
        scratch_shapes=[pltpu.SemaphoreType.DMA((64,))],
    )(*results)


def shifted(block, distance):
    devices = range(lax.axis_size("section"))
    route = [(i - distance, i) for i in devices if i - distance in devices]
    return lax.ppermute(block, "section", route)


def plain_sums(operands):
    (
        a, o, c, b, u, dqkv, g1, g2, dh, co, dq, up, dctx,
        gains, patch_own, decoded_own, caption_own, exch, cot,
    ) = operands
    is_first = lax.axis_index("section") == 0
    up = up.reshape(ENC_ROWS, D)

    def encoder_parts():
        return (
            jnp.concatenate([dot_tn(a, dqkv), dot_tn(o, g1)], 1), jnp.zeros((D, 2 * D), WIDE),
            jnp.zeros((D, 2 * D), WIDE), dot_tn(b, dh), dot_tn(u, g2),
        )

    def decoder_parts():
        rows = slice(0, DEC_ROWS)
        return (
            jnp.concatenate([dot_tn(a[rows], dqkv[rows]), dot_tn(o[rows], g1[rows])], 1),
            jnp.concatenate([dot_tn(c, dq), dot_tn(co, g2[rows])], 1),
            dot_tn(up, dctx), dot_tn(b[rows], dh[rows]), dot_tn(u[rows], cot),
        )

    parts = lax.cond(is_first, encoder_parts, decoder_parts)
    sums = [lax.psum_scatter(part, "dp", scatter_dimension=0, tiled=True) for part in parts]
    last = jnp.where(is_first, shifted(sums[2], -1), sums[1])
    moved = lax.ppermute(exch, "section", [(0, 1), (1, 0)])

    def unpad(block):
        shaped = block[:ENC_ROWS].reshape(MICRO * IMG_MB, IMG_ROWS, HALF)
        return shaped[:, :PATCHES].reshape(-1, HALF).astype(WIDE)

    return (
        jnp.where(is_first, moved[:DEC_ROWS], decoded_own),
        jnp.where(is_first, moved[DEC_ROWS:].astype(WIDE), caption_own),
        jnp.where(is_first, unpad(patch_own), unpad(moved)),
        jnp.concatenate([sums[0], last], 1),
        sums[3],
        sums[4],
        lax.psum_scatter(gains[:3], "dp", scatter_dimension=1, tiled=True),
    )


def with_section(results):
    return tuple(results[:3]) + tuple(share[None] for share in results[3:])


def local(patches, captions, segments, seg_images, attn_w, w_in, w_out, norm_gains, cotangent):
    n_dp = lax.axis_size("dp")
    kept = main_call(
        patches, captions, segments, seg_images, attn_w, w_in, w_out, norm_gains, cotangent
    )
    operands = list(kept) + [cotangent]
    if n_dp & (n_dp - 1) == 0 and (D // n_dp) % 16 == 0:
        results = kernel_sums(n_dp, operands)
    else:
        results = with_section(plain_sums(operands))
    return tuple(results)


def solution(mesh):
    placed = (
        P("dp", None),
        P("dp", None),
        P("dp", None),
        P("dp", None),
        P("section", None, None),
        P("section", None, None),
        P("section", None, None),
        P("section", None, None),
        P("dp", None),
    )
    return jax.shard_map(
        local,
        mesh=mesh,
        in_specs=placed,
        out_specs=(
            P("dp", "section"),
            P("dp", "section"),
            P("dp", "section"),
            P("section", "dp", None),
            P("section", "dp", None),
            P("section", "dp", None),
            P("section", None, "dp"),
        ),
        check_vma=False,
    )
```

```python
import functools
import jax
import jax.numpy as jnp
from jax import lax
from jax.experimental import pallas as pl
from jax.experimental.pallas import tpu as pltpu
from jax.sharding import PartitionSpec as P

D = 768
FF = 3072
HEADS = 12
HEAD = 64
PATCHES = 196
ROW = 128
SEGS = 4
MICRO = 2
IMG_MB = 2
ROWS_MB = 2
NORM_EPS = 1e-06
SCORE_SCALE = 0.125
MASKED = -1e30
ROOT_HALF = 0.7071067811865476
INV_ROOT_TWO_PI = 0.3989422804014327
MESH = pl.DeviceIdType.MESH
MIB = 1 << 20

LOW = jnp.bfloat16
WIDE = jnp.float32
IMG_ROWS = -(-PATCHES // 16) * 16
ENC_MB = IMG_MB * IMG_ROWS
ENC_ROWS = MICRO * ENC_MB
DEC_MB = ROWS_MB * ROW
DEC_ROWS = MICRO * DEC_MB
PAIR = 2 * HEAD
PAIRS = HEADS // 2
HALF = D // 2
QUARTER = D // 4
CROSS_PAIRS = 2
EXPAND_UNROLL = 1
BACK_UNROLL = 1
CONTEXT_UNROLL = 1
PROJECT_UNROLL = 1
BACK_PAIRS = 2
ROW_PAIRS = 3
SELF_PAIRS = 3
SELF_BACK_PAIRS = 3
DEEP = 256
SHALLOW = 384
CROSS_BACK_PAIRS = 2


def dot_nn(left, right):
    return lax.dot_general(left, right, (((1,), (0,)), ((), ())), preferred_element_type=WIDE)


def dot_nt(left, right):
    return lax.dot_general(left, right, (((1,), (1,)), ((), ())), preferred_element_type=WIDE)


def dot_tn(left, right):
    return lax.dot_general(left, right, (((0,), (0,)), ((), ())), preferred_element_type=WIDE)


def rows_at(start, size):
    return pl.ds(pl.multiple_of(start, 16), size)


def cols_at(start, size):
    if isinstance(start, int):
        return slice(start, start + size)
    return pl.ds(pl.multiple_of(start, 128), size)


def norm_hat(values):
    centred = values - jnp.mean(values, -1, keepdims=True)
    inverse = lax.rsqrt(jnp.mean(centred * centred, -1, keepdims=True) + NORM_EPS)
    return centred * inverse, inverse


def norm_low(values, gain):
    return (norm_hat(values)[0] * gain).astype(LOW)


def norm_back(upstream, values, gain):
    normed, inverse = norm_hat(values)
    scaled = upstream * gain
    inner = (
        scaled
        - jnp.mean(scaled, -1, keepdims=True)
        - normed * jnp.mean(scaled * normed, -1, keepdims=True)
    )
    return inner * inverse, jnp.sum(upstream * normed, 0, keepdims=True)


def gelu_parts(hidden):
    normal_cdf = 0.5 * (1.0 + lax.erf(hidden * ROOT_HALF))
    slope = normal_cdf + hidden * INV_ROOT_TWO_PI * jnp.exp(-0.5 * hidden * hidden)
    return hidden * normal_cdf, slope


def first_lanes(rows):
    return lax.broadcasted_iota(jnp.int32, (rows, PAIR), 1) < HEAD


def split_pair(block):
    first = (lax.broadcasted_iota(jnp.int32, (1, PAIR), 1) < HEAD).astype(WIDE)
    return jnp.concatenate([block * first.astype(LOW), block * (1.0 - first).astype(LOW)], 0)


def join_pair(stacked):
    rows = stacked.shape[0] // 2
    return jnp.where(first_lanes(rows), stacked[:rows], stacked[rows:])


def attend(pairs, bias):
    stacked = [split_pair(queries) * SCORE_SCALE for queries, _, _ in pairs]
    scores = [dot_nt(stack, pair[1]) + bias for stack, pair in zip(stacked, pairs)]
    powers = [jnp.exp(block - jnp.max(block, -1, keepdims=True)) for block in scores]
    scales = [1.0 / jnp.sum(block, -1, keepdims=True) for block in powers]
    return [
        join_pair(dot_nn(block.astype(LOW), pair[2]) * scale).astype(LOW)
        for block, pair, scale in zip(powers, pairs, scales)
    ]


def attend_back(pairs, bias):
    stacked = [split_pair(pair[0]) * SCORE_SCALE for pair in pairs]
    grads = [split_pair(pair[3]) for pair in pairs]
    scores = [dot_nt(pair[1], stack) + bias for pair, stack in zip(pairs, stacked)]
    grad_chances = [dot_nt(pair[2], grad) for pair, grad in zip(pairs, grads)]
    powers = [jnp.exp(block - jnp.max(block, 0, keepdims=True)) for block in scores]
    chances = [block * (1.0 / jnp.sum(block, 0, keepdims=True)) for block in powers]
    inner = [jnp.sum(left * right, 0, keepdims=True) for left, right in zip(grad_chances, chances)]
    grad_scores = [
        (chance * (grad - mean)).astype(LOW)
        for chance, grad, mean in zip(chances, grad_chances, inner)
    ]
    grad_keys = [dot_nn(grad, stack) for grad, stack in zip(grad_scores, stacked)]
    grad_values = [dot_nn(chance.astype(LOW), grad) for chance, grad in zip(chances, grads)]
    grad_queries = [
        join_pair(dot_tn(grad, pair[1])) * SCORE_SCALE for grad, pair in zip(grad_scores, pairs)
    ]
    return [
        tuple(part.astype(LOW) for part in parts)
        for parts in zip(grad_queries, grad_keys, grad_values)
    ]


def pair_cols(pair, column=0):
    start = column * D + pair * PAIR
    return cols_at(start, PAIR) if not isinstance(start, int) else slice(start, start + PAIR)


def tiles(width, body):
    loop(D // width, lambda j: body(cols_at(j * width, width), j * width))


def pair_group(step, size):
    first = (step % (PAIRS // size)) * size
    return [first + pair for pair in range(size)]


def attend_rows(qkv, rows, mixed, bias, group):
    pairs = [[qkv[rows, pair_cols(pair, part)] for part in range(3)] for pair in group]
    for pair, result in zip(group, attend(pairs, bias)):
        mixed[rows, pair_cols(pair)] = result


def attend_rows_back(qkv, rows, grad_mixed, grad_rows, bias, group):
    pairs = [
        [qkv[rows, pair_cols(pair, part)] for part in range(3)]
        + [grad_mixed[grad_rows, pair_cols(pair)]]
        for pair in group
    ]
    for pair, results in zip(group, attend_back(pairs, bias)):
        for part in range(3):
            qkv[rows, pair_cols(pair, part)] = results[part]


def loop(count, body, unroll=1):
    def several(i, carry):
        for k in range(unroll):
            body(i * unroll + k)
        return carry

    if count == unroll:
        several(0, 0)
    else:
        lax.fori_loop(0, count // unroll, several, 0)


def main_kernel(*refs):
    (
        patches, captions, segments, seg_images, attn_w, w_in, w_out, gains, cot,
        a_out, o_out, c_out, b_out, u_out, dqkv_out, g1_out, g2_out, dh_out,
        co_out, dq_out, up_out, dctx_out, gain_out, patch_own, decoded_own, caption_own, exch_out,
        wa, wi, wo, wctx, x, ct, a, o, b, c, qkv, u, slope, x1, x2, g1, g2, landed, dmix, ctx,
        co, cq, g2w, tmp, sent, bias, bias_t, exch, decoded_half,
        gain_rows, load_sem, out_sem, up_send, up_recv, ctx_send, ctx_recv,
    ) = refs
    section = lax.axis_index("section")
    dp = lax.axis_index("dp")
    quarter = dp % 4
    side = dp + 2 * (1 - 2 * ((dp // 2) % 2))
    twin = dp + 1 - 2 * (dp % 2)
    other_quarter = quarter + 2 * (1 - 2 * (quarter // 2))
    barrier = pltpu.get_barrier_semaphore()
    for target in ({"section": 1 - section}, {"dp": side}, {"dp": twin}):
        pl.semaphore_signal(barrier, inc=1, device_id=target, device_id_type=MESH)
    pl.semaphore_wait(barrier, 3)

    gain_out[...] = jnp.zeros_like(gain_out)

    def across(src, index):
        return pltpu.make_async_remote_copy(
            src_ref=src, dst_ref=landed.at[index], send_sem=up_send.at[index],
            recv_sem=up_recv.at[index], device_id={"section": 1 - section}, device_id_type=MESH)

    def ctx_part(index):
        return wctx.at[rows_at(index * QUARTER, QUARTER), :]

    def ctx_copy(src, part, target, slot):
        return pltpu.make_async_remote_copy(
            src_ref=src, dst_ref=ctx_part(part), send_sem=ctx_send.at[slot],
            recv_sem=ctx_recv.at[slot], device_id=target, device_id_type=MESH)

    def load(src, dst, slot):
        return pltpu.make_async_copy(src, dst, load_sem.at[slot])

    weight_loads = [
        load(attn_w.at[0, :, 0 : 3 * D], wa.at[:, 0 : 3 * D], 0),
        load(attn_w.at[0, :, 3 * D :], wa.at[:, 3 * D :], 1),
        load(w_in.at[0], wi, 2),
        load(w_out.at[0], wo, 3),
    ]

    gain_in = load(gains.at[0], gain_rows, 6)
    gain_in.start()

    def store(src, dst, slot):
        return pltpu.make_async_copy(src, dst, out_sem.at[slot])

    def add_gain(index, row):
        gain_out[index : index + 1, :] = gain_out[index : index + 1, :] + row

    def encoder():
        ctx_copy(
            attn_w.at[0, rows_at(quarter * QUARTER, QUARTER), 4 * D : 6 * D], quarter,
            {"section": 1 - section}, 0,
        ).start()
        rows_in = load(patches, g1.at[0 : patches.shape[0]], 4)
        rows_in.start()
        for copy in weight_loads:
            copy.start()
        rows_in.wait()
        for image in range(MICRO * IMG_MB):
            low_rows = g1[image * PATCHES : (image + 1) * PATCHES, :]
            x[image * IMG_ROWS : image * IMG_ROWS + PATCHES, :] = low_rows
            x[image * IMG_ROWS + PATCHES : (image + 1) * IMG_ROWS, :] = jnp.zeros(
                (IMG_ROWS - PATCHES, D), LOW
            )
        key_bias = jnp.where(
            lax.broadcasted_iota(jnp.int32, (1, IMG_ROWS), 1) < PATCHES, 0.0, MASKED
        )
        key_bias_t = jnp.where(
            lax.broadcasted_iota(jnp.int32, (IMG_ROWS, 1), 0) < PATCHES, 0.0, MASKED
        )

        def forward(micro):
            base = micro * ENC_MB
            rows = rows_at(base, ENC_MB)

            def low_norm(i):
                part = rows_at(base + i * IMG_ROWS, IMG_ROWS)
                a[part, :] = norm_low(x[part, :].astype(WIDE), first_gain)

            loop(IMG_MB, low_norm)

            @pl.when(micro == 0)
            def _():
                weight_loads[0].wait()

            def project(j):
                cols = cols_at(j * D, D)
                qkv[rows, cols] = dot_nn(a[rows, :], wa[:, cols]).astype(LOW)

            loop(3, project, PROJECT_UNROLL)

            def attend_image(i):
                image, group = i // (PAIRS // ROW_PAIRS), pair_group(i, ROW_PAIRS)
                attend_rows(qkv, rows_at(base + image * IMG_ROWS, IMG_ROWS), o, key_bias, group)

            loop(IMG_MB * PAIRS // ROW_PAIRS, attend_image)

            @pl.when(micro == 0)
            def _():
                weight_loads[1].wait()

            def tile(cols, start):
                mixed = dot_nn(o[rows, :], wa[:, cols_at(3 * D + start, SHALLOW)])
                x1[rows, cols] = x[rows, cols].astype(WIDE) + mixed

            tiles(SHALLOW, tile)

            def mid_norm(i):
                part = rows_at(base + i * IMG_ROWS, IMG_ROWS)
                b[part, :] = norm_low(x1[part, :], second_gain)

            loop(IMG_MB, mid_norm)

            @pl.when(micro == 0)
            def _():
                weight_loads[2].wait()

            @pl.when(micro > 0)
            def _():
                store(u.at[0:ENC_MB], u_out.at[rows], 3).wait()

            def expand(j):
                cols = cols_at(j * 512, 512)
                active, bend = gelu_parts(dot_nn(b[rows, :], wi[:, cols]))
                u[0:ENC_MB, cols] = active.astype(LOW)
                slope[rows, cols] = bend.astype(LOW)

            loop(FF // 512, expand, EXPAND_UNROLL)

            @pl.when(micro == 0)
            def _():
                weight_loads[3].wait()

            def tile(cols, start):
                x2[rows, cols] = x1[rows, cols] + dot_nn(u[0:ENC_MB, :], wo[:, cols])

            tiles(DEEP, tile)
            store(u.at[0:ENC_MB], u_out.at[rows], 3).start()

            def top_norm(i):
                part = rows_at(base + i * IMG_ROWS, IMG_ROWS)
                c[part, :] = norm_low(x2[part, :], third_gain)

            loop(IMG_MB, top_norm)
            across(c.at[rows, :], micro).start()

        loop(MICRO, forward)
        stores = [store(a, a_out, 0), store(o, o_out, 1), store(b, b_out, 2)]
        for copy in stores:
            copy.start()

        def backward(micro):
            base = micro * ENC_MB
            rows = rows_at(base, ENC_MB)
            across(c.at[rows, :], micro).wait()

            def top_norm(i):
                part = rows_at(base + i * IMG_ROWS, IMG_ROWS)
                upstream = landed[micro, rows_at(i * IMG_ROWS, IMG_ROWS), :].astype(WIDE)
                grad, gain_row = norm_back(upstream, x2[part, :], third_gain)
                x2[part, :] = grad
                g2[part, :] = grad.astype(LOW)
                add_gain(2, gain_row)

            loop(IMG_MB, top_norm)

            def expand(j):
                cols = cols_at(j * D, D)
                hidden = dot_nt(g2[rows, :], wo[cols, :])
                slope[rows, cols] = (hidden * slope[rows, cols].astype(WIDE)).astype(LOW)

            loop(FF // D, expand, BACK_UNROLL)
            store(slope.at[rows], dh_out.at[rows], 7).start()
            store(g2.at[rows], g2_out.at[rows], 6).start()
            def tile(cols, start):
                tmp[0:ENC_MB, cols] = dot_nt(slope[rows, :], wi[cols_at(start, DEEP), :])

            tiles(DEEP, tile)

            def mid_norm(i):
                part = rows_at(base + i * IMG_ROWS, IMG_ROWS)
                grad, gain_row = norm_back(
                    tmp[rows_at(i * IMG_ROWS, IMG_ROWS), :], x1[part, :], second_gain
                )
                grad = grad + x2[part, :]
                x1[part, :] = grad
                g1[part, :] = grad.astype(LOW)
                add_gain(1, gain_row)

            loop(IMG_MB, mid_norm)
            store(g1.at[rows], g1_out.at[rows], 5).start()
            def tile(cols, start):
                grads = dot_nt(g1[rows, :], wa[cols_at(start, SHALLOW), 3 * D : 4 * D])
                dmix[0:ENC_MB, cols] = grads.astype(LOW)

            tiles(SHALLOW, tile)

            def attend_image(i):
                image = i // (PAIRS // BACK_PAIRS)
                attend_rows_back(
                    qkv, rows_at(base + image * IMG_ROWS, IMG_ROWS), dmix,
                    rows_at(image * IMG_ROWS, IMG_ROWS), key_bias_t,
                    pair_group(i, BACK_PAIRS),
                )

            loop(IMG_MB * PAIRS // BACK_PAIRS, attend_image)
            def tile(cols, start):
                tmp[0:ENC_MB, cols] = dot_nt(qkv[rows, :], wa[cols_at(start, DEEP), 0 : 3 * D])

            tiles(DEEP, tile)

            def low_norm(i):
                part = rows_at(base + i * IMG_ROWS, IMG_ROWS)
                grad, gain_row = norm_back(
                    tmp[rows_at(i * IMG_ROWS, IMG_ROWS), :], x[part, :].astype(WIDE), first_gain
                )
                x1[part, :] = x1[part, :] + grad
                exch[part, :] = x1[part, HALF:].astype(LOW)
                add_gain(0, gain_row)

            loop(IMG_MB, low_norm)
            store(qkv.at[rows], dqkv_out.at[rows], 4).start()
            store(x1.at[rows, 0:HALF], patch_own.at[rows], 8).start()

        loop(MICRO, backward)
        store(exch, exch_out, 9).start()
        late = [
            store(qkv, dqkv_out, 4), store(g1, g1_out, 5), store(g2, g2_out, 6),
            store(slope, dh_out, 7), store(x1.at[:, 0:HALF], patch_own, 8), store(exch, exch_out, 9),
        ]
        for copy in stores + late + [store(u.at[0:ENC_MB], u_out.at[0:ENC_MB], 3)]:
            copy.wait()
        ctx_copy(
            attn_w.at[0, rows_at(quarter * QUARTER, QUARTER), 4 * D : 6 * D], quarter,
            {"section": 1 - section}, 0,
        ).wait_send()

    def decoder():
        rows_in = load(captions, x.at[0:DEC_ROWS], 4)
        cot_in = load(cot, ct, 5)
        rows_in.start()
        for copy in weight_loads:
            copy.start()
        cot_in.start()
        rows_in.wait()
        full = slice(0, DEC_ROWS)

        def low_norm(i):
            part = rows_at(i * ROW, ROW)
            a[part, :] = norm_low(x[part, :].astype(WIDE), first_gain)

        loop(DEC_ROWS // ROW, low_norm)
        weight_loads[0].wait()

        def project(j):
            cols = cols_at(j * D, D)
            qkv[full, cols] = dot_nn(a[full, :], wa[:, cols]).astype(LOW)

        loop(3, project)

        def segment_pair(row):
            across_rows = jnp.broadcast_to(
                segments[pl.ds(row, 1), :].astype(WIDE), (ROW, ROW)
            )
            return across_rows, across_rows.T

        def self_bias(row, transposed):
            along, down = segment_pair(row)
            sub = lax.broadcasted_iota(jnp.int32, (ROW, ROW), 0)
            lane = lax.broadcasted_iota(jnp.int32, (ROW, ROW), 1)
            order = (lane >= sub) if transposed else (sub >= lane)
            single = jnp.where((along == down) & order, 0.0, MASKED)
            return jnp.concatenate([single, single], 1 if transposed else 0)

        def self_attend(row):
            row_bias = self_bias(row, False)

            def some(i):
                attend_rows(qkv, rows_at(row * ROW, ROW), o, row_bias, pair_group(i, SELF_PAIRS))

            loop(PAIRS // SELF_PAIRS, some)

        loop(DEC_ROWS // ROW, self_attend)
        weight_loads[1].wait()
        def tile(cols, start):
            mixed = dot_nn(o[full, :], wa[:, cols_at(3 * D + start, SHALLOW)])
            x1[full, cols] = x[full, cols].astype(WIDE) + mixed

        tiles(SHALLOW, tile)

        def mid_norm(i):
            part = rows_at(i * ROW, ROW)
            c[part, :] = norm_low(x1[part, :], second_gain)

        loop(DEC_ROWS // ROW, mid_norm)
        def tile(cols, start):
            cq[:, cols] = dot_nn(c[full, :], wa[:, cols_at(4 * D + start, SHALLOW)]).astype(LOW)

        tiles(SHALLOW, tile)
        weight_loads[3].wait()
        cot_in.wait()

        def cot_project(j):
            cols = cols_at(j * D, D)
            slope[full, cols] = dot_nt(ct[...], wo[cols, :]).astype(LOW)

        loop(FF // D, cot_project)
        weight_loads[2].wait()

        ctx_copy(ctx_part(quarter), quarter, {"section": 1 - section}, 0).wait_recv()
        ctx_copy(ctx_part(quarter), quarter, {"dp": side}, 1).start()
        ctx_copy(ctx_part(quarter), quarter, {"dp": twin}, 2).start()
        ctx_copy(ctx_part(quarter), other_quarter, {"dp": side}, 1).wait_recv()
        ctx_copy(ctx_part(other_quarter), other_quarter, {"dp": twin}, 3).start()
        ctx_copy(ctx_part(quarter), quarter, {"dp": twin}, 2).wait_recv()
        ctx_copy(ctx_part(quarter), quarter, {"dp": twin}, 3).wait_recv()

        def cross_bias(micro):
            key = lax.broadcasted_iota(jnp.int32, (ROW, ENC_MB), 1)
            key_t = lax.broadcasted_iota(jnp.int32, (ENC_MB, ROW), 0)

            def one(i):
                row = micro * ROWS_MB + i
                along, down = segment_pair(row)
                image_along = jnp.zeros((ROW, ROW), WIDE)
                image_down = jnp.zeros((ROW, ROW), WIDE)
                for seg in range(SEGS):
                    image = seg_images[row, seg].astype(WIDE)
                    image_along = jnp.where(along == seg, image, image_along)
                    image_down = jnp.where(down == seg, image, image_down)
                allowed = jnp.zeros((ROW, ENC_MB), jnp.bool_)
                allowed_t = jnp.zeros((ENC_MB, ROW), jnp.bool_)
                for image in range(IMG_MB):
                    low, high = image * IMG_ROWS, image * IMG_ROWS + PATCHES
                    allowed = allowed | (
                        (key >= low) & (key < high) & (image_down[:, 0:1] == image)
                    )
                    allowed_t = allowed_t | (
                        (key_t >= low) & (key_t < high) & (image_along[0:1, :] == image)
                    )
                bias[rows_at(i * ROW, ROW), :] = jnp.where(allowed, 0.0, MASKED)
                bias_t[i] = jnp.where(allowed_t, 0.0, MASKED)

            loop(ROWS_MB, one)

        def cross(micro):
            cross_bias(micro)
            base = micro * DEC_MB
            rows = rows_at(base, DEC_MB)
            keys = rows_at(micro * ENC_MB, ENC_MB)
            across(sent.at[micro], micro).wait_recv()

            def context(j):
                cols = cols_at(j * D, D)
                ctx[keys, cols] = dot_nn(landed[micro], wctx[:, cols]).astype(LOW)

            loop(2, context, CONTEXT_UNROLL)

            def attend_some(i):
                half_bias = bias[...]
                group = [i * CROSS_PAIRS + k for k in range(CROSS_PAIRS)]
                pairs = [
                    (cq[rows, pair_cols(pair)], ctx[keys, pair_cols(pair)], ctx[keys, pair_cols(pair, 1)])
                    for pair in group
                ]
                results = attend(pairs, jnp.concatenate([half_bias, half_bias], 0))
                for pair, result in zip(group, results):
                    co[rows, pair_cols(pair)] = result

            loop(PAIRS // CROSS_PAIRS, attend_some)
            def tile(cols, start):
                mixed = dot_nn(co[rows, :], wa[:, cols_at(5 * D + start, SHALLOW)])
                x2[rows, cols] = x1[rows, cols] + mixed

            tiles(SHALLOW, tile)

            def top_norm(i):
                part = rows_at(base + i * ROW, ROW)
                b[part, :] = norm_low(x2[part, :], third_gain)

            loop(ROWS_MB, top_norm)

            def expand(j):
                cols = cols_at(j * 512, 512)
                active, bend = gelu_parts(dot_nn(b[rows, :], wi[:, cols]))
                u[rows, cols] = active.astype(LOW)
                slope[rows, cols] = (bend * slope[rows, cols].astype(WIDE)).astype(LOW)

            loop(FF // 512, expand, EXPAND_UNROLL)
            def tile(cols, start):
                tmp[0:DEC_MB, cols] = dot_nt(slope[rows, :], wi[cols_at(start, DEEP), :])

            tiles(DEEP, tile)

            def top_back(i):
                part = rows_at(base + i * ROW, ROW)
                grad, gain_row = norm_back(tmp[rows_at(i * ROW, ROW), :], x2[part, :], third_gain)
                grad = grad + ct[part, :].astype(WIDE)
                g2w[part, :] = grad
                g2[part, :] = grad.astype(LOW)
                add_gain(2, gain_row)

            loop(ROWS_MB, top_back)
            def tile(cols, start):
                grads = dot_nt(g2[rows, :], wa[cols_at(start, SHALLOW), 5 * D : 6 * D])
                dmix[0:DEC_MB, cols] = grads.astype(LOW)

            tiles(SHALLOW, tile)

            def attend_back_some(i):
                parts = [bias_t[j] for j in range(ROWS_MB)]
                group = [i * CROSS_BACK_PAIRS + k for k in range(CROSS_BACK_PAIRS)]
                pairs = [
                    (
                        cq[rows, pair_cols(pair)], ctx[keys, pair_cols(pair)],
                        ctx[keys, pair_cols(pair, 1)], dmix[0:DEC_MB, pair_cols(pair)],
                    )
                    for pair in group
                ]
                results = attend_back(pairs, jnp.concatenate(parts + parts, 1))
                for pair, grads in zip(group, results):
                    cq[rows, pair_cols(pair)] = grads[0]
                    ctx[keys, pair_cols(pair)] = grads[1]
                    ctx[keys, pair_cols(pair, 1)] = grads[2]

            loop(PAIRS // CROSS_BACK_PAIRS, attend_back_some)
            def tile(cols, start):
                sent[micro, :, cols] = dot_nt(ctx[keys, :], wctx[cols_at(start, DEEP), :]).astype(LOW)

            tiles(DEEP, tile)
            across(sent.at[micro], micro).start()

        loop(MICRO, cross)
        stores = [
            store(a.at[full], a_out.at[full], 0), store(o.at[full], o_out.at[full], 1),
            store(b.at[full], b_out.at[full], 2), store(u.at[full], u_out.at[full], 3),
            store(slope.at[full], dh_out.at[full], 7), store(g2.at[full], g2_out.at[full], 6),
            store(co, co_out, 10), store(cq, dq_out, 11), store(landed, up_out, 12),
            store(ctx, dctx_out, 13), store(c.at[full], c_out.at[full], 14),
        ]
        for copy in stores:
            copy.start()

        def finish(micro):
            base = micro * DEC_MB
            rows = rows_at(base, DEC_MB)
            def tile(cols, start):
                tmp[0:DEC_MB, cols] = dot_nt(cq[rows, :], wa[cols_at(start, SHALLOW), 4 * D : 5 * D])

            tiles(SHALLOW, tile)

            def mid_back(i):
                part = rows_at(base + i * ROW, ROW)
                grad, gain_row = norm_back(tmp[rows_at(i * ROW, ROW), :], x1[part, :], second_gain)
                grad = grad + g2w[part, :]
                x1[part, :] = grad
                g1[part, :] = grad.astype(LOW)
                add_gain(1, gain_row)

            loop(ROWS_MB, mid_back)
            def tile(cols, start):
                grads = dot_nt(g1[rows, :], wa[cols_at(start, SHALLOW), 3 * D : 4 * D])
                dmix[0:DEC_MB, cols] = grads.astype(LOW)

            tiles(SHALLOW, tile)

            def self_back(i):
                row_bias = self_bias(micro * ROWS_MB + i, True)

                def some(j):
                    attend_rows_back(
                        qkv, rows_at(base + i * ROW, ROW), dmix, rows_at(i * ROW, ROW), row_bias,
                        pair_group(j, SELF_BACK_PAIRS),
                    )

                loop(PAIRS // SELF_BACK_PAIRS, some)

            loop(ROWS_MB, self_back)
            def tile(cols, start):
                tmp[0:DEC_MB, cols] = dot_nt(qkv[rows, :], wa[cols_at(start, DEEP), 0 : 3 * D])

            tiles(DEEP, tile)

            def low_back(i):
                part = rows_at(base + i * ROW, ROW)
                grad, gain_row = norm_back(
                    tmp[rows_at(i * ROW, ROW), :], x[part, :].astype(WIDE), first_gain
                )
                x1[part, :] = x1[part, :] + grad
                exch[rows_at(DEC_ROWS + base + i * ROW, ROW), :] = x1[part, 0:HALF].astype(LOW)
                add_gain(0, gain_row)

            loop(ROWS_MB, low_back)
            for half, kept in enumerate((exch, decoded_half)):
                cols = slice(half * HALF, (half + 1) * HALF)
                kept[rows, :] = (x2[rows, cols] + dot_nn(u[rows, :], wo[:, cols])).astype(LOW)

        loop(MICRO, finish)
        late = [
            store(qkv.at[full], dqkv_out.at[full], 4), store(g1.at[full], g1_out.at[full], 5),
            store(x1.at[full, HALF:], caption_own, 8), store(exch, exch_out, 9),
            store(decoded_half, decoded_own, 15),
        ]
        for copy in late:
            copy.start()
        for copy in stores + late:
            copy.wait()
        for micro in range(MICRO):
            across(sent.at[micro], micro).wait_send()
        ctx_copy(ctx_part(quarter), quarter, {"dp": side}, 1).wait_send()
        ctx_copy(ctx_part(quarter), quarter, {"dp": twin}, 2).wait_send()
        ctx_copy(ctx_part(quarter), quarter, {"dp": twin}, 3).wait_send()

    gain_in.wait()
    first_gain, second_gain, third_gain = gain_rows[0:1, :], gain_rows[1:2, :], gain_rows[2:3, :]

    @pl.when(section == 0)
    def _():
        encoder()

    @pl.when(section == 1)
    def _():
        decoder()


def main_call(patches, captions, segments, seg_images, attn_w, w_in, w_out, gains, cot):
    def low(*shape):
        return jax.ShapeDtypeStruct(shape, LOW)

    def wide(*shape):
        return jax.ShapeDtypeStruct(shape, WIDE)

    outs = [
        low(ENC_ROWS, D), low(ENC_ROWS, D), low(DEC_ROWS, D), low(ENC_ROWS, D), low(ENC_ROWS, FF),
        low(ENC_ROWS, 3 * D), low(ENC_ROWS, D), low(ENC_ROWS, D), low(ENC_ROWS, FF),
        low(DEC_ROWS, D), low(DEC_ROWS, D), low(MICRO, ENC_MB, D), low(ENC_ROWS, 2 * D),
        wide(8, D), wide(ENC_ROWS, HALF), low(DEC_ROWS, HALF), wide(DEC_ROWS, HALF),
        low(2 * DEC_ROWS, HALF),
    ]
    any_spec = pl.BlockSpec(memory_space=pl.ANY)
    vmem_spec = pl.BlockSpec(memory_space=pltpu.VMEM)
    out_specs = [any_spec] * len(outs)
    out_specs[13] = vmem_spec
    vmem = pltpu.VMEM
    scratch = [
        vmem((D, 6 * D), LOW), vmem((D, FF), LOW), vmem((FF, D), LOW), vmem((D, 2 * D), LOW),
        vmem((ENC_ROWS, D), LOW), vmem((DEC_ROWS, D), LOW),
        vmem((ENC_ROWS, D), LOW), vmem((ENC_ROWS, D), LOW), vmem((ENC_ROWS, D), LOW),
        vmem((ENC_ROWS, D), LOW),
        vmem((ENC_ROWS, 3 * D), LOW), vmem((max(ENC_MB, DEC_ROWS), FF), LOW), vmem((ENC_ROWS, FF), LOW),
        vmem((ENC_ROWS, D), WIDE), vmem((ENC_ROWS, D), WIDE),
        vmem((ENC_ROWS, D), LOW), vmem((ENC_ROWS, D), LOW),
        vmem((MICRO, ENC_MB, D), LOW), vmem((max(ENC_MB, DEC_ROWS), D), LOW),
        vmem((ENC_ROWS, 2 * D), LOW),
        vmem((DEC_ROWS, D), LOW), vmem((DEC_ROWS, D), LOW), vmem((DEC_ROWS, D), WIDE),
        vmem((ENC_MB, D), WIDE), vmem((MICRO, ENC_MB, D), LOW),
        vmem((DEC_MB, ENC_MB), WIDE), vmem((ROWS_MB, ENC_MB, ROW), WIDE),
        vmem((2 * DEC_ROWS, HALF), LOW), vmem((DEC_ROWS, HALF), LOW),
        vmem((3, D), WIDE), pltpu.SemaphoreType.DMA((7,)), pltpu.SemaphoreType.DMA((16,)),
        pltpu.SemaphoreType.DMA((MICRO,)), pltpu.SemaphoreType.DMA((MICRO,)),
        pltpu.SemaphoreType.DMA((4,)), pltpu.SemaphoreType.DMA((4,)),
    ]
    return pl.pallas_call(
        main_kernel,
        name="layers",
        out_shape=outs,
        in_specs=[any_spec, any_spec, vmem_spec, pl.BlockSpec(memory_space=pltpu.SMEM)]
        + [any_spec] * 5,
        out_specs=out_specs,
        scratch_shapes=scratch,
        compiler_params=pltpu.CompilerParams(
            collective_id=1, has_side_effects=True, vmem_limit_bytes=63 * MIB
        ),
    )(patches, captions, segments, seg_images, attn_w, w_in, w_out, gains, cot)


CHUNK = 256
SLOTS = 8
FIRST_LAG = 2
FAR_EVERY = 6
LAG = 4
GAIN_STEPS = 5
OUT_IDS = 12
ONLY_DEC = 12
CTX_IDS = 6


def grads_kernel(n_bits, *refs):
    (
        a_in, o_in, c_in, b_in, u_in, dqkv_in, g1_in, g2_in, dh_in, co_in, dq_in, up_in, dctx_in,
        gains_in, patch_own, decoded_own, caption_own, exch_in, cot_in,
        shares, gain_share, patch_out, decoded_out, caption_out,
        a, o, c, b, u, dqkv, g1, g2, dh, co, dq, up, dctx, cot,
        part, ctx_sum, exch, patch_rows, gain_sum, gain_in,
    ) = refs[:44]
    recv = refs[44 : 44 + n_bits]
    load_sem, own_sem, send_sem, recv_sem, gain_send, gain_recv, far_send, far_recv = refs[44 + n_bits :]
    section = lax.axis_index("section")
    dp = lax.axis_index("dp")
    bits = [(dp // (1 << k)) % 2 for k in range(n_bits)]
    partners = [{"dp": dp + (1 << k) * (1 - 2 * bits[k])} for k in range(n_bits)]
    across = {"section": 1 - section}
    barrier = pltpu.get_barrier_semaphore()

    def greet(target):
        pl.semaphore_signal(barrier, inc=1, device_id=target, device_id_type=MESH)

    for target in partners:
        greet(target)

    @pl.when(section == 1)
    def _():
        pl.semaphore_wait(barrier, n_bits)
        greet(across)

    @pl.when(section == 0)
    def _():
        pl.semaphore_wait(barrier, n_bits + 1)
        greet(across)

    rows = part.shape[-2]
    owners = 1 << n_bits
    total = recv[0].shape[0]
    begin = ONLY_DEC * (1 - section)

    def remote(src, dst, send, receive, target):
        return pltpu.make_async_remote_copy(
            src_ref=src, dst_ref=dst, send_sem=send, recv_sem=receive, device_id=target,
            device_id_type=MESH)

    def gain_copy(k):
        return remote(gain_sum.at[k], gain_in.at[k], gain_send.at[k], gain_recv.at[k], partners[k])

    def exch_copy():
        return remote(exch_in, exch, far_send.at[0], far_recv.at[0], across)

    def ctx_copy():
        return remote(ctx_sum, shares.at[0:CTX_IDS], far_send.at[1], far_recv.at[1], across)

    gain_sum[0] = gains_in[...]
    gain_copy(0).start()

    def load_plan(is_dec):
        count = DEC_ROWS if is_dec else ENC_ROWS

        def short(src, dst):
            return src.at[0:count], dst.at[0:count]

        plan = {
            0: short(u_in, u), 1: short(g2_in, g2), 2: short(b_in, b), 3: short(dh_in, dh),
            4: short(a_in, a), 5: short(dqkv_in, dqkv), 6: short(o_in, o), 7: short(g1_in, g1),
        }
        if is_dec:
            only = {
                8: (up_in, up), 9: (dctx_in, dctx), 10: (c_in, c), 11: (dq_in, dq),
                12: (co_in, co), 13: (cot_in, cot),
            }
            plan = {**only, **plan}
        return plan

    def need(is_dec, *slots):
        plan = load_plan(is_dec)
        for slot in slots:
            pltpu.make_async_copy(*plan[slot], load_sem.at[slot]).wait()

    for is_dec in (False, True):
        @pl.when(section == int(is_dec))
        def _(is_dec=is_dec):
            for slot, (src, dst) in load_plan(is_dec).items():
                pltpu.make_async_copy(src, dst, load_sem.at[slot]).start()
            if is_dec:
                pltpu.make_async_copy(decoded_own, decoded_out, load_sem.at[14]).start()
                pltpu.make_async_copy(caption_own, caption_out, load_sem.at[15]).start()
            else:
                pltpu.make_async_copy(patch_own, patch_rows, load_sem.at[14]).start()

    def core_copy(index):
        slot = index % SLOTS
        return remote(part.at[slot, 1 - bits[0]], recv[0].at[index], send_sem.at[0, index],
                      recv_sem.at[0, index], partners[0])

    near_first = list(range(1, n_bits))
    far_first = list(range(2, n_bits)) + [1]

    def stage_cut(order, stage, index, flip):
        bit = order[stage - 1]
        left = sorted(order[stage - 1 :], reverse=True)
        value = bits[bit] + flip * (1 - 2 * bits[bit])
        return (index,) + (slice(None),) * left.index(bit) + (value,)

    def stage_copy(order, stage, index):
        return remote(
            recv[stage - 1].at[stage_cut(order, stage, index, 1)], recv[stage].at[index],
            send_sem.at[stage, index], recv_sem.at[stage, index], partners[order[stage - 1]])

    def in_order(index, action):
        is_far = index % FAR_EVERY == FAR_EVERY // 2

        @pl.when(is_far)
        def _():
            action(far_first)

        @pl.when(jnp.logical_not(is_far))
        def _():
            action(near_first)

    def advance(i):
        for stage in range(n_bits):
            j = i - FIRST_LAG - stage * LAG

            @pl.when((j >= begin) & (j < total))
            def _(stage=stage, j=j):
                if stage == 0:
                    core_copy(j).wait()
                    summed = part[j % SLOTS, bits[0]].astype(WIDE) + recv[0][j].astype(WIDE)
                    recv[0][j] = summed.astype(LOW)
                    in_order(j, lambda order: stage_copy(order, 1, j).start())
                elif stage < n_bits - 1:
                    def step(order):
                        stage_copy(order, stage, j).wait()
                        mine = recv[stage - 1][stage_cut(order, stage, j, 0)]
                        summed = mine.astype(WIDE) + recv[stage][j].astype(WIDE)
                        recv[stage][j] = summed.astype(LOW)
                        stage_copy(order, stage + 1, j).start()

                    in_order(j, step)
                else:
                    def step(order):
                        stage_copy(order, stage, j).wait()

                    in_order(j, step)
                    last = jnp.where(j % FAR_EVERY == FAR_EVERY // 2, bits[far_first[-1]], bits[near_first[-1]])
                    mine = recv[stage - 1][j, last]
                    summed = mine.astype(WIDE) + recv[stage][j].astype(WIDE)

                    @pl.when(j < CTX_IDS)
                    def _():
                        ctx_sum[j] = summed

                    @pl.when(j >= CTX_IDS)
                    def _():
                        shares[j - CTX_IDS] = summed

        for k in range(n_bits):
            @pl.when(i == ONLY_DEC + GAIN_STEPS * (k + 1))
            def _(k=k):
                gain_copy(k).wait()
                summed = gain_sum[k] + gain_in[k]
                if k == n_bits - 1:
                    own = jnp.zeros((8, rows), WIDE)
                    for owner in range(owners):
                        own = jnp.where(dp == owner, summed[:, owner * rows : (owner + 1) * rows], own)
                    gain_share[...] = own
                else:
                    gain_sum[k + 1] = summed
                    gain_copy(k + 1).start()

    def place(index, first_owner, block):
        for k in range(block.shape[0] // rows):
            owner = first_owner + k
            path = tuple((owner >> bit) & 1 for bit in reversed(range(1, n_bits)))
            part[(index % SLOTS, owner & 1) + path] = block[k * rows : (k + 1) * rows].astype(LOW)

    def simple_phase(first, count, left, right, col, row_count):
        def step(i):
            index = first + i
            cols = cols_at(col + i * CHUNK, CHUNK)
            if row_count is None:
                value = dot_tn(left[...].reshape(-1, D), right[:, cols])
            else:
                value = dot_tn(left[0:row_count, :], right[0:row_count, cols])
            place(index, 0, value)
            core_copy(index).start()
            advance(index)
        loop(count, step)

    def out_phase(first, right, row_count):
        share = FF // owners
        blocks = share // rows
        step_owners = D // share

        def step(i):
            cols = cols_at(i * CHUNK, CHUNK)
            base = first + i * blocks
            for piece in range(FF // D):
                value = dot_tn(u[0:row_count, piece * D : (piece + 1) * D], right[0:row_count, cols])
                for k in range(step_owners):
                    for q in range(blocks):
                        low = k * share + q * rows
                        place(base + q, piece * step_owners + k, value[low : low + rows])
            loop(blocks, lambda q: core_copy(base + q).start())
            loop(blocks, lambda q: advance(base + q))
        loop(D // CHUNK, step)

    @pl.when(section == 1)
    def _():
        need(True, 8, 9)
        simple_phase(0, CTX_IDS, up, dctx, 0, None)
        need(True, 10, 11)
        simple_phase(CTX_IDS, 3, c, dq, 0, DEC_ROWS)
        need(True, 12, 1)
        simple_phase(CTX_IDS + 3, 3, co, g2, 0, DEC_ROWS)

    for is_dec in (False, True):
        @pl.when(section == int(is_dec))
        def _(is_dec=is_dec):
            count = DEC_ROWS if is_dec else ENC_ROWS
            need(is_dec, 0, 13 if is_dec else 1)
            out_phase(ONLY_DEC, cot if is_dec else g2, count)
            need(is_dec, 2, 3)
            simple_phase(ONLY_DEC + OUT_IDS, FF // CHUNK, b, dh, 0, count)

    @pl.when(section == 1)
    def _():
        pl.semaphore_wait(barrier, 1)
        ctx_copy().start()

    exch_copy().start()

    for is_dec in (False, True):
        @pl.when(section == int(is_dec))
        def _(is_dec=is_dec):
            count = DEC_ROWS if is_dec else ENC_ROWS
            need(is_dec, 4, 5)
            first = ONLY_DEC + OUT_IDS + FF // CHUNK
            simple_phase(first, 3 * D // CHUNK, a, dqkv, 0, count)
            need(is_dec, 6, 7)
            simple_phase(first + 3 * D // CHUNK, D // CHUNK, o, g1, 0, count)

    exch_copy().wait()

    @pl.when(section == 0)
    def _():
        pltpu.make_async_copy(patch_own, patch_rows, load_sem.at[14]).wait()
        for image in range(MICRO * IMG_MB):
            patch_out[image * PATCHES : (image + 1) * PATCHES, :] = patch_rows[
                image * IMG_ROWS : image * IMG_ROWS + PATCHES, :
            ]
        decoded_out[...] = exch[0:DEC_ROWS, :]
        caption_out[...] = exch[DEC_ROWS : 2 * DEC_ROWS, :].astype(WIDE)

    @pl.when(section == 1)
    def _():
        pltpu.make_async_copy(decoded_own, decoded_out, load_sem.at[14]).wait()
        pltpu.make_async_copy(caption_own, caption_out, load_sem.at[15]).wait()
        for image in range(MICRO * IMG_MB):
            patch_out[image * PATCHES : (image + 1) * PATCHES, :] = exch[
                image * IMG_ROWS : image * IMG_ROWS + PATCHES, :
            ].astype(WIDE)

    loop(FIRST_LAG + (n_bits - 1) * LAG, lambda i: advance(total + i))

    @pl.when(section == 0)
    def _():
        ctx_copy().wait_recv()

    @pl.when(section == 1)
    def _():
        ctx_copy().wait_send()


def grads_call(n_dp, *operands):
    n_bits = n_dp.bit_length() - 1
    rows = D // n_dp
    share = FF // n_dp
    total = ONLY_DEC + 2 * OUT_IDS + 4 * D // CHUNK
    vmem = pltpu.VMEM
    pair = (2,) * (n_bits - 1)
    any_spec = pl.BlockSpec(memory_space=pl.ANY)
    vmem_spec = pl.BlockSpec(memory_space=pltpu.VMEM)
    sem = pltpu.SemaphoreType.DMA
    scratch = [
        vmem((ENC_ROWS, D), LOW), vmem((ENC_ROWS, D), LOW), vmem((DEC_ROWS, D), LOW),
        vmem((ENC_ROWS, D), LOW), vmem((ENC_ROWS, FF), LOW), vmem((ENC_ROWS, 3 * D), LOW),
        vmem((ENC_ROWS, D), LOW), vmem((ENC_ROWS, D), LOW), vmem((ENC_ROWS, FF), LOW),
        vmem((DEC_ROWS, D), LOW), vmem((DEC_ROWS, D), LOW), vmem((MICRO, ENC_MB, D), LOW),
        vmem((ENC_ROWS, 2 * D), LOW), vmem((DEC_ROWS, D), LOW),
        vmem((SLOTS, 2) + pair + (rows, CHUNK), LOW), vmem((CTX_IDS, rows, CHUNK), WIDE),
        vmem((2 * DEC_ROWS, HALF), LOW), vmem((ENC_ROWS, HALF), WIDE),
        vmem((n_bits, 8, D), WIDE), vmem((n_bits, 8, D), WIDE),
    ]
    scratch += [vmem((total,) + pair[k:] + (rows, CHUNK), LOW) for k in range(n_bits)]
    scratch += [
        sem((16,)), sem((1,)), sem((n_bits, total)), sem((n_bits, total)), sem((n_bits,)),
        sem((n_bits,)), sem((2,)), sem((2,)),
    ]
    in_specs = [any_spec] * len(operands)
    in_specs[13] = vmem_spec
    return pl.pallas_call(
        functools.partial(grads_kernel, n_bits),
        name="weight_sums",
        out_shape=(
            jax.ShapeDtypeStruct((total - CTX_IDS, rows, CHUNK), WIDE),
            jax.ShapeDtypeStruct((8, rows), WIDE),
            jax.ShapeDtypeStruct((MICRO * IMG_MB * PATCHES, HALF), WIDE),
            jax.ShapeDtypeStruct((DEC_ROWS, HALF), LOW),
            jax.ShapeDtypeStruct((DEC_ROWS, HALF), WIDE),
        ),
        in_specs=in_specs,
        out_specs=(vmem_spec,) * 5,
        scratch_shapes=scratch,
        compiler_params=pltpu.CompilerParams(
            collective_id=2, has_side_effects=True, vmem_limit_bytes=63 * MIB
        ),
    )(*operands)


def place_kernel(
    shares, gain_share, patch_in, decoded_in, caption_in,
    decoded_out, caption_out, patch_out, attn_out, in_out, out_out, gain_out, sem,
):
    rows = shares.shape[1]
    moves = [
        (patch_in, patch_out), (caption_in, caption_out), (decoded_in, decoded_out),
        (gain_share.at[0:3], gain_out.at[0]),
    ]
    first_w_in = CTX_IDS + OUT_IDS
    first_attn = first_w_in + FF // CHUNK
    blocks = OUT_IDS * CHUNK // D

    def cols(index):
        return slice(index * CHUNK, (index + 1) * CHUNK)

    for k in range(4 * D // CHUNK):
        moves.append((shares.at[first_attn + k], attn_out.at[0, :, cols(k)]))
    for k in range(CTX_IDS):
        moves.append((shares.at[k], attn_out.at[0, :, cols(4 * D // CHUNK + k)]))
    for k in range(FF // CHUNK):
        moves.append((shares.at[first_w_in + k], in_out.at[0, :, cols(k)]))
    for k in range(OUT_IDS):
        part = slice((k % blocks) * rows, (k % blocks + 1) * rows)
        moves.append((shares.at[CTX_IDS + k], out_out.at[0, part, cols(k // blocks)]))
    copies = [
        pltpu.make_async_copy(src, dst, sem.at[index]) for index, (src, dst) in enumerate(moves)
    ]
    for copy in copies:
        copy.start()
    for copy in copies:
        copy.wait()


def kernel_sums(n_dp, operands):
    results = grads_call(n_dp, *operands)
    rows = D // n_dp
    any_spec = pl.BlockSpec(memory_space=pl.ANY)
    patch_out, decoded_out, caption_out = results[2:]
    shapes = [decoded_out, caption_out, patch_out] + [
        jax.ShapeDtypeStruct(shape, WIDE)
        for shape in ((1, rows, 6 * D), (1, rows, FF), (1, FF // n_dp, D), (1, 3, rows))
    ]
    return pl.pallas_call(
        place_kernel,
        name="place_sums",
        out_shape=[jax.ShapeDtypeStruct(item.shape, item.dtype) for item in shapes],
        in_specs=[any_spec] * 5,
        out_specs=[pl.BlockSpec(memory_space=pltpu.VMEM)] * 7,
        scratch_shapes=[pltpu.SemaphoreType.DMA((64,))],
    )(*results)


def shifted(block, distance):
    devices = range(lax.axis_size("section"))
    route = [(i - distance, i) for i in devices if i - distance in devices]
    return lax.ppermute(block, "section", route)


def plain_sums(operands):
    (
        a, o, c, b, u, dqkv, g1, g2, dh, co, dq, up, dctx,
        gains, patch_own, decoded_own, caption_own, exch, cot,
    ) = operands
    is_first = lax.axis_index("section") == 0
    up = up.reshape(ENC_ROWS, D)

    def encoder_parts():
        return (
            jnp.concatenate([dot_tn(a, dqkv), dot_tn(o, g1)], 1), jnp.zeros((D, 2 * D), WIDE),
            jnp.zeros((D, 2 * D), WIDE), dot_tn(b, dh), dot_tn(u, g2),
        )

    def decoder_parts():
        rows = slice(0, DEC_ROWS)
        return (
            jnp.concatenate([dot_tn(a[rows], dqkv[rows]), dot_tn(o[rows], g1[rows])], 1),
            jnp.concatenate([dot_tn(c, dq), dot_tn(co, g2[rows])], 1),
            dot_tn(up, dctx), dot_tn(b[rows], dh[rows]), dot_tn(u[rows], cot),
        )

    parts = lax.cond(is_first, encoder_parts, decoder_parts)
    sums = [lax.psum_scatter(part, "dp", scatter_dimension=0, tiled=True) for part in parts]
    last = jnp.where(is_first, shifted(sums[2], -1), sums[1])
    moved = lax.ppermute(exch, "section", [(0, 1), (1, 0)])

    def unpad(block):
        shaped = block[:ENC_ROWS].reshape(MICRO * IMG_MB, IMG_ROWS, HALF)
        return shaped[:, :PATCHES].reshape(-1, HALF).astype(WIDE)

    return (
        jnp.where(is_first, moved[:DEC_ROWS], decoded_own),
        jnp.where(is_first, moved[DEC_ROWS:].astype(WIDE), caption_own),
        jnp.where(is_first, unpad(patch_own), unpad(moved)),
        jnp.concatenate([sums[0], last], 1),
        sums[3],
        sums[4],
        lax.psum_scatter(gains[:3], "dp", scatter_dimension=1, tiled=True),
    )


def with_section(results):
    return tuple(results[:3]) + tuple(share[None] for share in results[3:])


def local(patches, captions, segments, seg_images, attn_w, w_in, w_out, norm_gains, cotangent):
    n_dp = lax.axis_size("dp")
    kept = main_call(
        patches, captions, segments, seg_images, attn_w, w_in, w_out, norm_gains, cotangent
    )
    operands = list(kept) + [cotangent]
    if n_dp & (n_dp - 1) == 0 and (D // n_dp) % 16 == 0:
        results = kernel_sums(n_dp, operands)
    else:
        results = with_section(plain_sums(operands))
    return tuple(results)


def solution(mesh):
    placed = (
        P("dp", None),
        P("dp", None),
        P("dp", None),
        P("dp", None),
        P("section", None, None),
        P("section", None, None),
        P("section", None, None),
        P("section", None, None),
        P("dp", None),
    )
    return jax.shard_map(
        local,
        mesh=mesh,
        in_specs=placed,
        out_specs=(
            P("dp", "section"),
            P("dp", "section"),
            P("dp", "section"),
            P("section", "dp", None),
            P("section", "dp", None),
            P("section", "dp", None),
            P("section", None, "dp"),
        ),
        check_vma=False,
    )
```

```python
import functools
import jax
import jax.numpy as jnp
from jax import lax
from jax.experimental import pallas as pl
from jax.experimental.pallas import tpu as pltpu
from jax.sharding import PartitionSpec as P

D = 768
FF = 3072
HEADS = 12
HEAD = 64
PATCHES = 196
ROW = 128
SEGS = 4
MICRO = 2
IMG_MB = 2
ROWS_MB = 2
NORM_EPS = 1e-06
SCORE_SCALE = 0.125
MASKED = -1e30
ROOT_HALF = 0.7071067811865476
INV_ROOT_TWO_PI = 0.3989422804014327
MESH = pl.DeviceIdType.MESH
MIB = 1 << 20

LOW = jnp.bfloat16
WIDE = jnp.float32
IMG_ROWS = -(-PATCHES // 16) * 16
ENC_MB = IMG_MB * IMG_ROWS
ENC_ROWS = MICRO * ENC_MB
DEC_MB = ROWS_MB * ROW
DEC_ROWS = MICRO * DEC_MB
PAIR = 2 * HEAD
PAIRS = HEADS // 2
HALF = D // 2
QUARTER = D // 4
CROSS_PAIRS = 2
EXPAND_UNROLL = 1
BACK_UNROLL = 1
CONTEXT_UNROLL = 1
PROJECT_UNROLL = 1
BACK_PAIRS = 2
ROW_PAIRS = 3
SELF_PAIRS = 3
SELF_BACK_PAIRS = 3
DEEP = 256
SHALLOW = 384
CROSS_BACK_PAIRS = 2


def dot_nn(left, right):
    return lax.dot_general(left, right, (((1,), (0,)), ((), ())), preferred_element_type=WIDE)


def dot_nt(left, right):
    return lax.dot_general(left, right, (((1,), (1,)), ((), ())), preferred_element_type=WIDE)


def dot_tn(left, right):
    return lax.dot_general(left, right, (((0,), (0,)), ((), ())), preferred_element_type=WIDE)


def rows_at(start, size):
    return pl.ds(pl.multiple_of(start, 16), size)


def cols_at(start, size):
    if isinstance(start, int):
        return slice(start, start + size)
    return pl.ds(pl.multiple_of(start, 128), size)


def norm_hat(values):
    centred = values - jnp.mean(values, -1, keepdims=True)
    inverse = lax.rsqrt(jnp.mean(centred * centred, -1, keepdims=True) + NORM_EPS)
    return centred * inverse, inverse


def norm_low(values, gain):
    return (norm_hat(values)[0] * gain).astype(LOW)


def norm_back(upstream, values, gain):
    normed, inverse = norm_hat(values)
    scaled = upstream * gain
    inner = (
        scaled
        - jnp.mean(scaled, -1, keepdims=True)
        - normed * jnp.mean(scaled * normed, -1, keepdims=True)
    )
    return inner * inverse, jnp.sum(upstream * normed, 0, keepdims=True)


def gelu_parts(hidden):
    normal_cdf = 0.5 * (1.0 + lax.erf(hidden * ROOT_HALF))
    slope = normal_cdf + hidden * INV_ROOT_TWO_PI * jnp.exp(-0.5 * hidden * hidden)
    return hidden * normal_cdf, slope


def first_lanes(rows):
    return lax.broadcasted_iota(jnp.int32, (rows, PAIR), 1) < HEAD


def split_pair(block):
    first = (lax.broadcasted_iota(jnp.int32, (1, PAIR), 1) < HEAD).astype(WIDE)
    return jnp.concatenate([block * first.astype(LOW), block * (1.0 - first).astype(LOW)], 0)


def join_pair(stacked):
    rows = stacked.shape[0] // 2
    return jnp.where(first_lanes(rows), stacked[:rows], stacked[rows:])


def attend(pairs, bias):
    stacked = [split_pair(queries) * SCORE_SCALE for queries, _, _ in pairs]
    scores = [dot_nt(stack, pair[1]) + bias for stack, pair in zip(stacked, pairs)]
    powers = [jnp.exp(block - jnp.max(block, -1, keepdims=True)) for block in scores]
    scales = [1.0 / jnp.sum(block, -1, keepdims=True) for block in powers]
    return [
        join_pair(dot_nn(block.astype(LOW), pair[2]) * scale).astype(LOW)
        for block, pair, scale in zip(powers, pairs, scales)
    ]


def attend_back(pairs, bias):
    stacked = [split_pair(pair[0]) * SCORE_SCALE for pair in pairs]
    grads = [split_pair(pair[3]) for pair in pairs]
    scores = [dot_nt(pair[1], stack) + bias for pair, stack in zip(pairs, stacked)]
    grad_chances = [dot_nt(pair[2], grad) for pair, grad in zip(pairs, grads)]
    powers = [jnp.exp(block - jnp.max(block, 0, keepdims=True)) for block in scores]
    chances = [block * (1.0 / jnp.sum(block, 0, keepdims=True)) for block in powers]
    inner = [jnp.sum(left * right, 0, keepdims=True) for left, right in zip(grad_chances, chances)]
    grad_scores = [
        (chance * (grad - mean)).astype(LOW)
        for chance, grad, mean in zip(chances, grad_chances, inner)
    ]
    grad_keys = [dot_nn(grad, stack) for grad, stack in zip(grad_scores, stacked)]
    grad_values = [dot_nn(chance.astype(LOW), grad) for chance, grad in zip(chances, grads)]
    grad_queries = [
        join_pair(dot_tn(grad, pair[1])) * SCORE_SCALE for grad, pair in zip(grad_scores, pairs)
    ]
    return [
        tuple(part.astype(LOW) for part in parts)
        for parts in zip(grad_queries, grad_keys, grad_values)
    ]


def pair_cols(pair, column=0):
    start = column * D + pair * PAIR
    return cols_at(start, PAIR) if not isinstance(start, int) else slice(start, start + PAIR)


def tiles(width, body):
    loop(D // width, lambda j: body(cols_at(j * width, width), j * width))


def pair_group(step, size):
    first = (step % (PAIRS // size)) * size
    return [first + pair for pair in range(size)]


def attend_rows(qkv, rows, mixed, bias, group):
    pairs = [[qkv[rows, pair_cols(pair, part)] for part in range(3)] for pair in group]
    for pair, result in zip(group, attend(pairs, bias)):
        mixed[rows, pair_cols(pair)] = result


def attend_rows_back(qkv, rows, grad_mixed, grad_rows, bias, group):
    pairs = [
        [qkv[rows, pair_cols(pair, part)] for part in range(3)]
        + [grad_mixed[grad_rows, pair_cols(pair)]]
        for pair in group
    ]
    for pair, results in zip(group, attend_back(pairs, bias)):
        for part in range(3):
            qkv[rows, pair_cols(pair, part)] = results[part]


def loop(count, body, unroll=1):
    def several(i, carry):
        for k in range(unroll):
            body(i * unroll + k)
        return carry

    if count == unroll:
        several(0, 0)
    else:
        lax.fori_loop(0, count // unroll, several, 0)


def main_kernel(*refs):
    (
        patches, captions, segments, seg_images, attn_w, w_in, w_out, gains, cot,
        a_out, o_out, c_out, b_out, u_out, dqkv_out, g1_out, g2_out, dh_out,
        co_out, dq_out, up_out, dctx_out, gain_out, patch_own, decoded_own, caption_own, exch_out,
        wa, wi, wo, wctx, x, ct, a, o, b, c, qkv, u, slope, x1, x2, g1, g2, landed, dmix, ctx,
        co, cq, g2w, tmp, sent, bias, bias_t, exch, decoded_half,
        gain_rows, load_sem, out_sem, up_send, up_recv, ctx_send, ctx_recv,
    ) = refs
    section = lax.axis_index("section")
    dp = lax.axis_index("dp")
    quarter = dp % 4
    side = dp + 2 * (1 - 2 * ((dp // 2) % 2))
    twin = dp + 1 - 2 * (dp % 2)
    other_quarter = quarter + 2 * (1 - 2 * (quarter // 2))
    barrier = pltpu.get_barrier_semaphore()
    for target in ({"section": 1 - section}, {"dp": side}, {"dp": twin}):
        pl.semaphore_signal(barrier, inc=1, device_id=target, device_id_type=MESH)
    pl.semaphore_wait(barrier, 3)

    gain_out[...] = jnp.zeros_like(gain_out)

    def across(src, index):
        return pltpu.make_async_remote_copy(
            src_ref=src, dst_ref=landed.at[index], send_sem=up_send.at[index],
            recv_sem=up_recv.at[index], device_id={"section": 1 - section}, device_id_type=MESH)

    def ctx_part(index):
        return wctx.at[rows_at(index * QUARTER, QUARTER), :]

    def ctx_copy(src, part, target, slot):
        return pltpu.make_async_remote_copy(
            src_ref=src, dst_ref=ctx_part(part), send_sem=ctx_send.at[slot],
            recv_sem=ctx_recv.at[slot], device_id=target, device_id_type=MESH)

    def load(src, dst, slot):
        return pltpu.make_async_copy(src, dst, load_sem.at[slot])

    weight_loads = [
        load(attn_w.at[0, :, 0 : 3 * D], wa.at[:, 0 : 3 * D], 0),
        load(attn_w.at[0, :, 3 * D :], wa.at[:, 3 * D :], 1),
        load(w_in.at[0], wi, 2),
        load(w_out.at[0], wo, 3),
    ]

    gain_in = load(gains.at[0], gain_rows, 6)
    gain_in.start()

    def store(src, dst, slot):
        return pltpu.make_async_copy(src, dst, out_sem.at[slot])

    def add_gain(index, row):
        gain_out[index : index + 1, :] = gain_out[index : index + 1, :] + row

    def encoder():
        ctx_copy(
            attn_w.at[0, rows_at(quarter * QUARTER, QUARTER), 4 * D : 6 * D], quarter,
            {"section": 1 - section}, 0,
        ).start()
        rows_in = load(patches, g1.at[0 : patches.shape[0]], 4)
        rows_in.start()
        for copy in weight_loads:
            copy.start()
        rows_in.wait()
        for image in range(MICRO * IMG_MB):
            low_rows = g1[image * PATCHES : (image + 1) * PATCHES, :]
            x[image * IMG_ROWS : image * IMG_ROWS + PATCHES, :] = low_rows
            x[image * IMG_ROWS + PATCHES : (image + 1) * IMG_ROWS, :] = jnp.zeros(
                (IMG_ROWS - PATCHES, D), LOW
            )
        key_bias = jnp.where(
            lax.broadcasted_iota(jnp.int32, (1, IMG_ROWS), 1) < PATCHES, 0.0, MASKED
        )
        key_bias_t = jnp.where(
            lax.broadcasted_iota(jnp.int32, (IMG_ROWS, 1), 0) < PATCHES, 0.0, MASKED
        )

        def forward(micro):
            base = micro * ENC_MB
            rows = rows_at(base, ENC_MB)

            def low_norm(i):
                part = rows_at(base + i * IMG_ROWS, IMG_ROWS)
                a[part, :] = norm_low(x[part, :].astype(WIDE), first_gain)

            loop(IMG_MB, low_norm)

            @pl.when(micro == 0)
            def _():
                weight_loads[0].wait()

            def project(j):
                cols = cols_at(j * D, D)
                qkv[rows, cols] = dot_nn(a[rows, :], wa[:, cols]).astype(LOW)

            loop(3, project, PROJECT_UNROLL)

            def attend_image(i):
                image, group = i // (PAIRS // ROW_PAIRS), pair_group(i, ROW_PAIRS)
                attend_rows(qkv, rows_at(base + image * IMG_ROWS, IMG_ROWS), o, key_bias, group)

            loop(IMG_MB * PAIRS // ROW_PAIRS, attend_image)

            @pl.when(micro == 0)
            def _():
                weight_loads[1].wait()

            def tile(cols, start):
                mixed = dot_nn(o[rows, :], wa[:, cols_at(3 * D + start, SHALLOW)])
                x1[rows, cols] = x[rows, cols].astype(WIDE) + mixed

            tiles(SHALLOW, tile)

            def mid_norm(i):
                part = rows_at(base + i * IMG_ROWS, IMG_ROWS)
                b[part, :] = norm_low(x1[part, :], second_gain)

            loop(IMG_MB, mid_norm)

            @pl.when(micro == 0)
            def _():
                weight_loads[2].wait()

            @pl.when(micro > 0)
            def _():
                store(u.at[0:ENC_MB], u_out.at[rows], 3).wait()

            def expand(j):
                cols = cols_at(j * 512, 512)
                active, bend = gelu_parts(dot_nn(b[rows, :], wi[:, cols]))
                u[0:ENC_MB, cols] = active.astype(LOW)
                slope[rows, cols] = bend.astype(LOW)

            loop(FF // 512, expand, EXPAND_UNROLL)

            @pl.when(micro == 0)
            def _():
                weight_loads[3].wait()

            def tile(cols, start):
                x2[rows, cols] = x1[rows, cols] + dot_nn(u[0:ENC_MB, :], wo[:, cols])

            tiles(DEEP, tile)
            store(u.at[0:ENC_MB], u_out.at[rows], 3).start()

            def top_norm(i):
                part = rows_at(base + i * IMG_ROWS, IMG_ROWS)
                c[part, :] = norm_low(x2[part, :], third_gain)

            loop(IMG_MB, top_norm)
            across(c.at[rows, :], micro).start()

        loop(MICRO, forward)
        stores = [store(a, a_out, 0), store(o, o_out, 1), store(b, b_out, 2)]
        for copy in stores:
            copy.start()

        def backward(micro):
            base = micro * ENC_MB
            rows = rows_at(base, ENC_MB)
            across(c.at[rows, :], micro).wait()

            def top_norm(i):
                part = rows_at(base + i * IMG_ROWS, IMG_ROWS)
                upstream = landed[micro, rows_at(i * IMG_ROWS, IMG_ROWS), :].astype(WIDE)
                grad, gain_row = norm_back(upstream, x2[part, :], third_gain)
                x2[part, :] = grad
                g2[part, :] = grad.astype(LOW)
                add_gain(2, gain_row)

            loop(IMG_MB, top_norm)

            def expand(j):
                cols = cols_at(j * D, D)
                hidden = dot_nt(g2[rows, :], wo[cols, :])
                slope[rows, cols] = (hidden * slope[rows, cols].astype(WIDE)).astype(LOW)

            loop(FF // D, expand, BACK_UNROLL)
            store(slope.at[rows], dh_out.at[rows], 7).start()
            store(g2.at[rows], g2_out.at[rows], 6).start()
            def tile(cols, start):
                tmp[0:ENC_MB, cols] = dot_nt(slope[rows, :], wi[cols_at(start, DEEP), :])

            tiles(DEEP, tile)

            def mid_norm(i):
                part = rows_at(base + i * IMG_ROWS, IMG_ROWS)
                grad, gain_row = norm_back(
                    tmp[rows_at(i * IMG_ROWS, IMG_ROWS), :], x1[part, :], second_gain
                )
                grad = grad + x2[part, :]
                x1[part, :] = grad
                g1[part, :] = grad.astype(LOW)
                add_gain(1, gain_row)

            loop(IMG_MB, mid_norm)
            store(g1.at[rows], g1_out.at[rows], 5).start()
            def tile(cols, start):
                grads = dot_nt(g1[rows, :], wa[cols_at(start, SHALLOW), 3 * D : 4 * D])
                dmix[0:ENC_MB, cols] = grads.astype(LOW)

            tiles(SHALLOW, tile)

            def attend_image(i):
                image = i // (PAIRS // BACK_PAIRS)
                attend_rows_back(
                    qkv, rows_at(base + image * IMG_ROWS, IMG_ROWS), dmix,
                    rows_at(image * IMG_ROWS, IMG_ROWS), key_bias_t,
                    pair_group(i, BACK_PAIRS),
                )

            loop(IMG_MB * PAIRS // BACK_PAIRS, attend_image)
            def tile(cols, start):
                tmp[0:ENC_MB, cols] = dot_nt(qkv[rows, :], wa[cols_at(start, DEEP), 0 : 3 * D])

            tiles(DEEP, tile)

            def low_norm(i):
                part = rows_at(base + i * IMG_ROWS, IMG_ROWS)
                grad, gain_row = norm_back(
                    tmp[rows_at(i * IMG_ROWS, IMG_ROWS), :], x[part, :].astype(WIDE), first_gain
                )
                x1[part, :] = x1[part, :] + grad
                exch[part, :] = x1[part, HALF:].astype(LOW)
                add_gain(0, gain_row)

            loop(IMG_MB, low_norm)
            store(qkv.at[rows], dqkv_out.at[rows], 4).start()
            store(x1.at[rows, 0:HALF], patch_own.at[rows], 8).start()

        loop(MICRO, backward)
        store(exch, exch_out, 9).start()
        late = [
            store(qkv, dqkv_out, 4), store(g1, g1_out, 5), store(g2, g2_out, 6),
            store(slope, dh_out, 7), store(x1.at[:, 0:HALF], patch_own, 8), store(exch, exch_out, 9),
        ]
        for copy in stores + late + [store(u.at[0:ENC_MB], u_out.at[0:ENC_MB], 3)]:
            copy.wait()
        ctx_copy(
            attn_w.at[0, rows_at(quarter * QUARTER, QUARTER), 4 * D : 6 * D], quarter,
            {"section": 1 - section}, 0,
        ).wait_send()

    def decoder():
        rows_in = load(captions, x.at[0:DEC_ROWS], 4)
        cot_in = load(cot, ct, 5)
        rows_in.start()
        for copy in weight_loads:
            copy.start()
        cot_in.start()
        rows_in.wait()
        full = slice(0, DEC_ROWS)

        def low_norm(i):
            part = rows_at(i * ROW, ROW)
            a[part, :] = norm_low(x[part, :].astype(WIDE), first_gain)

        loop(DEC_ROWS // ROW, low_norm)
        weight_loads[0].wait()

        def project(j):
            cols = cols_at(j * D, D)
            qkv[full, cols] = dot_nn(a[full, :], wa[:, cols]).astype(LOW)

        loop(3, project)

        def segment_pair(row):
            across_rows = jnp.broadcast_to(
                segments[pl.ds(row, 1), :].astype(WIDE), (ROW, ROW)
            )
            return across_rows, across_rows.T

        def self_bias(row, transposed):
            along, down = segment_pair(row)
            sub = lax.broadcasted_iota(jnp.int32, (ROW, ROW), 0)
            lane = lax.broadcasted_iota(jnp.int32, (ROW, ROW), 1)
            order = (lane >= sub) if transposed else (sub >= lane)
            single = jnp.where((along == down) & order, 0.0, MASKED)
            return jnp.concatenate([single, single], 1 if transposed else 0)

        def self_attend(row):
            row_bias = self_bias(row, False)

            def some(i):
                attend_rows(qkv, rows_at(row * ROW, ROW), o, row_bias, pair_group(i, SELF_PAIRS))

            loop(PAIRS // SELF_PAIRS, some)

        loop(DEC_ROWS // ROW, self_attend)
        weight_loads[1].wait()
        def tile(cols, start):
            mixed = dot_nn(o[full, :], wa[:, cols_at(3 * D + start, SHALLOW)])
            x1[full, cols] = x[full, cols].astype(WIDE) + mixed

        tiles(SHALLOW, tile)

        def mid_norm(i):
            part = rows_at(i * ROW, ROW)
            c[part, :] = norm_low(x1[part, :], second_gain)

        loop(DEC_ROWS // ROW, mid_norm)
        def tile(cols, start):
            cq[:, cols] = dot_nn(c[full, :], wa[:, cols_at(4 * D + start, SHALLOW)]).astype(LOW)

        tiles(SHALLOW, tile)
        weight_loads[3].wait()
        cot_in.wait()

        def cot_project(j):
            cols = cols_at(j * D, D)
            slope[full, cols] = dot_nt(ct[...], wo[cols, :]).astype(LOW)

        loop(FF // D, cot_project)
        weight_loads[2].wait()

        ctx_copy(ctx_part(quarter), quarter, {"section": 1 - section}, 0).wait_recv()
        ctx_copy(ctx_part(quarter), quarter, {"dp": side}, 1).start()
        ctx_copy(ctx_part(quarter), quarter, {"dp": twin}, 2).start()
        ctx_copy(ctx_part(quarter), other_quarter, {"dp": side}, 1).wait_recv()
        ctx_copy(ctx_part(other_quarter), other_quarter, {"dp": twin}, 3).start()
        ctx_copy(ctx_part(quarter), quarter, {"dp": twin}, 2).wait_recv()
        ctx_copy(ctx_part(quarter), quarter, {"dp": twin}, 3).wait_recv()

        def cross_bias(micro):
            key = lax.broadcasted_iota(jnp.int32, (ROW, ENC_MB), 1)
            key_t = lax.broadcasted_iota(jnp.int32, (ENC_MB, ROW), 0)

            def one(i):
                row = micro * ROWS_MB + i
                along, down = segment_pair(row)
                image_along = jnp.zeros((ROW, ROW), WIDE)
                image_down = jnp.zeros((ROW, ROW), WIDE)
                for seg in range(SEGS):
                    image = seg_images[row, seg].astype(WIDE)
                    image_along = jnp.where(along == seg, image, image_along)
                    image_down = jnp.where(down == seg, image, image_down)
                allowed = jnp.zeros((ROW, ENC_MB), jnp.bool_)
                allowed_t = jnp.zeros((ENC_MB, ROW), jnp.bool_)
                for image in range(IMG_MB):
                    low, high = image * IMG_ROWS, image * IMG_ROWS + PATCHES
                    allowed = allowed | (
                        (key >= low) & (key < high) & (image_down[:, 0:1] == image)
                    )
                    allowed_t = allowed_t | (
                        (key_t >= low) & (key_t < high) & (image_along[0:1, :] == image)
                    )
                bias[rows_at(i * ROW, ROW), :] = jnp.where(allowed, 0.0, MASKED)
                bias_t[i] = jnp.where(allowed_t, 0.0, MASKED)

            loop(ROWS_MB, one)

        def cross(micro):
            cross_bias(micro)
            base = micro * DEC_MB
            rows = rows_at(base, DEC_MB)
            keys = rows_at(micro * ENC_MB, ENC_MB)
            across(sent.at[micro], micro).wait_recv()

            def context(j):
                cols = cols_at(j * D, D)
                ctx[keys, cols] = dot_nn(landed[micro], wctx[:, cols]).astype(LOW)

            loop(2, context, CONTEXT_UNROLL)

            def attend_some(i):
                half_bias = bias[...]
                group = [i * CROSS_PAIRS + k for k in range(CROSS_PAIRS)]
                pairs = [
                    (cq[rows, pair_cols(pair)], ctx[keys, pair_cols(pair)], ctx[keys, pair_cols(pair, 1)])
                    for pair in group
                ]
                results = attend(pairs, jnp.concatenate([half_bias, half_bias], 0))
                for pair, result in zip(group, results):
                    co[rows, pair_cols(pair)] = result

            loop(PAIRS // CROSS_PAIRS, attend_some)
            def tile(cols, start):
                mixed = dot_nn(co[rows, :], wa[:, cols_at(5 * D + start, SHALLOW)])
                x2[rows, cols] = x1[rows, cols] + mixed

            tiles(SHALLOW, tile)

            def top_norm(i):
                part = rows_at(base + i * ROW, ROW)
                b[part, :] = norm_low(x2[part, :], third_gain)

            loop(ROWS_MB, top_norm)

            def expand(j):
                cols = cols_at(j * 512, 512)
                active, bend = gelu_parts(dot_nn(b[rows, :], wi[:, cols]))
                u[rows, cols] = active.astype(LOW)
                slope[rows, cols] = (bend * slope[rows, cols].astype(WIDE)).astype(LOW)

            loop(FF // 512, expand, EXPAND_UNROLL)
            def tile(cols, start):
                tmp[0:DEC_MB, cols] = dot_nt(slope[rows, :], wi[cols_at(start, DEEP), :])

            tiles(DEEP, tile)

            def top_back(i):
                part = rows_at(base + i * ROW, ROW)
                grad, gain_row = norm_back(tmp[rows_at(i * ROW, ROW), :], x2[part, :], third_gain)
                grad = grad + ct[part, :].astype(WIDE)
                g2w[part, :] = grad
                g2[part, :] = grad.astype(LOW)
                add_gain(2, gain_row)

            loop(ROWS_MB, top_back)
            def tile(cols, start):
                grads = dot_nt(g2[rows, :], wa[cols_at(start, SHALLOW), 5 * D : 6 * D])
                dmix[0:DEC_MB, cols] = grads.astype(LOW)

            tiles(SHALLOW, tile)

            def attend_back_some(i):
                parts = [bias_t[j] for j in range(ROWS_MB)]
                group = [i * CROSS_BACK_PAIRS + k for k in range(CROSS_BACK_PAIRS)]
                pairs = [
                    (
                        cq[rows, pair_cols(pair)], ctx[keys, pair_cols(pair)],
                        ctx[keys, pair_cols(pair, 1)], dmix[0:DEC_MB, pair_cols(pair)],
                    )
                    for pair in group
                ]
                results = attend_back(pairs, jnp.concatenate(parts + parts, 1))
                for pair, grads in zip(group, results):
                    cq[rows, pair_cols(pair)] = grads[0]
                    ctx[keys, pair_cols(pair)] = grads[1]
                    ctx[keys, pair_cols(pair, 1)] = grads[2]

            loop(PAIRS // CROSS_BACK_PAIRS, attend_back_some)
            def tile(cols, start):
                sent[micro, :, cols] = dot_nt(ctx[keys, :], wctx[cols_at(start, DEEP), :]).astype(LOW)

            tiles(DEEP, tile)
            across(sent.at[micro], micro).start()

        loop(MICRO, cross)
        stores = [
            store(a.at[full], a_out.at[full], 0), store(o.at[full], o_out.at[full], 1),
            store(b.at[full], b_out.at[full], 2), store(u.at[full], u_out.at[full], 3),
            store(slope.at[full], dh_out.at[full], 7), store(g2.at[full], g2_out.at[full], 6),
            store(co, co_out, 10), store(cq, dq_out, 11), store(landed, up_out, 12),
            store(ctx, dctx_out, 13), store(c.at[full], c_out.at[full], 14),
        ]
        for copy in stores:
            copy.start()

        def finish(micro):
            base = micro * DEC_MB
            rows = rows_at(base, DEC_MB)
            def tile(cols, start):
                tmp[0:DEC_MB, cols] = dot_nt(cq[rows, :], wa[cols_at(start, SHALLOW), 4 * D : 5 * D])

            tiles(SHALLOW, tile)

            def mid_back(i):
                part = rows_at(base + i * ROW, ROW)
                grad, gain_row = norm_back(tmp[rows_at(i * ROW, ROW), :], x1[part, :], second_gain)
                grad = grad + g2w[part, :]
                x1[part, :] = grad
                g1[part, :] = grad.astype(LOW)
                add_gain(1, gain_row)

            loop(ROWS_MB, mid_back)
            def tile(cols, start):
                grads = dot_nt(g1[rows, :], wa[cols_at(start, SHALLOW), 3 * D : 4 * D])
                dmix[0:DEC_MB, cols] = grads.astype(LOW)

            tiles(SHALLOW, tile)

            def self_back(i):
                row_bias = self_bias(micro * ROWS_MB + i, True)

                def some(j):
                    attend_rows_back(
                        qkv, rows_at(base + i * ROW, ROW), dmix, rows_at(i * ROW, ROW), row_bias,
                        pair_group(j, SELF_BACK_PAIRS),
                    )

                loop(PAIRS // SELF_BACK_PAIRS, some)

            loop(ROWS_MB, self_back)
            def tile(cols, start):
                tmp[0:DEC_MB, cols] = dot_nt(qkv[rows, :], wa[cols_at(start, DEEP), 0 : 3 * D])

            tiles(DEEP, tile)

            def low_back(i):
                part = rows_at(base + i * ROW, ROW)
                grad, gain_row = norm_back(
                    tmp[rows_at(i * ROW, ROW), :], x[part, :].astype(WIDE), first_gain
                )
                x1[part, :] = x1[part, :] + grad
                exch[rows_at(DEC_ROWS + base + i * ROW, ROW), :] = x1[part, 0:HALF].astype(LOW)
                add_gain(0, gain_row)

            loop(ROWS_MB, low_back)
            for half, kept in enumerate((exch, decoded_half)):
                cols = slice(half * HALF, (half + 1) * HALF)
                kept[rows, :] = (x2[rows, cols] + dot_nn(u[rows, :], wo[:, cols])).astype(LOW)

        loop(MICRO, finish)
        late = [
            store(qkv.at[full], dqkv_out.at[full], 4), store(g1.at[full], g1_out.at[full], 5),
            store(x1.at[full, HALF:], caption_own, 8), store(exch, exch_out, 9),
            store(decoded_half, decoded_own, 15),
        ]
        for copy in late:
            copy.start()
        for copy in stores + late:
            copy.wait()
        for micro in range(MICRO):
            across(sent.at[micro], micro).wait_send()
        ctx_copy(ctx_part(quarter), quarter, {"dp": side}, 1).wait_send()
        ctx_copy(ctx_part(quarter), quarter, {"dp": twin}, 2).wait_send()
        ctx_copy(ctx_part(quarter), quarter, {"dp": twin}, 3).wait_send()

    gain_in.wait()
    first_gain, second_gain, third_gain = gain_rows[0:1, :], gain_rows[1:2, :], gain_rows[2:3, :]

    @pl.when(section == 0)
    def _():
        encoder()

    @pl.when(section == 1)
    def _():
        decoder()


def main_call(patches, captions, segments, seg_images, attn_w, w_in, w_out, gains, cot):
    def low(*shape):
        return jax.ShapeDtypeStruct(shape, LOW)

    def wide(*shape):
        return jax.ShapeDtypeStruct(shape, WIDE)

    outs = [
        low(ENC_ROWS, D), low(ENC_ROWS, D), low(DEC_ROWS, D), low(ENC_ROWS, D), low(ENC_ROWS, FF),
        low(ENC_ROWS, 3 * D), low(ENC_ROWS, D), low(ENC_ROWS, D), low(ENC_ROWS, FF),
        low(DEC_ROWS, D), low(DEC_ROWS, D), low(MICRO, ENC_MB, D), low(ENC_ROWS, 2 * D),
        wide(8, D), wide(ENC_ROWS, HALF), low(DEC_ROWS, HALF), wide(DEC_ROWS, HALF),
        low(2 * DEC_ROWS, HALF),
    ]
    any_spec = pl.BlockSpec(memory_space=pl.ANY)
    vmem_spec = pl.BlockSpec(memory_space=pltpu.VMEM)
    out_specs = [any_spec] * len(outs)
    out_specs[13] = vmem_spec
    vmem = pltpu.VMEM
    scratch = [
        vmem((D, 6 * D), LOW), vmem((D, FF), LOW), vmem((FF, D), LOW), vmem((D, 2 * D), LOW),
        vmem((ENC_ROWS, D), LOW), vmem((DEC_ROWS, D), LOW),
        vmem((ENC_ROWS, D), LOW), vmem((ENC_ROWS, D), LOW), vmem((ENC_ROWS, D), LOW),
        vmem((ENC_ROWS, D), LOW),
        vmem((ENC_ROWS, 3 * D), LOW), vmem((max(ENC_MB, DEC_ROWS), FF), LOW), vmem((ENC_ROWS, FF), LOW),
        vmem((ENC_ROWS, D), WIDE), vmem((ENC_ROWS, D), WIDE),
        vmem((ENC_ROWS, D), LOW), vmem((ENC_ROWS, D), LOW),
        vmem((MICRO, ENC_MB, D), LOW), vmem((max(ENC_MB, DEC_ROWS), D), LOW),
        vmem((ENC_ROWS, 2 * D), LOW),
        vmem((DEC_ROWS, D), LOW), vmem((DEC_ROWS, D), LOW), vmem((DEC_ROWS, D), WIDE),
        vmem((ENC_MB, D), WIDE), vmem((MICRO, ENC_MB, D), LOW),
        vmem((DEC_MB, ENC_MB), WIDE), vmem((ROWS_MB, ENC_MB, ROW), WIDE),
        vmem((2 * DEC_ROWS, HALF), LOW), vmem((DEC_ROWS, HALF), LOW),
        vmem((3, D), WIDE), pltpu.SemaphoreType.DMA((7,)), pltpu.SemaphoreType.DMA((16,)),
        pltpu.SemaphoreType.DMA((MICRO,)), pltpu.SemaphoreType.DMA((MICRO,)),
        pltpu.SemaphoreType.DMA((4,)), pltpu.SemaphoreType.DMA((4,)),
    ]
    return pl.pallas_call(
        main_kernel,
        name="layers",
        out_shape=outs,
        in_specs=[any_spec, any_spec, vmem_spec, pl.BlockSpec(memory_space=pltpu.SMEM)]
        + [any_spec] * 5,
        out_specs=out_specs,
        scratch_shapes=scratch,
        compiler_params=pltpu.CompilerParams(
            collective_id=1, has_side_effects=True, vmem_limit_bytes=63 * MIB
        ),
    )(patches, captions, segments, seg_images, attn_w, w_in, w_out, gains, cot)


CHUNK = 256
SLOTS = 8
FIRST_LAG = 2
FIRST_ENC = (6, 7, 0, 1)
FIRST_DEC = (8, 9, 10, 11)
FAR_EVERY = 6
LAG = 4
GAIN_STEPS = 5
OUT_IDS = 12
ONLY_DEC = 12
CTX_IDS = 6


def grads_kernel(n_bits, *refs):
    (
        a_in, o_in, c_in, b_in, u_in, dqkv_in, g1_in, g2_in, dh_in, co_in, dq_in, up_in, dctx_in,
        gains_in, patch_own, decoded_own, caption_own, exch_in, cot_in,
        shares, gain_share, patch_out, decoded_out, caption_out,
        a, o, c, b, u, dqkv, g1, g2, dh, co, dq, up, dctx, cot,
        part, ctx_sum, exch, patch_rows, gain_sum, gain_in,
    ) = refs[:44]
    recv = refs[44 : 44 + n_bits]
    load_sem, own_sem, send_sem, recv_sem, gain_send, gain_recv, far_send, far_recv = refs[44 + n_bits :]
    section = lax.axis_index("section")
    dp = lax.axis_index("dp")
    bits = [(dp // (1 << k)) % 2 for k in range(n_bits)]
    partners = [{"dp": dp + (1 << k) * (1 - 2 * bits[k])} for k in range(n_bits)]
    across = {"section": 1 - section}
    barrier = pltpu.get_barrier_semaphore()

    def greet(target):
        pl.semaphore_signal(barrier, inc=1, device_id=target, device_id_type=MESH)

    for target in partners:
        greet(target)

    @pl.when(section == 1)
    def _():
        pl.semaphore_wait(barrier, n_bits)
        greet(across)

    @pl.when(section == 0)
    def _():
        pl.semaphore_wait(barrier, n_bits + 1)
        greet(across)

    rows = part.shape[-2]
    owners = 1 << n_bits
    total = recv[0].shape[0]
    begin = ONLY_DEC * (1 - section)

    def remote(src, dst, send, receive, target):
        return pltpu.make_async_remote_copy(
            src_ref=src, dst_ref=dst, send_sem=send, recv_sem=receive, device_id=target,
            device_id_type=MESH)

    def gain_copy(k):
        return remote(gain_sum.at[k], gain_in.at[k], gain_send.at[k], gain_recv.at[k], partners[k])

    def exch_copy():
        return remote(exch_in, exch, far_send.at[0], far_recv.at[0], across)

    def ctx_copy():
        return remote(ctx_sum, shares.at[0:CTX_IDS], far_send.at[1], far_recv.at[1], across)

    gain_sum[0] = gains_in[...]
    gain_copy(0).start()

    def load_plan(is_dec):
        count = DEC_ROWS if is_dec else ENC_ROWS

        def short(src, dst):
            return src.at[0:count], dst.at[0:count]

        plan = {
            0: short(u_in, u), 1: short(g2_in, g2), 2: short(b_in, b), 3: short(dh_in, dh),
            4: short(a_in, a), 5: short(dqkv_in, dqkv), 6: short(o_in, o), 7: short(g1_in, g1),
        }
        if is_dec:
            only = {
                8: (up_in, up), 9: (dctx_in, dctx), 10: (c_in, c), 11: (dq_in, dq),
                12: (co_in, co), 13: (cot_in, cot),
            }
            plan = {**only, **plan}
        return plan

    def need(is_dec, *slots):
        plan = load_plan(is_dec)
        for slot in slots:
            pltpu.make_async_copy(*plan[slot], load_sem.at[slot]).wait()

    def fetch(is_dec, *slots):
        plan = load_plan(is_dec)
        for slot in slots:
            pltpu.make_async_copy(*plan[slot], load_sem.at[slot]).start()

    def fetch_rest(is_dec):
        fetch(is_dec, *[k for k in load_plan(is_dec) if k not in (FIRST_DEC if is_dec else FIRST_ENC)])
        if is_dec:
            pltpu.make_async_copy(decoded_own, decoded_out, load_sem.at[14]).start()
            pltpu.make_async_copy(caption_own, caption_out, load_sem.at[15]).start()
        else:
            pltpu.make_async_copy(patch_own, patch_rows, load_sem.at[14]).start()

    for is_dec in (False, True):
        @pl.when(section == int(is_dec))
        def _(is_dec=is_dec):
            fetch(is_dec, *(FIRST_DEC if is_dec else FIRST_ENC))

    def core_copy(index):
        slot = index % SLOTS
        return remote(part.at[slot, 1 - bits[0]], recv[0].at[index], send_sem.at[0, index],
                      recv_sem.at[0, index], partners[0])

    near_first = list(range(1, n_bits))
    far_first = list(range(2, n_bits)) + [1]

    def stage_cut(order, stage, index, flip):
        bit = order[stage - 1]
        left = sorted(order[stage - 1 :], reverse=True)
        value = bits[bit] + flip * (1 - 2 * bits[bit])
        return (index,) + (slice(None),) * left.index(bit) + (value,)

    def stage_copy(order, stage, index):
        return remote(
            recv[stage - 1].at[stage_cut(order, stage, index, 1)], recv[stage].at[index],
            send_sem.at[stage, index], recv_sem.at[stage, index], partners[order[stage - 1]])

    def in_order(index, action):
        is_far = index % FAR_EVERY == FAR_EVERY // 2

        @pl.when(is_far)
        def _():
            action(far_first)

        @pl.when(jnp.logical_not(is_far))
        def _():
            action(near_first)

    def advance(i):
        for stage in range(n_bits):
            j = i - FIRST_LAG - stage * LAG

            @pl.when((j >= begin) & (j < total))
            def _(stage=stage, j=j):
                if stage == 0:
                    core_copy(j).wait()
                    summed = part[j % SLOTS, bits[0]].astype(WIDE) + recv[0][j].astype(WIDE)
                    recv[0][j] = summed.astype(LOW)
                    in_order(j, lambda order: stage_copy(order, 1, j).start())
                elif stage < n_bits - 1:
                    def step(order):
                        stage_copy(order, stage, j).wait()
                        mine = recv[stage - 1][stage_cut(order, stage, j, 0)]
                        summed = mine.astype(WIDE) + recv[stage][j].astype(WIDE)
                        recv[stage][j] = summed.astype(LOW)
                        stage_copy(order, stage + 1, j).start()

                    in_order(j, step)
                else:
                    def step(order):
                        stage_copy(order, stage, j).wait()

                    in_order(j, step)
                    last = jnp.where(j % FAR_EVERY == FAR_EVERY // 2, bits[far_first[-1]], bits[near_first[-1]])
                    mine = recv[stage - 1][j, last]
                    summed = mine.astype(WIDE) + recv[stage][j].astype(WIDE)

                    @pl.when(j < CTX_IDS)
                    def _():
                        ctx_sum[j] = summed

                    @pl.when(j >= CTX_IDS)
                    def _():
                        shares[j - CTX_IDS] = summed

        for k in range(n_bits):
            @pl.when(i == ONLY_DEC + GAIN_STEPS * (k + 1))
            def _(k=k):
                gain_copy(k).wait()
                summed = gain_sum[k] + gain_in[k]
                if k == n_bits - 1:
                    own = jnp.zeros((8, rows), WIDE)
                    for owner in range(owners):
                        own = jnp.where(dp == owner, summed[:, owner * rows : (owner + 1) * rows], own)
                    gain_share[...] = own
                else:
                    gain_sum[k + 1] = summed
                    gain_copy(k + 1).start()

    def place(index, first_owner, block):
        for k in range(block.shape[0] // rows):
            owner = first_owner + k
            path = tuple((owner >> bit) & 1 for bit in reversed(range(1, n_bits)))
            part[(index % SLOTS, owner & 1) + path] = block[k * rows : (k + 1) * rows].astype(LOW)

    def simple_phase(first, count, left, right, col, row_count):
        def step(i):
            index = first + i
            cols = cols_at(col + i * CHUNK, CHUNK)
            if row_count is None:
                value = dot_tn(left[...].reshape(-1, D), right[:, cols])
            else:
                value = dot_tn(left[0:row_count, :], right[0:row_count, cols])
            place(index, 0, value)
            core_copy(index).start()
            advance(index)
        loop(count, step)

    def out_phase(first, right, row_count):
        share = FF // owners
        blocks = share // rows
        step_owners = D // share

        def step(i):
            cols = cols_at(i * CHUNK, CHUNK)
            base = first + i * blocks
            for piece in range(FF // D):
                value = dot_tn(u[0:row_count, piece * D : (piece + 1) * D], right[0:row_count, cols])
                for k in range(step_owners):
                    for q in range(blocks):
                        low = k * share + q * rows
                        place(base + q, piece * step_owners + k, value[low : low + rows])
            loop(blocks, lambda q: core_copy(base + q).start())
            loop(blocks, lambda q: advance(base + q))
        loop(D // CHUNK, step)

    @pl.when(section == 1)
    def _():
        need(True, 8, 9)
        fetch_rest(True)
        simple_phase(0, CTX_IDS, up, dctx, 0, None)
        need(True, 10, 11)
        simple_phase(CTX_IDS, 3, c, dq, 0, DEC_ROWS)
        need(True, 12, 1)
        simple_phase(CTX_IDS + 3, 3, co, g2, 0, DEC_ROWS)

    for is_dec in (False, True):
        @pl.when(section == int(is_dec))
        def _(is_dec=is_dec):
            count = DEC_ROWS if is_dec else ENC_ROWS
            need(is_dec, 6, 7)
            if not is_dec:
                fetch_rest(False)
            simple_phase(ONLY_DEC, D // CHUNK, o, g1, 0, count)
            need(is_dec, 0, 13 if is_dec else 1)
            out_phase(ONLY_DEC + D // CHUNK, cot if is_dec else g2, count)
            need(is_dec, 2, 3)
            simple_phase(ONLY_DEC + D // CHUNK + OUT_IDS, FF // CHUNK, b, dh, 0, count)

    @pl.when(section == 1)
    def _():
        pl.semaphore_wait(barrier, 1)
        ctx_copy().start()

    exch_copy().start()

    for is_dec in (False, True):
        @pl.when(section == int(is_dec))
        def _(is_dec=is_dec):
            count = DEC_ROWS if is_dec else ENC_ROWS
            need(is_dec, 4, 5)
            first = ONLY_DEC + D // CHUNK + OUT_IDS + FF // CHUNK
            simple_phase(first, 3 * D // CHUNK, a, dqkv, 0, count)

    exch_copy().wait()

    @pl.when(section == 0)
    def _():
        pltpu.make_async_copy(patch_own, patch_rows, load_sem.at[14]).wait()
        for image in range(MICRO * IMG_MB):
            patch_out[image * PATCHES : (image + 1) * PATCHES, :] = patch_rows[
                image * IMG_ROWS : image * IMG_ROWS + PATCHES, :
            ]
        decoded_out[...] = exch[0:DEC_ROWS, :]
        caption_out[...] = exch[DEC_ROWS : 2 * DEC_ROWS, :].astype(WIDE)

    @pl.when(section == 1)
    def _():
        pltpu.make_async_copy(decoded_own, decoded_out, load_sem.at[14]).wait()
        pltpu.make_async_copy(caption_own, caption_out, load_sem.at[15]).wait()
        for image in range(MICRO * IMG_MB):
            patch_out[image * PATCHES : (image + 1) * PATCHES, :] = exch[
                image * IMG_ROWS : image * IMG_ROWS + PATCHES, :
            ].astype(WIDE)

    loop(FIRST_LAG + (n_bits - 1) * LAG, lambda i: advance(total + i))

    @pl.when(section == 0)
    def _():
        ctx_copy().wait_recv()

    @pl.when(section == 1)
    def _():
        ctx_copy().wait_send()


def grads_call(n_dp, *operands):
    n_bits = n_dp.bit_length() - 1
    rows = D // n_dp
    share = FF // n_dp
    total = ONLY_DEC + 2 * OUT_IDS + 4 * D // CHUNK
    vmem = pltpu.VMEM
    pair = (2,) * (n_bits - 1)
    any_spec = pl.BlockSpec(memory_space=pl.ANY)
    vmem_spec = pl.BlockSpec(memory_space=pltpu.VMEM)
    sem = pltpu.SemaphoreType.DMA
    scratch = [
        vmem((ENC_ROWS, D), LOW), vmem((ENC_ROWS, D), LOW), vmem((DEC_ROWS, D), LOW),
        vmem((ENC_ROWS, D), LOW), vmem((ENC_ROWS, FF), LOW), vmem((ENC_ROWS, 3 * D), LOW),
        vmem((ENC_ROWS, D), LOW), vmem((ENC_ROWS, D), LOW), vmem((ENC_ROWS, FF), LOW),
        vmem((DEC_ROWS, D), LOW), vmem((DEC_ROWS, D), LOW), vmem((MICRO, ENC_MB, D), LOW),
        vmem((ENC_ROWS, 2 * D), LOW), vmem((DEC_ROWS, D), LOW),
        vmem((SLOTS, 2) + pair + (rows, CHUNK), LOW), vmem((CTX_IDS, rows, CHUNK), WIDE),
        vmem((2 * DEC_ROWS, HALF), LOW), vmem((ENC_ROWS, HALF), WIDE),
        vmem((n_bits, 8, D), WIDE), vmem((n_bits, 8, D), WIDE),
    ]
    scratch += [vmem((total,) + pair[k:] + (rows, CHUNK), LOW) for k in range(n_bits)]
    scratch += [
        sem((16,)), sem((1,)), sem((n_bits, total)), sem((n_bits, total)), sem((n_bits,)),
        sem((n_bits,)), sem((2,)), sem((2,)),
    ]
    in_specs = [any_spec] * len(operands)
    in_specs[13] = vmem_spec
    return pl.pallas_call(
        functools.partial(grads_kernel, n_bits),
        name="weight_sums",
        out_shape=(
            jax.ShapeDtypeStruct((total - CTX_IDS, rows, CHUNK), WIDE),
            jax.ShapeDtypeStruct((8, rows), WIDE),
            jax.ShapeDtypeStruct((MICRO * IMG_MB * PATCHES, HALF), WIDE),
            jax.ShapeDtypeStruct((DEC_ROWS, HALF), LOW),
            jax.ShapeDtypeStruct((DEC_ROWS, HALF), WIDE),
        ),
        in_specs=in_specs,
        out_specs=(vmem_spec,) * 5,
        scratch_shapes=scratch,
        compiler_params=pltpu.CompilerParams(
            collective_id=2, has_side_effects=True, vmem_limit_bytes=63 * MIB
        ),
    )(*operands)


def place_kernel(
    shares, gain_share, patch_in, decoded_in, caption_in,
    decoded_out, caption_out, patch_out, attn_out, in_out, out_out, gain_out, sem,
):
    rows = shares.shape[1]
    moves = [
        (patch_in, patch_out), (caption_in, caption_out), (decoded_in, decoded_out),
        (gain_share.at[0:3], gain_out.at[0]),
    ]
    mixed_ids = D // CHUNK
    first_w_out = CTX_IDS + mixed_ids
    first_w_in = first_w_out + OUT_IDS
    first_attn = first_w_in + FF // CHUNK
    blocks = OUT_IDS * CHUNK // D

    def cols(index):
        return slice(index * CHUNK, (index + 1) * CHUNK)

    for k in range(3 * mixed_ids):
        moves.append((shares.at[first_attn + k], attn_out.at[0, :, cols(k)]))
    for k in range(mixed_ids):
        moves.append((shares.at[CTX_IDS + k], attn_out.at[0, :, cols(3 * mixed_ids + k)]))
    for k in range(CTX_IDS):
        moves.append((shares.at[k], attn_out.at[0, :, cols(4 * D // CHUNK + k)]))
    for k in range(FF // CHUNK):
        moves.append((shares.at[first_w_in + k], in_out.at[0, :, cols(k)]))
    for k in range(OUT_IDS):
        part = slice((k % blocks) * rows, (k % blocks + 1) * rows)
        moves.append((shares.at[first_w_out + k], out_out.at[0, part, cols(k // blocks)]))
    copies = [
        pltpu.make_async_copy(src, dst, sem.at[index]) for index, (src, dst) in enumerate(moves)
    ]
    for copy in copies:
        copy.start()
    for copy in copies:
        copy.wait()


def kernel_sums(n_dp, operands):
    results = grads_call(n_dp, *operands)
    rows = D // n_dp
    any_spec = pl.BlockSpec(memory_space=pl.ANY)
    patch_out, decoded_out, caption_out = results[2:]
    shapes = [decoded_out, caption_out, patch_out] + [
        jax.ShapeDtypeStruct(shape, WIDE)
        for shape in ((1, rows, 6 * D), (1, rows, FF), (1, FF // n_dp, D), (1, 3, rows))
    ]
    return pl.pallas_call(
        place_kernel,
        name="place_sums",
        out_shape=[jax.ShapeDtypeStruct(item.shape, item.dtype) for item in shapes],
        in_specs=[any_spec] * 5,
        out_specs=[pl.BlockSpec(memory_space=pltpu.VMEM)] * 7,
        scratch_shapes=[pltpu.SemaphoreType.DMA((64,))],
    )(*results)


def shifted(block, distance):
    devices = range(lax.axis_size("section"))
    route = [(i - distance, i) for i in devices if i - distance in devices]
    return lax.ppermute(block, "section", route)


def plain_sums(operands):
    (
        a, o, c, b, u, dqkv, g1, g2, dh, co, dq, up, dctx,
        gains, patch_own, decoded_own, caption_own, exch, cot,
    ) = operands
    is_first = lax.axis_index("section") == 0
    up = up.reshape(ENC_ROWS, D)

    def encoder_parts():
        return (
            jnp.concatenate([dot_tn(a, dqkv), dot_tn(o, g1)], 1), jnp.zeros((D, 2 * D), WIDE),
            jnp.zeros((D, 2 * D), WIDE), dot_tn(b, dh), dot_tn(u, g2),
        )

    def decoder_parts():
        rows = slice(0, DEC_ROWS)
        return (
            jnp.concatenate([dot_tn(a[rows], dqkv[rows]), dot_tn(o[rows], g1[rows])], 1),
            jnp.concatenate([dot_tn(c, dq), dot_tn(co, g2[rows])], 1),
            dot_tn(up, dctx), dot_tn(b[rows], dh[rows]), dot_tn(u[rows], cot),
        )

    parts = lax.cond(is_first, encoder_parts, decoder_parts)
    sums = [lax.psum_scatter(part, "dp", scatter_dimension=0, tiled=True) for part in parts]
    last = jnp.where(is_first, shifted(sums[2], -1), sums[1])
    moved = lax.ppermute(exch, "section", [(0, 1), (1, 0)])

    def unpad(block):
        shaped = block[:ENC_ROWS].reshape(MICRO * IMG_MB, IMG_ROWS, HALF)
        return shaped[:, :PATCHES].reshape(-1, HALF).astype(WIDE)

    return (
        jnp.where(is_first, moved[:DEC_ROWS], decoded_own),
        jnp.where(is_first, moved[DEC_ROWS:].astype(WIDE), caption_own),
        jnp.where(is_first, unpad(patch_own), unpad(moved)),
        jnp.concatenate([sums[0], last], 1),
        sums[3],
        sums[4],
        lax.psum_scatter(gains[:3], "dp", scatter_dimension=1, tiled=True),
    )


def with_section(results):
    return tuple(results[:3]) + tuple(share[None] for share in results[3:])


def local(patches, captions, segments, seg_images, attn_w, w_in, w_out, norm_gains, cotangent):
    n_dp = lax.axis_size("dp")
    kept = main_call(
        patches, captions, segments, seg_images, attn_w, w_in, w_out, norm_gains, cotangent
    )
    operands = list(kept) + [cotangent]
    if n_dp & (n_dp - 1) == 0 and (D // n_dp) % 16 == 0:
        results = kernel_sums(n_dp, operands)
    else:
        results = with_section(plain_sums(operands))
    return tuple(results)


def solution(mesh):
    placed = (
        P("dp", None),
        P("dp", None),
        P("dp", None),
        P("dp", None),
        P("section", None, None),
        P("section", None, None),
        P("section", None, None),
        P("section", None, None),
        P("dp", None),
    )
    return jax.shard_map(
        local,
        mesh=mesh,
        in_specs=placed,
        out_specs=(
            P("dp", "section"),
            P("dp", "section"),
            P("dp", "section"),
            P("section", "dp", None),
            P("section", "dp", None),
            P("section", "dp", None),
            P("section", None, "dp"),
        ),
        check_vma=False,
    )
```
